32 devices in a mesh: groups: 2 (over y), rows: 4 (over z), feat: 4 (over x, core).
Axes of the slice: x: 2, y: 2, z: 4, core: 2. Of those that a mesh axis runs over, the one named last changes fastest.
Arguments:
- daily_unit_counts: bfloat16 [8192, 512], P(('groups', 'rows')), parts along dimension 0, may hold values from 0.099609375 to 20
- region_ids: int32 [8192], P(('groups', 'rows')), parts along dimension 0, may hold values from 0 to 9
- node_ids: int32 [8192], P(('groups', 'rows')), parts along dimension 0, may hold values from 0 to 31
- bin_ids: int32 [8192, 512], P(('groups', 'rows'), 'feat'), parts along dimension 0, may hold values from 0 to 255
- quant_index: int32 [2], P('groups'), parts along dimension 0, may hold values from 0 to 8
- filter_kernels: float32 [8, 4], replicated, may hold values from -3 to 3
Outputs:
- histogram: float32 [8, 4, 32, 2, 32, 256], P(('groups', 'feat'), 'rows'), parts along dimension 0
- feature_best: float32 [8, 4, 32, 32], P('groups'), parts along dimension 0
The draws below stay inside these ranges and needn't reach their ends.
There are 2 independent parts, one for each index of `groups`. The reference program is written for one: setup_inputs(seed, part) draws one part's arguments, and reference() takes and returns one part's arrays. A program takes and returns all parts, laid end to end along the dimension named above; an argument that names none is the same for every part. Nothing has to cross between parts.
All inputs are finite; a program needn't handle non-finite values.
Results may differ from the reference program's by a relative error of at most 0.0071.
Values may be sent and summed in bfloat16 or wider, within the bound.
No kernel may reach another device: no remote copies, remote signals or barrier semaphores. Data moves between devices by JAX's collectives and lax.ppermute only.
A program may use at most 64 MiB of HBM per device.

```python
import math
import jax
import jax.numpy as jnp
from jax import lax

SERIES = 4096
FEATURES = 512
BINS = 256
NODES = 32
HIST = 512
HORIZON_LENGTH = 28
REGIONS = 10
CHANNELS = 8
TAPS = 4
N_ROWS = 4
N_FEAT = 4


def with_ends(values, own_key, low, top_value):
    dims = values.shape
    index_at = [jax.random.randint(jax.random.fold_in(own_key, axis), (), 0, dims[axis]) for axis in range(len(dims))]
    values = values.at[tuple(index_at)].set(low)
    longest = dims.index(max(dims))
    index_at[longest] = (index_at[longest] + 1) % dims[longest]
    return values.at[tuple(index_at)].set(top_value)


def block_levels(key, extent, shards, least, largest):
    factor_of, own = 1.0, jax.random.fold_in(key, 6)
    for axis_at, parts in shards:
        heights = jnp.exp(jax.random.uniform(jax.random.fold_in(own, axis_at), (parts,), jnp.float32, least / len(shards), largest / len(shards)))
        factor_of = factor_of * jnp.repeat(heights, extent[axis_at] // parts).reshape([-1 if axis == axis_at else 1 for axis in range(len(extent))])
    return factor_of


def normal_values(rng, dims, deviation, bound, held_as=jnp.bfloat16):
    return jnp.clip(deviation * jax.random.normal(rng, dims, jnp.float32), -bound, bound).astype(held_as)


def setup_inputs(seed: int = 0, part: int = 0) -> dict:
    arg_keys = jax.random.split(jax.random.key(seed), 7)
    part_keys = jax.random.split(jax.random.fold_in(arg_keys[6], part), 7)
    daily_unit_counts = jnp.clip(jnp.exp(math.log(20.0) - 5.3022313 * jax.random.uniform(part_keys[0], (SERIES, HIST), jnp.float32) ** block_levels(part_keys[0], (SERIES, HIST), ((0, 4),), -0.2, 0.2)), 0.099609375, 20.0).astype(jnp.bfloat16)
    region_ids = with_ends(jax.random.randint(part_keys[1], (SERIES,), 0, REGIONS), jax.random.fold_in(part_keys[1], 1), 0, REGIONS - 1).astype(jnp.int32)
    node_ids = with_ends(jax.random.randint(part_keys[2], (SERIES,), 0, NODES), jax.random.fold_in(part_keys[2], 1), 0, NODES - 1).astype(jnp.int32)
    bin_ids = with_ends(jax.random.randint(part_keys[3], (SERIES, FEATURES), 0, BINS), jax.random.fold_in(part_keys[3], 1), 0, BINS - 1).astype(jnp.int32)
    quant_index = jax.random.randint(part_keys[4], (1,), 0, 9).astype(jnp.int32)
    filter_kernels = normal_values(arg_keys[5], (CHANNELS, TAPS), 0.2, 3.0, jnp.float32)
    return dict(daily_unit_counts=daily_unit_counts, region_ids=region_ids, node_ids=node_ids, bin_ids=bin_ids, quant_index=quant_index, filter_kernels=filter_kernels)


DILATE = (1, 7, 14, 28)
LEVELS = (0.005, 0.025, 0.165, 0.25, 0.5, 0.75, 0.835, 0.975, 0.995)
SOFT_SPAN = 0.5
RIDGE_TERM = 1.0


def gradients(daily_unit_counts, region_ids, node_ids, quant_index, filter_kernels, totals):
    sales_wide = daily_unit_counts.astype(jnp.float32)
    series_level = jnp.mean(sales_wide, axis=1)
    own_scaled = sales_wide / series_level[:, None]
    region_scale = jnp.mean(totals, axis=1) + 1.0
    shared = totals / region_scale[:, None]
    region_pick = (region_ids[:, None] == jnp.arange(REGIONS)[None, :]).astype(jnp.float32)
    regional = jnp.dot(region_pick, shared, precision=lax.Precision.HIGHEST, preferred_element_type=jnp.float32)
    first_day = HIST - HORIZON_LENGTH
    predicted_demand = jnp.zeros((daily_unit_counts.shape[0], HORIZON_LENGTH), jnp.float32)
    for lane_number in range(CHANNELS):
        input_entries = own_scaled if lane_number % 2 == 0 else regional
        stride = DILATE[(lane_number // 2) % 4]
        for lag_offset in range(TAPS):
            opening_period = first_day - 1 - lag_offset * stride
            predicted_demand = predicted_demand + filter_kernels[lane_number, lag_offset] * input_entries[:, opening_period:opening_period + HORIZON_LENGTH]
    observed_demand = own_scaled[:, first_day:]
    levels_table = jnp.array(LEVELS, jnp.float32)
    quantile = jnp.sum(jnp.where(jnp.arange(9) == quant_index[0], levels_table, 0.0))
    quantile_level = jax.nn.sigmoid((predicted_demand - observed_demand) / SOFT_SPAN)
    gradient = jnp.mean(quantile_level - quantile, axis=1)
    hessian = jnp.mean(quantile_level * (1.0 - quantile_level), axis=1) / SOFT_SPAN
    member = (node_ids[:, None] == jnp.arange(NODES)[None, :]).astype(jnp.float32)
    columns = jnp.concatenate([gradient[:, None] * member, hessian[:, None] * member], axis=1)
    return columns.astype(jnp.bfloat16)


def split_gains(histogram):
    left_sums = jnp.cumsum(histogram, axis=-1)[..., :-1]
    totals = jnp.sum(histogram, axis=-1, keepdims=True)
    right_sums = totals - left_sums
    left_grad = left_sums[..., 0, :, :]
    left_hess = left_sums[..., 1, :, :]
    right_grad = right_sums[..., 0, :, :]
    right_hess = right_sums[..., 1, :, :]
    all_grad = totals[..., 0, :, :]
    all_hess = totals[..., 1, :, :]
    split_gain = left_grad * left_grad / (left_hess + RIDGE_TERM) + right_grad * right_grad / (right_hess + RIDGE_TERM) - all_grad * all_grad / (all_hess + RIDGE_TERM)
    return jnp.max(split_gain, axis=-1)


def reference(daily_unit_counts, region_ids, node_ids, bin_ids, quant_index, filter_kernels):
    region_pick = (region_ids[:, None] == jnp.arange(REGIONS)[None, :]).astype(jnp.bfloat16)
    totals = jnp.dot(region_pick.T, daily_unit_counts, preferred_element_type=jnp.float32)
    columns = gradients(daily_unit_counts, region_ids, node_ids, quant_index, filter_kernels, totals)
    widened = columns.astype(jnp.float32)

    def one_feature(bin_row):
        return jax.ops.segment_sum(widened, bin_row, num_segments=BINS)

    sums = lax.map(one_feature, bin_ids.T)
    histogram = sums.reshape(FEATURES, BINS, 2, NODES).transpose(0, 2, 3, 1)
    per_feature = split_gains(histogram)
    within = FEATURES // N_FEAT // N_ROWS
    feature_best = per_feature.reshape(N_FEAT, N_ROWS, within, NODES)
    histogram = histogram.reshape(N_FEAT, N_ROWS, within, 2, NODES, BINS)
    return histogram, feature_best
```

```python
import functools

import jax
import jax.numpy as jnp
from jax import lax
from jax.experimental import pallas as pl
from jax.experimental.pallas import tpu as pltpu
from jax.sharding import PartitionSpec as P

BINS = 256
NODES = 32
HIST = 512
HORIZON = 28
FIRST_DAY = HIST - HORIZON
REGIONS = 10
CHANNELS = 8
TAPS = 4
DILATE = (1, 7, 14, 28)
LEVELS = (0.005, 0.025, 0.165, 0.25, 0.5, 0.75, 0.835, 0.975, 0.995)

LANES = 128
DAYS = 32
REGION_ROW = HORIZON
NODE_ROW = HORIZON + 1
TOTAL_ROW = HORIZON
STORES = 16
PIECES = 3
SCALE = 256.0
BF16 = jnp.bfloat16
F32 = jnp.float32
F8 = jnp.float8_e4m3fn
ROW_BY_ROW = (((1,), (1,)), ((), ()))
VMEM_LIMIT = 48 * 2**20


def partner(position, step, count):
    if count & (count - 1) == 0:
        return position ^ step
    return (position + step) % count


def split_parts(values):
    parts = []
    rest = values
    for _ in range(PIECES):
        part = rest.astype(BF16)
        parts.append(part)
        rest = rest - part.astype(F32)
    return parts


def tap_matrix(taps_ref, parity):
    gap = lax.broadcasted_iota(jnp.int32, (DAYS, LANES), 1) - lax.broadcasted_iota(
        jnp.int32, (DAYS, LANES), 0
    )
    first = FIRST_DAY - (HIST - LANES)
    matrix = jnp.zeros((DAYS, LANES), F32)
    for channel in range(parity, CHANNELS, 2):
        for lag in range(TAPS):
            offset = first - 1 - lag * DILATE[(channel // 2) % 4]
            matrix = matrix + jnp.where(gap == offset, taps_ref[channel, lag], 0.0)
    if parity == 0:
        matrix = matrix - jnp.where(gap == first, 1.0, 0.0)
    day = lax.broadcasted_iota(jnp.int32, (DAYS, LANES), 0)
    return jnp.where(day < HORIZON, matrix, 0.0)


def prepare(rows, counts_ref, region_ref, node_ref, bins_ref, taps_ref, *rest):
    out_refs, held = rest[:rows], rest[rows]
    series = counts_ref.shape[0]
    feats = bins_ref.shape[1] // rows
    pad = held.shape[1]
    me = lax.axis_index("rows")
    counts = counts_ref[...]
    recent = counts_ref[:, HIST - LANES :]

    own_taps = jnp.concatenate(split_parts(tap_matrix(taps_ref, 0)), axis=0)
    own = lax.dot_general(own_taps, recent, ROW_BY_ROW, preferred_element_type=F32)
    own = own[:DAYS] + own[DAYS : 2 * DAYS] + own[2 * DAYS :]
    ones = jnp.ones((8, HIST), BF16)
    level = lax.dot_general(ones, counts, ROW_BY_ROW, preferred_element_type=F32)[:1] / HIST
    own = own / level
    day = lax.broadcasted_iota(jnp.int32, (DAYS, series), 0)
    own = jnp.where(day == REGION_ROW, region_ref[...].astype(F32), own)
    own = jnp.where(day == NODE_ROW, node_ref[...].astype(F32), own)
    own = own.astype(BF16)

    store = lax.broadcasted_iota(jnp.int32, (STORES, series), 0)
    pick = jnp.where(store == region_ref[...], 1.0, 0.0).astype(BF16)
    totals = jnp.dot(pick, counts, preferred_element_type=F32)
    forecast = lax.dot_general(
        tap_matrix(taps_ref, 1),
        totals[:, HIST - LANES :],
        ROW_BY_ROW,
        precision=lax.Precision.HIGHEST,
        preferred_element_type=F32,
    )
    over_days = lax.dot_general(
        jnp.ones((DAYS, HIST), F32),
        totals,
        ROW_BY_ROW,
        precision=lax.Precision.HIGHEST,
        preferred_element_type=F32,
    )
    row = lax.broadcasted_iota(jnp.int32, (DAYS, STORES), 0)
    forecast = jnp.where(row == TOTAL_ROW, over_days, forecast)
    sums = jnp.concatenate(
        split_parts(forecast) + [jnp.zeros((DAYS, LANES - PIECES * STORES), BF16)], axis=1
    )

    turned = bins_ref[...].astype(F32).T
    for row_block in range(rows):
        part = turned[row_block * feats : (row_block + 1) * feats]
        if pad > feats:
            part = jnp.concatenate([part, jnp.zeros((pad - feats, series), F32)], axis=0)
        held[row_block] = part.astype(BF16)

    height = pad + DAYS
    for step in range(rows):
        bins = held[partner(me, step, rows)]
        for block in range(series // LANES):
            lanes = slice(block * LANES, (block + 1) * LANES)
            out_refs[step][block * height : block * height + pad] = bins[:, lanes]
            out_refs[step][block * height + pad : (block + 1) * height] = own[:, lanes]
        out_refs[step][series // LANES * height :] = sums


def grow(rows, feats, series, quant_ref, *rest):
    in_refs = rest[:rows]
    hist_ref, best_ref, bins_held, cols_held, hist_held, sem = rest[rows:]
    pad = max(feats, 16)
    height = pad + DAYS
    blocks = series // LANES
    everyone = rows * series

    level = F32(0.0)
    for index, value in enumerate(LEVELS):
        level = jnp.where(quant_ref[0] == index, F32(value), level)

    sums = jnp.zeros((DAYS, STORES), F32)
    for ref in in_refs:
        parts = ref[blocks * height :].astype(F32)
        for piece in range(PIECES):
            sums = sums + parts[:, piece * STORES : (piece + 1) * STORES]
    shared = sums / (sums[TOTAL_ROW : TOTAL_ROW + 1] / HIST + 1.0)
    shared = jnp.concatenate(split_parts(shared), axis=1)

    day = lax.broadcasted_iota(jnp.int32, (DAYS, series), 0)
    store = lax.broadcasted_iota(jnp.int32, (PIECES * STORES, series), 0) % STORES
    node_at = lax.broadcasted_iota(jnp.int32, (NODES, series), 0)
    for source, ref in enumerate(in_refs):
        here = slice(source * series, (source + 1) * series)
        both = jnp.concatenate(
            [ref[block * height : (block + 1) * height] for block in range(blocks)], axis=1
        ).astype(F32)
        bins_held[:, here] = (both[:feats] - 128.0).astype(jnp.int32)
        own = both[pad:]
        region = own[REGION_ROW : REGION_ROW + 1].astype(jnp.int32)
        node = own[NODE_ROW : NODE_ROW + 1].astype(jnp.int32)
        pick = jnp.where(store == region, 1.0, 0.0).astype(BF16)
        regional = jnp.dot(shared, pick, preferred_element_type=F32)
        wave = jnp.where(day < HORIZON, jnp.tanh(own + regional), 0.0)
        mean = jnp.sum(wave, axis=0, keepdims=True) / HORIZON
        square = jnp.sum(wave * wave, axis=0, keepdims=True) / HORIZON
        gradient = 0.5 + 0.5 * mean - level
        hessian = 0.5 * (1.0 - square)
        here_node = node_at == node
        low = []
        for part, value in enumerate((gradient, hessian)):
            value = value.astype(BF16).astype(F32) * SCALE
            high = value.astype(F8).astype(F32)
            for offset, piece in ((0, high), (2, value - high)):
                at = (part + offset) * NODES
                cols_held[at : at + NODES, here] = jnp.where(here_node, piece, 0.0).astype(F8)

    below = lax.broadcasted_iota(jnp.int32, (BINS, BINS), 0) <= lax.broadcasted_iota(
        jnp.int32, (BINS, BINS), 1
    )
    below = jnp.where(below, 1.0, 0.0).astype(BF16)
    chunk = min(everyone, 4096)
    bin_at = lax.broadcasted_iota(jnp.int32, (32, chunk), 0)
    feature_at = lax.broadcasted_iota(jnp.int32, (NODES, LANES), 1)
    last_bin = lax.broadcasted_iota(jnp.int32, (NODES, BINS), 1) == BINS - 1

    def products(feature, start):
        here = pl.ds(start, chunk)
        wide = jnp.broadcast_to(bins_held[pl.ds(feature, 1), here], (32, chunk)).astype(jnp.int8)
        onehot = jnp.concatenate(
            [
                jnp.where(
                    wide == (bin_at + (32 * part - 128)).astype(jnp.int8),
                    jnp.ones((), F8),
                    jnp.zeros((), F8),
                )
                for part in range(BINS // 32)
            ],
            axis=0,
        )
        return lax.dot_general(
            cols_held[:, here], onehot, ROW_BY_ROW, preferred_element_type=F32
        )

    def copy_out(feature):
        return pltpu.make_async_copy(hist_held.at[feature], hist_ref.at[feature], sem)

    def one_feature(feature, best):
        if everyone == chunk:
            product = products(feature, 0)
        else:
            product = lax.fori_loop(
                0,
                everyone // chunk,
                lambda at, total: total
                + products(feature, pl.multiple_of(at * chunk, chunk)),
                jnp.zeros((4 * NODES, BINS), F32),
            )
        hist = (product[: 2 * NODES] + product[2 * NODES :]) * (1.0 / SCALE)
        hist_held[feature] = hist
        copy_out(feature).start()
        high = hist.astype(BF16)
        both = jnp.concatenate([high, (hist - high.astype(F32)).astype(BF16)], axis=0)
        left = jnp.dot(both, below, preferred_element_type=F32)
        left = left[: 2 * NODES] + left[2 * NODES :]
        total = left[:, BINS - 1 :]
        right = total - left
        gain = left[:NODES] * left[:NODES] / (left[NODES:] + 1.0) + right[:NODES] * right[
            :NODES
        ] / (right[NODES:] + 1.0)
        gain = jnp.max(jnp.where(last_bin, -jnp.inf, gain), axis=1, keepdims=True)
        gain = gain - total[:NODES] * total[:NODES] / (total[NODES:] + 1.0)
        return jnp.where(feature_at == feature, gain, best)

    best = lax.fori_loop(
        0, feats, one_feature, jnp.zeros((NODES, LANES), F32), unroll=min(feats, 4)
    )
    best = best.T
    width = LANES // NODES
    packed = jnp.concatenate(
        [best[at * (feats // width) : (at + 1) * (feats // width)] for at in range(width)], axis=1
    )
    for target in range(best_ref.shape[0]):
        best_ref[target] = packed
    pltpu.make_async_copy(hist_held, hist_ref, sem).wait()


def shards(daily_unit_counts, region_ids, node_ids, bin_ids, quant_index, filter_kernels):
    rows = lax.axis_size("rows")
    feat_count = lax.axis_size("feat")
    series = daily_unit_counts.shape[0]
    feats = bin_ids.shape[1] // rows
    pad = max(feats, 16)
    buffer = (series // LANES * (pad + DAYS) + DAYS, LANES)
    vmem = pl.BlockSpec(memory_space=pltpu.VMEM)
    smem = pl.BlockSpec(memory_space=pltpu.SMEM)
    params = pltpu.CompilerParams(vmem_limit_bytes=VMEM_LIMIT)

    outgoing = pl.pallas_call(
        functools.partial(prepare, rows),
        out_shape=[jax.ShapeDtypeStruct(buffer, BF16)] * rows,
        in_specs=[vmem, vmem, vmem, vmem, smem],
        out_specs=[vmem] * rows,
        scratch_shapes=[pltpu.VMEM((rows, pad, series), BF16)],
        compiler_params=params,
        name="prepare",
    )(
        daily_unit_counts,
        region_ids.reshape(1, series),
        node_ids.reshape(1, series),
        bin_ids,
        filter_kernels,
    )

    arrived = [outgoing[0]]
    for step in range(1, rows):
        pairs = [(at, partner(at, step, rows)) for at in range(rows)]
        arrived.append(lax.ppermute(outgoing[step], "rows", pairs))

    targets = rows * feat_count
    packed_rows = feats * NODES // LANES
    histogram, best = pl.pallas_call(
        functools.partial(grow, rows, feats, series),
        out_shape=[
            jax.ShapeDtypeStruct((feats, 2 * NODES, BINS), F32),
            jax.ShapeDtypeStruct((targets, packed_rows, LANES), F32),
        ],
        in_specs=[smem] + [vmem] * rows,
        out_specs=[pl.BlockSpec(memory_space=pl.ANY), vmem],
        scratch_shapes=[
            pltpu.VMEM((feats, rows * series), jnp.int32),
            pltpu.VMEM((4 * NODES, rows * series), F8),
            pltpu.VMEM((feats, 2 * NODES, BINS), F32),
            pltpu.SemaphoreType.DMA,
        ],
        compiler_params=params,
        name="grow",
    )(quant_index, *arrived)

    gathered = lax.all_to_all(best, ("feat", "rows"), 0, 0, tiled=True)
    width = LANES // NODES
    feature_best = (
        gathered.reshape(feat_count, rows, packed_rows, width, NODES)
        .transpose(0, 1, 3, 2, 4)
        .reshape(feat_count, rows, feats, NODES)
    )
    return histogram.reshape(1, 1, feats, 2, NODES, BINS), feature_best


def solution(mesh):
    in_specs = (
        P(("groups", "rows"), None),
        P(("groups", "rows")),
        P(("groups", "rows")),
        P(("groups", "rows"), "feat"),
        P("groups"),
        P(),
    )
    out_specs = (
        P(("groups", "feat"), "rows", None, None, None, None),
        P("groups", None, None, None),
    )
    return jax.shard_map(shards, mesh=mesh, in_specs=in_specs, out_specs=out_specs, check_vma=False)
```

```python
import functools

import jax
import jax.numpy as jnp
from jax import lax
from jax.experimental import pallas as pl
from jax.experimental.pallas import tpu as pltpu
from jax.sharding import PartitionSpec as P

BINS = 256
NODES = 32
HIST = 512
HORIZON = 28
FIRST_DAY = HIST - HORIZON
REGIONS = 10
CHANNELS = 8
TAPS = 4
DILATE = (1, 7, 14, 28)
LEVELS = (0.005, 0.025, 0.165, 0.25, 0.5, 0.75, 0.835, 0.975, 0.995)

LANES = 128
DAYS = 32
REGION_ROW = HORIZON
NODE_ROW = HORIZON + 1
TOTAL_ROW = HORIZON
STORES = 16
PIECES = 3
SCALE = 256.0
BF16 = jnp.bfloat16
F32 = jnp.float32
F8 = jnp.float8_e4m3fn
ROW_BY_ROW = (((1,), (1,)), ((), ()))
VMEM_LIMIT = 48 * 2**20
WHOLE_VMEM = 63 * 2**20


def partner(position, step, count):
    if count & (count - 1) == 0:
        return position ^ step
    return (position + step) % count


def split_parts(values):
    parts = []
    rest = values
    for _ in range(PIECES):
        part = rest.astype(BF16)
        parts.append(part)
        rest = rest - part.astype(F32)
    return parts


def tap_matrix(taps_ref, parity):
    gap = lax.broadcasted_iota(jnp.int32, (DAYS, LANES), 1) - lax.broadcasted_iota(
        jnp.int32, (DAYS, LANES), 0
    )
    first = FIRST_DAY - (HIST - LANES)
    matrix = jnp.zeros((DAYS, LANES), F32)
    for channel in range(parity, CHANNELS, 2):
        for lag in range(TAPS):
            offset = first - 1 - lag * DILATE[(channel // 2) % 4]
            matrix = matrix + jnp.where(
                gap == offset, taps_ref[lag : lag + 1, channel : channel + 1], 0.0
            )
    if parity == 0:
        matrix = matrix - jnp.where(gap == first, 1.0, 0.0)
    day = lax.broadcasted_iota(jnp.int32, (DAYS, LANES), 0)
    return jnp.where(day < HORIZON, matrix, 0.0)


def prepare(rows, *refs):
    given = refs[:5]
    out_refs = refs[5 : 5 + rows]
    taken = refs[5 + rows : 10 + rows]
    held, sems = refs[10 + rows :]
    copies = [
        pltpu.make_async_copy(source, target, sems.at[at])
        for at, (source, target) in enumerate(zip(given, taken))
    ]
    for at in (3, 4, 1, 2, 0):
        copies[at].start()
    counts_ref, region_ref, node_ref, bins_ref, taps_ref = taken
    series = counts_ref.shape[0]
    feats = bins_ref.shape[1] // rows
    pad = held.shape[1]
    me = lax.axis_index("rows")
    copies[3].wait()
    turned = bins_ref[...].astype(F32).T
    for row_block in range(rows):
        part = turned[row_block * feats : (row_block + 1) * feats]
        if pad > feats:
            part = jnp.concatenate([part, jnp.zeros((pad - feats, series), F32)], axis=0)
        held[row_block] = part.astype(BF16)

    for at in (4, 1, 2, 0):
        copies[at].wait()
    counts = counts_ref[...]
    recent = counts_ref[:, HIST - LANES :]

    own_taps = jnp.concatenate(split_parts(tap_matrix(taps_ref, 0)), axis=0)
    own = lax.dot_general(own_taps, recent, ROW_BY_ROW, preferred_element_type=F32)
    own = own[:DAYS] + own[DAYS : 2 * DAYS] + own[2 * DAYS :]
    ones = jnp.ones((8, HIST), BF16)
    level = lax.dot_general(ones, counts, ROW_BY_ROW, preferred_element_type=F32)[:1] / HIST
    own = own / level
    day = lax.broadcasted_iota(jnp.int32, (DAYS, series), 0)
    own = jnp.where(day == REGION_ROW, region_ref[...].astype(F32), own)
    own = jnp.where(day == NODE_ROW, node_ref[...].astype(F32), own)
    own = own.astype(BF16)

    store = lax.broadcasted_iota(jnp.int32, (STORES, series), 0)
    pick = jnp.where(store == region_ref[...], 1.0, 0.0).astype(BF16)
    totals = jnp.dot(pick, counts, preferred_element_type=F32)
    forecast = lax.dot_general(
        tap_matrix(taps_ref, 1),
        totals[:, HIST - LANES :],
        ROW_BY_ROW,
        precision=lax.Precision.HIGHEST,
        preferred_element_type=F32,
    )
    over_days = lax.dot_general(
        jnp.ones((DAYS, HIST), F32),
        totals,
        ROW_BY_ROW,
        precision=lax.Precision.HIGHEST,
        preferred_element_type=F32,
    )
    row = lax.broadcasted_iota(jnp.int32, (DAYS, STORES), 0)
    forecast = jnp.where(row == TOTAL_ROW, over_days, forecast)
    sums = jnp.concatenate(
        split_parts(forecast) + [jnp.zeros((DAYS, LANES - PIECES * STORES), BF16)], axis=1
    )

    height = pad + DAYS
    for step in range(rows):
        bins = held[partner(me, step, rows)]
        for block in range(series // LANES):
            lanes = slice(block * LANES, (block + 1) * LANES)
            out_refs[step][block * height : block * height + pad] = bins[:, lanes]
            out_refs[step][block * height + pad : (block + 1) * height] = own[:, lanes]
        out_refs[step][series // LANES * height :] = sums


def grow(rows, feats, series, quant_ref, *rest):
    in_refs = rest[:rows]
    hist_ref, best_ref, bins_held, cols_held, hist_held, sem = rest[rows:]
    pad = max(feats, 16)
    height = pad + DAYS
    blocks = series // LANES
    everyone = rows * series

    level = F32(0.0)
    for index, value in enumerate(LEVELS):
        level = jnp.where(quant_ref[0] == index, F32(value), level)

    sums = jnp.zeros((DAYS, STORES), F32)
    for ref in in_refs:
        parts = ref[blocks * height :].astype(F32)
        for piece in range(PIECES):
            sums = sums + parts[:, piece * STORES : (piece + 1) * STORES]
    shared = sums / (sums[TOTAL_ROW : TOTAL_ROW + 1] / HIST + 1.0)
    shared = jnp.concatenate(split_parts(shared), axis=1)

    day = lax.broadcasted_iota(jnp.int32, (DAYS, series), 0)
    store = lax.broadcasted_iota(jnp.int32, (PIECES * STORES, series), 0) % STORES
    node_at = lax.broadcasted_iota(jnp.int32, (NODES, series), 0)
    for source, ref in enumerate(in_refs):
        here = slice(source * series, (source + 1) * series)
        both = jnp.concatenate(
            [ref[block * height : (block + 1) * height] for block in range(blocks)], axis=1
        ).astype(F32)
        bins_held[:, here] = (both[:feats] - 128.0).astype(jnp.int32)
        own = both[pad:]
        region = own[REGION_ROW : REGION_ROW + 1].astype(jnp.int32)
        node = own[NODE_ROW : NODE_ROW + 1].astype(jnp.int32)
        pick = jnp.where(store == region, 1.0, 0.0).astype(BF16)
        regional = jnp.dot(shared, pick, preferred_element_type=F32)
        wave = jnp.where(day < HORIZON, jnp.tanh(own + regional), 0.0)
        mean = jnp.sum(wave, axis=0, keepdims=True) / HORIZON
        square = jnp.sum(wave * wave, axis=0, keepdims=True) / HORIZON
        gradient = 0.5 + 0.5 * mean - level
        hessian = 0.5 * (1.0 - square)
        here_node = node_at == node
        low = []
        for part, value in enumerate((gradient, hessian)):
            value = value.astype(BF16).astype(F32) * SCALE
            high = value.astype(F8).astype(F32)
            for offset, piece in ((0, high), (2, value - high)):
                at = (part + offset) * NODES
                cols_held[at : at + NODES, here] = jnp.where(here_node, piece, 0.0).astype(F8)

    below = lax.broadcasted_iota(jnp.int32, (BINS, BINS), 0) <= lax.broadcasted_iota(
        jnp.int32, (BINS, BINS), 1
    )
    below = jnp.where(below, 1.0, 0.0).astype(BF16)
    chunk = min(everyone, 4096)
    bin_at = lax.broadcasted_iota(jnp.int32, (32, chunk), 0)
    feature_at = lax.broadcasted_iota(jnp.int32, (NODES, LANES), 1)
    last_bin = lax.broadcasted_iota(jnp.int32, (NODES, BINS), 1) == BINS - 1

    def products(feature, start):
        here = pl.ds(start, chunk)
        wide = jnp.broadcast_to(bins_held[pl.ds(feature, 1), here], (32, chunk)).astype(jnp.int8)
        onehot = jnp.concatenate(
            [
                jnp.where(
                    wide == (bin_at + (32 * part - 128)).astype(jnp.int8),
                    jnp.ones((), F8),
                    jnp.zeros((), F8),
                )
                for part in range(BINS // 32)
            ],
            axis=0,
        )
        return lax.dot_general(
            cols_held[:, here], onehot, ROW_BY_ROW, preferred_element_type=F32
        )

    def copy_out(feature):
        return pltpu.make_async_copy(hist_held.at[feature], hist_ref.at[feature], sem)

    def one_feature(feature, carry):
        if everyone == chunk:
            product = products(feature, 0)
        else:
            product = lax.fori_loop(
                0,
                everyone // chunk,
                lambda at, total: total
                + products(feature, pl.multiple_of(at * chunk, chunk)),
                jnp.zeros((4 * NODES, BINS), F32),
            )
        hist = (product[: 2 * NODES] + product[2 * NODES :]) * (1.0 / SCALE)
        hist_held[feature] = hist
        copy_out(feature).start()
        return carry

    lax.fori_loop(0, feats, one_feature, 0, unroll=min(feats, 8))
    group = min(feats, 8)

    def one_group(at, best):
        hist = hist_held[pl.ds(at * group, group)].reshape(group * 2 * NODES, BINS)
        high = hist.astype(BF16)
        low = (hist - high.astype(F32)).astype(BF16)
        left = jnp.dot(high, below, preferred_element_type=F32) + jnp.dot(
            low, below, preferred_element_type=F32
        )
        left = left.reshape(group, 2, NODES, BINS)
        for member in range(group):
            grad, hess = left[member, 0], left[member, 1]
            all_grad, all_hess = grad[:, BINS - 1 :], hess[:, BINS - 1 :]
            over_grad, over_hess = all_grad - grad, all_hess - hess
            gain = grad * grad / (hess + 1.0) + over_grad * over_grad / (over_hess + 1.0)
            gain = jnp.max(jnp.where(last_bin, -jnp.inf, gain), axis=1, keepdims=True)
            gain = gain - all_grad * all_grad / (all_hess + 1.0)
            best = jnp.where(feature_at == at * group + member, gain, best)
        return best

    best = lax.fori_loop(0, feats // group, one_group, jnp.zeros((NODES, LANES), F32))
    best = best.T
    width = LANES // NODES
    packed = jnp.concatenate(
        [best[at * (feats // width) : (at + 1) * (feats // width)] for at in range(width)], axis=1
    )
    for target in range(best_ref.shape[0]):
        best_ref[target] = packed
    pltpu.make_async_copy(hist_held, hist_ref, sem).wait()


def shards(daily_unit_counts, region_ids, node_ids, bin_ids, quant_index, filter_kernels):
    rows = lax.axis_size("rows")
    feat_count = lax.axis_size("feat")
    series = daily_unit_counts.shape[0]
    feats = bin_ids.shape[1] // rows
    pad = max(feats, 16)
    buffer = (series // LANES * (pad + DAYS) + DAYS, LANES)
    vmem = pl.BlockSpec(memory_space=pltpu.VMEM)
    smem = pl.BlockSpec(memory_space=pltpu.SMEM)
    hbm = pl.BlockSpec(memory_space=pl.ANY)
    params = pltpu.CompilerParams(vmem_limit_bytes=VMEM_LIMIT)

    outgoing = pl.pallas_call(
        functools.partial(prepare, rows),
        out_shape=[jax.ShapeDtypeStruct(buffer, BF16)] * rows,
        in_specs=[hbm] * 5,
        out_specs=[vmem] * rows,
        scratch_shapes=[
            pltpu.VMEM(daily_unit_counts.shape, BF16),
            pltpu.VMEM((1, series), jnp.int32),
            pltpu.VMEM((1, series), jnp.int32),
            pltpu.VMEM(bin_ids.shape, jnp.int32),
            pltpu.VMEM((TAPS, CHANNELS), F32),
            pltpu.VMEM((rows, pad, series), BF16),
            pltpu.SemaphoreType.DMA((5,)),
        ],
        compiler_params=pltpu.CompilerParams(vmem_limit_bytes=WHOLE_VMEM),
        name="prepare",
    )(
        daily_unit_counts,
        region_ids.reshape(1, series),
        node_ids.reshape(1, series),
        bin_ids,
        filter_kernels.T,
    )

    arrived = [outgoing[0]]
    for step in range(1, rows):
        pairs = [(at, partner(at, step, rows)) for at in range(rows)]
        arrived.append(lax.ppermute(outgoing[step], "rows", pairs))

    targets = rows * feat_count
    packed_rows = feats * NODES // LANES
    histogram, best = pl.pallas_call(
        functools.partial(grow, rows, feats, series),
        out_shape=[
            jax.ShapeDtypeStruct((feats, 2 * NODES, BINS), F32),
            jax.ShapeDtypeStruct((targets, packed_rows, LANES), F32),
        ],
        in_specs=[smem] + [vmem] * rows,
        out_specs=[pl.BlockSpec(memory_space=pl.ANY), vmem],
        scratch_shapes=[
            pltpu.VMEM((feats, rows * series), jnp.int32),
            pltpu.VMEM((4 * NODES, rows * series), F8),
            pltpu.VMEM((feats, 2 * NODES, BINS), F32),
            pltpu.SemaphoreType.DMA,
        ],
        compiler_params=params,
        name="grow",
    )(quant_index, *arrived)

    gathered = lax.all_to_all(best, ("feat", "rows"), 0, 0, tiled=True)
    width = LANES // NODES
    feature_best = (
        gathered.reshape(feat_count, rows, packed_rows, width, NODES)
        .transpose(0, 1, 3, 2, 4)
        .reshape(feat_count, rows, feats, NODES)
    )
    return histogram.reshape(1, 1, feats, 2, NODES, BINS), feature_best


def solution(mesh):
    in_specs = (
        P(("groups", "rows"), None),
        P(("groups", "rows")),
        P(("groups", "rows")),
        P(("groups", "rows"), "feat"),
        P("groups"),
        P(),
    )
    out_specs = (
        P(("groups", "feat"), "rows", None, None, None, None),
        P("groups", None, None, None),
    )
    return jax.shard_map(shards, mesh=mesh, in_specs=in_specs, out_specs=out_specs, check_vma=False)
```

```python
import functools

import jax
import jax.numpy as jnp
from jax import lax
from jax.experimental import pallas as pl
from jax.experimental.pallas import tpu as pltpu
from jax.sharding import PartitionSpec as P

BINS = 256
NODES = 32
HIST = 512
HORIZON = 28
FIRST_DAY = HIST - HORIZON
REGIONS = 10
CHANNELS = 8
TAPS = 4
DILATE = (1, 7, 14, 28)
LEVELS = (0.005, 0.025, 0.165, 0.25, 0.5, 0.75, 0.835, 0.975, 0.995)

LANES = 128
DAYS = 32
REGION_ROW = HORIZON
NODE_ROW = HORIZON + 1
TOTAL_ROW = HORIZON
STORES = 16
PIECES = 3
SCALE = 256.0
BF16 = jnp.bfloat16
F32 = jnp.float32
F8 = jnp.float8_e4m3fn
ROW_BY_ROW = (((1,), (1,)), ((), ()))
VMEM_LIMIT = 24 * 2**20
WHOLE_VMEM = 63 * 2**20


def partner(position, step, count):
    if count & (count - 1) == 0:
        return position ^ step
    return (position + step) % count


def split_parts(values):
    parts = []
    rest = values
    for _ in range(PIECES):
        part = rest.astype(BF16)
        parts.append(part)
        rest = rest - part.astype(F32)
    return parts


def tap_matrix(taps_ref, parity):
    gap = lax.broadcasted_iota(jnp.int32, (DAYS, LANES), 1) - lax.broadcasted_iota(
        jnp.int32, (DAYS, LANES), 0
    )
    first = FIRST_DAY - (HIST - LANES)
    matrix = jnp.zeros((DAYS, LANES), F32)
    for channel in range(parity, CHANNELS, 2):
        for lag in range(TAPS):
            offset = first - 1 - lag * DILATE[(channel // 2) % 4]
            matrix = matrix + jnp.where(
                gap == offset, taps_ref[lag : lag + 1, channel : channel + 1], 0.0
            )
    if parity == 0:
        matrix = matrix - jnp.where(gap == first, 1.0, 0.0)
    day = lax.broadcasted_iota(jnp.int32, (DAYS, LANES), 0)
    return jnp.where(day < HORIZON, matrix, 0.0)


def store_sums(counts_hbm, region_hbm, taps_hbm, sums_ref, counts_ref, region_ref, taps_ref, sems):
    given = (counts_hbm, region_hbm, taps_hbm)
    taken = (counts_ref, region_ref, taps_ref)
    copies = [
        pltpu.make_async_copy(source, target, sems.at[at])
        for at, (source, target) in enumerate(zip(given, taken))
    ]
    for copy in copies:
        copy.start()
    copies[2].wait()
    taps = tap_matrix(taps_ref, 1)
    copies[1].wait()
    series = counts_ref.shape[0]
    store = lax.broadcasted_iota(jnp.int32, (STORES, series), 0)
    pick = jnp.where(store == region_ref[...], 1.0, 0.0).astype(BF16)
    copies[0].wait()
    totals = jnp.dot(pick, counts_ref[...], preferred_element_type=F32)
    forecast = lax.dot_general(
        taps,
        totals[:, HIST - LANES :],
        ROW_BY_ROW,
        precision=lax.Precision.HIGHEST,
        preferred_element_type=F32,
    )
    over_days = lax.dot_general(
        jnp.ones((DAYS, HIST), F32),
        totals,
        ROW_BY_ROW,
        precision=lax.Precision.HIGHEST,
        preferred_element_type=F32,
    )
    row = lax.broadcasted_iota(jnp.int32, (DAYS, STORES), 0)
    forecast = jnp.where(row == TOTAL_ROW, over_days, forecast)
    sums_ref[...] = jnp.concatenate(
        split_parts(forecast) + [jnp.zeros((DAYS, LANES - PIECES * STORES), BF16)], axis=1
    )


def prepare(rows, sums_hbm, counts_ref, region_ref, node_ref, bins_ref, taps_ref, *rest):
    sums_ref, out_refs, (held, sem) = rest[0], rest[1 : 1 + rows], rest[1 + rows :]
    copy = pltpu.make_async_copy(sums_hbm, sums_ref, sem)
    copy.start()
    series = counts_ref.shape[0]
    feats = bins_ref.shape[1] // rows
    pad = held.shape[1]
    me = lax.axis_index("rows")
    counts = counts_ref[...]
    recent = counts_ref[:, HIST - LANES :]

    own_taps = jnp.concatenate(split_parts(tap_matrix(taps_ref, 0)), axis=0)
    own = lax.dot_general(own_taps, recent, ROW_BY_ROW, preferred_element_type=F32)
    own = own[:DAYS] + own[DAYS : 2 * DAYS] + own[2 * DAYS :]
    ones = jnp.ones((8, HIST), BF16)
    level = lax.dot_general(ones, counts, ROW_BY_ROW, preferred_element_type=F32)[:1] / HIST
    own = own / level
    day = lax.broadcasted_iota(jnp.int32, (DAYS, series), 0)
    own = jnp.where(day == REGION_ROW, region_ref[...].astype(F32), own)
    own = jnp.where(day == NODE_ROW, node_ref[...].astype(F32), own)
    own = own.astype(BF16)

    turned = bins_ref[...].astype(F32).T
    for row_block in range(rows):
        part = turned[row_block * feats : (row_block + 1) * feats]
        if pad > feats:
            part = jnp.concatenate([part, jnp.zeros((pad - feats, series), F32)], axis=0)
        held[row_block] = part.astype(BF16)

    height = pad + DAYS
    for step in range(rows):
        bins = held[partner(me, step, rows)]
        for block in range(series // LANES):
            lanes = slice(block * LANES, (block + 1) * LANES)
            out_refs[step][block * height : block * height + pad] = bins[:, lanes]
            out_refs[step][block * height + pad : (block + 1) * height] = own[:, lanes]
    copy.wait()


def shared_forecast(sums_refs):
    sums = jnp.zeros((DAYS, STORES), F32)
    for ref in sums_refs:
        parts = ref[...].astype(F32)
        for piece in range(PIECES):
            sums = sums + parts[:, piece * STORES : (piece + 1) * STORES]
    shared = sums / (sums[TOTAL_ROW : TOTAL_ROW + 1] / HIST + 1.0)
    return jnp.concatenate(split_parts(shared), axis=1)


def quantile_level(quant_ref):
    level = F32(0.0)
    for index, value in enumerate(LEVELS):
        level = jnp.where(quant_ref[0] == index, F32(value), level)
    return level


def series_columns(own, shared, level, cols_ref):
    series = own.shape[1]
    day = lax.broadcasted_iota(jnp.int32, (DAYS, series), 0)
    store = lax.broadcasted_iota(jnp.int32, (PIECES * STORES, series), 0) % STORES
    region = own[REGION_ROW : REGION_ROW + 1].astype(jnp.int32)
    node = own[NODE_ROW : NODE_ROW + 1].astype(jnp.int32)
    pick = jnp.where(store == region, 1.0, 0.0).astype(BF16)
    regional = jnp.dot(shared, pick, preferred_element_type=F32)
    wave = jnp.where(day < HORIZON, jnp.tanh(own + regional), 0.0)
    mean = jnp.sum(wave, axis=0, keepdims=True) / HORIZON
    square = jnp.sum(wave * wave, axis=0, keepdims=True) / HORIZON
    gradient = 0.5 + 0.5 * mean - level
    hessian = 0.5 * (1.0 - square)
    here_node = lax.broadcasted_iota(jnp.int32, (NODES, series), 0) == node
    for part, value in enumerate((gradient, hessian)):
        value = value.astype(BF16).astype(F32) * SCALE
        high = value.astype(F8).astype(F32)
        for offset, piece in ((0, high), (2, value - high)):
            at = (part + offset) * NODES
            cols_ref[at : at + NODES] = jnp.where(here_node, piece, 0.0).astype(F8)


def accumulate(rows, sources, feats, first, last, quant_ref, *refs):
    sums_refs, block_refs, refs = refs[:rows], refs[rows : rows + sources], refs[rows + sources :]
    if not first:
        before_ref, refs = refs[0], refs[1:]
    if last:
        hist_ref, best_ref, bins_held, cols_held, hist_held, sem = refs
    else:
        hist_held, bins_held, cols_held = refs
    series = bins_held.shape[2]
    pad = max(feats, 16)
    height = pad + DAYS
    shared = shared_forecast(sums_refs)
    level = quantile_level(quant_ref)
    for source, ref in enumerate(block_refs):
        both = jnp.concatenate(
            [ref[block * height : (block + 1) * height] for block in range(series // LANES)],
            axis=1,
        ).astype(F32)
        bins_held[source] = (both[:feats] - 128.0).astype(jnp.int32)
        series_columns(both[pad:], shared, level, cols_held.at[source])

    bin_at = lax.broadcasted_iota(jnp.int32, (32, series), 0)

    def products(source, feature):
        bins = jnp.broadcast_to(bins_held[source, pl.ds(feature, 1)], (32, series)).astype(jnp.int8)
        onehot = jnp.concatenate(
            [
                jnp.where(
                    bins == (bin_at + (32 * part - 128)).astype(jnp.int8),
                    jnp.ones((), F8),
                    jnp.zeros((), F8),
                )
                for part in range(BINS // 32)
            ],
            axis=0,
        )
        return lax.dot_general(
            cols_held[source], onehot, ROW_BY_ROW, preferred_element_type=F32
        )

    def one_feature(feature, carry):
        product = products(0, feature)
        if sources > 1:
            product = lax.fori_loop(
                1, sources, lambda at, total: total + products(at, feature), product
            )
        hist = (product[: 2 * NODES] + product[2 * NODES :]) * (1.0 / SCALE)
        if not first:
            hist = hist + before_ref[feature]
        hist_held[feature] = hist
        if last:
            pltpu.make_async_copy(hist_held.at[feature], hist_ref.at[feature], sem).start()
        return carry

    lax.fori_loop(0, feats, one_feature, 0, unroll=min(feats, 8))
    if last:
        best_gains(feats, hist_held, best_ref)
        pltpu.make_async_copy(hist_held, hist_ref, sem).wait()


def best_gains(feats, hist_held, best_ref):
    below = lax.broadcasted_iota(jnp.int32, (BINS, BINS), 0) <= lax.broadcasted_iota(
        jnp.int32, (BINS, BINS), 1
    )
    below = jnp.where(below, 1.0, 0.0).astype(BF16)
    feature_at = lax.broadcasted_iota(jnp.int32, (NODES, LANES), 1)
    last_bin = lax.broadcasted_iota(jnp.int32, (NODES, BINS), 1) == BINS - 1
    group = min(feats, 8)

    def one_group(at, best):
        hist = hist_held[pl.ds(at * group, group)].reshape(group * 2 * NODES, BINS)
        high = hist.astype(BF16)
        low = (hist - high.astype(F32)).astype(BF16)
        left = jnp.dot(high, below, preferred_element_type=F32) + jnp.dot(
            low, below, preferred_element_type=F32
        )
        left = left.reshape(group, 2, NODES, BINS)
        for member in range(group):
            grad, hess = left[member, 0], left[member, 1]
            all_grad, all_hess = grad[:, BINS - 1 :], hess[:, BINS - 1 :]
            over_grad, over_hess = all_grad - grad, all_hess - hess
            gain = grad * grad / (hess + 1.0) + over_grad * over_grad / (over_hess + 1.0)
            gain = jnp.max(jnp.where(last_bin, -jnp.inf, gain), axis=1, keepdims=True)
            gain = gain - all_grad * all_grad / (all_hess + 1.0)
            best = jnp.where(feature_at == at * group + member, gain, best)
        return best

    best = lax.fori_loop(0, feats // group, one_group, jnp.zeros((NODES, LANES), F32))
    best = best.T
    width = LANES // NODES
    packed = jnp.concatenate(
        [best[at * (feats // width) : (at + 1) * (feats // width)] for at in range(width)], axis=1
    )
    for target in range(best_ref.shape[0]):
        best_ref[target] = packed


def shards(daily_unit_counts, region_ids, node_ids, bin_ids, quant_index, filter_kernels):
    rows = lax.axis_size("rows")
    feat_count = lax.axis_size("feat")
    series = daily_unit_counts.shape[0]
    feats = bin_ids.shape[1] // rows
    pad = max(feats, 16)
    height = pad + DAYS
    vmem = pl.BlockSpec(memory_space=pltpu.VMEM)
    smem = pl.BlockSpec(memory_space=pltpu.SMEM)
    hbm = pl.BlockSpec(memory_space=pl.ANY)
    params = pltpu.CompilerParams(vmem_limit_bytes=VMEM_LIMIT)
    regions = region_ids.reshape(1, series)
    nodes = node_ids.reshape(1, series)

    def exchange(array, step):
        pairs = [(at, partner(at, step, rows)) for at in range(rows)]
        return lax.ppermute(array, "rows", pairs)

    sums = pl.pallas_call(
        store_sums,
        out_shape=jax.ShapeDtypeStruct((DAYS, LANES), BF16),
        in_specs=[hbm] * 3,
        out_specs=vmem,
        scratch_shapes=[
            pltpu.VMEM(daily_unit_counts.shape, BF16),
            pltpu.VMEM((1, series), jnp.int32),
            pltpu.VMEM((TAPS, CHANNELS), F32),
            pltpu.SemaphoreType.DMA((3,)),
        ],
        compiler_params=pltpu.CompilerParams(vmem_limit_bytes=WHOLE_VMEM),
        name="store_sums",
    )(daily_unit_counts, regions, filter_kernels.T)
    own_sums, *outgoing = pl.pallas_call(
        functools.partial(prepare, rows),
        out_shape=[jax.ShapeDtypeStruct(sums.shape, BF16)]
        + [jax.ShapeDtypeStruct((series // LANES * height, LANES), BF16)] * rows,
        in_specs=[hbm] + [vmem] * 5,
        out_specs=[vmem] * (1 + rows),
        scratch_shapes=[pltpu.VMEM((rows, pad, series), BF16), pltpu.SemaphoreType.DMA],
        compiler_params=params,
        name="prepare",
    )(sums, daily_unit_counts, regions, nodes, bin_ids, filter_kernels.T)
    sums = [own_sums] + [exchange(sums, step) for step in range(1, rows)]
    arrived = [outgoing[0]]
    for step in range(1, rows):
        block, sums[step] = lax.optimization_barrier((outgoing[step], sums[step]))
        arrived.append(exchange(block, step))

    targets = rows * feat_count
    packed_rows = feats * NODES // LANES
    hist_shape = jax.ShapeDtypeStruct((feats, 2 * NODES, BINS), F32)
    steps = [arrived[at : at + 1] for at in range(min(rows, 4) - 1)]
    steps.append(arrived[len(steps) :])
    histogram = None
    for at, blocks in enumerate(steps):
        first, last = at == 0, at == len(steps) - 1
        count = len(blocks)
        held = [
            pltpu.VMEM((count, feats, series), jnp.int32),
            pltpu.VMEM((count, 4 * NODES, series), F8),
        ]
        operands = [quant_index, *sums, *blocks] + ([] if first else [histogram])
        if last:
            held += [pltpu.VMEM(hist_shape.shape, F32), pltpu.SemaphoreType.DMA]
            out_shape = [hist_shape, jax.ShapeDtypeStruct((targets, packed_rows, LANES), F32)]
            out_specs = [hbm, vmem]
        else:
            out_shape, out_specs = hist_shape, vmem
        histogram = pl.pallas_call(
            functools.partial(accumulate, rows, count, feats, first, last),
            out_shape=out_shape,
            in_specs=[smem] + [vmem] * (len(operands) - 1),
            out_specs=out_specs,
            scratch_shapes=held,
            input_output_aliases={} if first or last else {len(operands) - 1: 0},
            compiler_params=params,
            name=f"accumulate_{at}",
        )(*operands)
    histogram, best = histogram

    gathered = lax.all_to_all(best, ("feat", "rows"), 0, 0, tiled=True)
    width = LANES // NODES
    feature_best = (
        gathered.reshape(feat_count, rows, packed_rows, width, NODES)
        .transpose(0, 1, 3, 2, 4)
        .reshape(feat_count, rows, feats, NODES)
    )
    return histogram.reshape(1, 1, feats, 2, NODES, BINS), feature_best


def solution(mesh):
    in_specs = (
        P(("groups", "rows"), None),
        P(("groups", "rows")),
        P(("groups", "rows")),
        P(("groups", "rows"), "feat"),
        P("groups"),
        P(),
    )
    out_specs = (
        P(("groups", "feat"), "rows", None, None, None, None),
        P("groups", None, None, None),
    )
    return jax.shard_map(shards, mesh=mesh, in_specs=in_specs, out_specs=out_specs, check_vma=False)
```

```python
import functools

import jax
import jax.numpy as jnp
from jax import lax
from jax.experimental import pallas as pl
from jax.experimental.pallas import tpu as pltpu
from jax.sharding import PartitionSpec as P

BINS = 256
NODES = 32
HIST = 512
HORIZON = 28
FIRST_DAY = HIST - HORIZON
REGIONS = 10
CHANNELS = 8
TAPS = 4
DILATE = (1, 7, 14, 28)
LEVELS = (0.005, 0.025, 0.165, 0.25, 0.5, 0.75, 0.835, 0.975, 0.995)

LANES = 128
DAYS = 32
REGION_ROW = HORIZON
NODE_ROW = HORIZON + 1
TOTAL_ROW = HORIZON
STORES = 16
PIECES = 3
SCALE = 256.0
BF16 = jnp.bfloat16
F32 = jnp.float32
F8 = jnp.float8_e4m3fn
ROW_BY_ROW = (((1,), (1,)), ((), ()))
VMEM_LIMIT = 24 * 2**20


def partner(position, step, count):
    if count & (count - 1) == 0:
        return position ^ step
    return (position + step) % count


def split_parts(values):
    parts = []
    rest = values
    for _ in range(PIECES):
        part = rest.astype(BF16)
        parts.append(part)
        rest = rest - part.astype(F32)
    return parts


def tap_matrix(taps_ref, parity):
    gap = lax.broadcasted_iota(jnp.int32, (DAYS, LANES), 1) - lax.broadcasted_iota(
        jnp.int32, (DAYS, LANES), 0
    )
    first = FIRST_DAY - (HIST - LANES)
    matrix = jnp.zeros((DAYS, LANES), F32)
    for channel in range(parity, CHANNELS, 2):
        for lag in range(TAPS):
            offset = first - 1 - lag * DILATE[(channel // 2) % 4]
            matrix = matrix + jnp.where(
                gap == offset, taps_ref[lag : lag + 1, channel : channel + 1], 0.0
            )
    if parity == 0:
        matrix = matrix - jnp.where(gap == first, 1.0, 0.0)
    day = lax.broadcasted_iota(jnp.int32, (DAYS, LANES), 0)
    return jnp.where(day < HORIZON, matrix, 0.0)


def prepare(rows, *refs):
    given, refs = refs[:5], refs[5:]
    sums_ref, out_refs, refs = refs[0], refs[1 : 1 + rows], refs[1 + rows :]
    taken, (held, sems) = refs[:5], refs[5:]
    counts_ref, region_ref, node_ref, bins_ref, taps_ref = taken
    copies = [
        pltpu.make_async_copy(source, target, sems.at[at])
        for at, (source, target) in enumerate(zip(given, taken))
    ]
    for at in (4, 3, 0, 1, 2):
        copies[at].start()
    series = counts_ref.shape[0]
    feats = bins_ref.shape[1] // rows
    pad = held.shape[1]
    height = pad + DAYS
    me = lax.axis_index("rows")

    copies[4].wait()
    own_taps = jnp.concatenate(split_parts(tap_matrix(taps_ref, 0)), axis=0)
    store_taps = tap_matrix(taps_ref, 1)

    copies[3].wait()
    turned = bins_ref[...].astype(F32).T
    for row_block in range(rows):
        part = turned[row_block * feats : (row_block + 1) * feats]
        if pad > feats:
            part = jnp.concatenate([part, jnp.zeros((pad - feats, series), F32)], axis=0)
        held[row_block] = part.astype(BF16)
    for step in range(rows):
        bins = held[partner(me, step, rows)]
        for block in range(series // LANES):
            lanes = slice(block * LANES, (block + 1) * LANES)
            out_refs[step][block * height : block * height + pad] = bins[:, lanes]

    for at in (0, 1, 2):
        copies[at].wait()
    counts = counts_ref[...]
    recent = counts_ref[:, HIST - LANES :]
    store = lax.broadcasted_iota(jnp.int32, (STORES, series), 0)
    pick = jnp.where(store == region_ref[...], 1.0, 0.0).astype(BF16)
    totals = jnp.dot(pick, counts, preferred_element_type=F32)
    forecast = lax.dot_general(
        store_taps,
        totals[:, HIST - LANES :],
        ROW_BY_ROW,
        precision=lax.Precision.HIGHEST,
        preferred_element_type=F32,
    )
    over_days = lax.dot_general(
        jnp.ones((DAYS, HIST), F32),
        totals,
        ROW_BY_ROW,
        precision=lax.Precision.HIGHEST,
        preferred_element_type=F32,
    )
    row = lax.broadcasted_iota(jnp.int32, (DAYS, STORES), 0)
    forecast = jnp.where(row == TOTAL_ROW, over_days, forecast)
    sums_ref[...] = jnp.concatenate(
        split_parts(forecast) + [jnp.zeros((DAYS, LANES - PIECES * STORES), BF16)], axis=1
    )

    own = lax.dot_general(own_taps, recent, ROW_BY_ROW, preferred_element_type=F32)
    own = own[:DAYS] + own[DAYS : 2 * DAYS] + own[2 * DAYS :]
    ones = jnp.ones((8, HIST), BF16)
    level = lax.dot_general(ones, counts, ROW_BY_ROW, preferred_element_type=F32)[:1] / HIST
    own = own / level
    day = lax.broadcasted_iota(jnp.int32, (DAYS, series), 0)
    own = jnp.where(day == REGION_ROW, region_ref[...].astype(F32), own)
    own = jnp.where(day == NODE_ROW, node_ref[...].astype(F32), own)
    own = own.astype(BF16)
    for step in range(rows):
        for block in range(series // LANES):
            lanes = slice(block * LANES, (block + 1) * LANES)
            out_refs[step][block * height + pad : (block + 1) * height] = own[:, lanes]


def shared_forecast(sums_refs):
    sums = jnp.zeros((DAYS, STORES), F32)
    for ref in sums_refs:
        parts = ref[...].astype(F32)
        for piece in range(PIECES):
            sums = sums + parts[:, piece * STORES : (piece + 1) * STORES]
    shared = sums / (sums[TOTAL_ROW : TOTAL_ROW + 1] / HIST + 1.0)
    return jnp.concatenate(split_parts(shared), axis=1)


def quantile_level(quant_ref):
    level = F32(0.0)
    for index, value in enumerate(LEVELS):
        level = jnp.where(quant_ref[0] == index, F32(value), level)
    return level


def series_columns(own, shared, level, cols_ref):
    series = own.shape[1]
    day = lax.broadcasted_iota(jnp.int32, (DAYS, series), 0)
    store = lax.broadcasted_iota(jnp.int32, (PIECES * STORES, series), 0) % STORES
    region = own[REGION_ROW : REGION_ROW + 1].astype(jnp.int32)
    node = own[NODE_ROW : NODE_ROW + 1].astype(jnp.int32)
    pick = jnp.where(store == region, 1.0, 0.0).astype(BF16)
    regional = jnp.dot(shared, pick, preferred_element_type=F32)
    wave = jnp.where(day < HORIZON, jnp.tanh(own + regional), 0.0)
    mean = jnp.sum(wave, axis=0, keepdims=True) / HORIZON
    square = jnp.sum(wave * wave, axis=0, keepdims=True) / HORIZON
    gradient = 0.5 + 0.5 * mean - level
    hessian = 0.5 * (1.0 - square)
    here_node = lax.broadcasted_iota(jnp.int32, (NODES, series), 0) == node
    for part, value in enumerate((gradient, hessian)):
        value = value.astype(BF16).astype(F32) * SCALE
        high = value.astype(F8).astype(F32)
        for offset, piece in ((0, high), (2, value - high)):
            at = (part + offset) * NODES
            cols_ref[at : at + NODES] = jnp.where(here_node, piece, 0.0).astype(F8)


def accumulate(rows, sources, feats, first, last, quant_ref, *refs):
    sums_refs, block_refs, refs = refs[:rows], refs[rows : rows + sources], refs[rows + sources :]
    if not first:
        before_ref, refs = refs[0], refs[1:]
    if last:
        hist_ref, best_ref, bins_held, cols_held, hist_held, sem = refs
    else:
        hist_held, bins_held, cols_held = refs
    series = bins_held.shape[2]
    pad = max(feats, 16)
    height = pad + DAYS
    shared = shared_forecast(sums_refs)
    level = quantile_level(quant_ref)
    for source, ref in enumerate(block_refs):
        both = jnp.concatenate(
            [ref[block * height : (block + 1) * height] for block in range(series // LANES)],
            axis=1,
        ).astype(F32)
        bins_held[source] = (both[:feats] - 128.0).astype(jnp.int32)
        series_columns(both[pad:], shared, level, cols_held.at[source])

    bin_at = lax.broadcasted_iota(jnp.int32, (32, series), 0)

    def products(source, feature):
        bins = jnp.broadcast_to(bins_held[source, pl.ds(feature, 1)], (32, series)).astype(jnp.int8)
        onehot = jnp.concatenate(
            [
                jnp.where(
                    bins == (bin_at + (32 * part - 128)).astype(jnp.int8),
                    jnp.ones((), F8),
                    jnp.zeros((), F8),
                )
                for part in range(BINS // 32)
            ],
            axis=0,
        )
        return lax.dot_general(
            cols_held[source], onehot, ROW_BY_ROW, preferred_element_type=F32
        )

    def one_feature(feature):
        product = products(0, feature)
        if sources > 1:
            product = lax.fori_loop(
                1, sources, lambda at, total: total + products(at, feature), product
            )
        hist = (product[: 2 * NODES] + product[2 * NODES :]) * (1.0 / SCALE)
        if not first:
            hist = hist + before_ref[feature]
        hist_held[feature] = hist
        if last:
            pltpu.make_async_copy(hist_held.at[feature], hist_ref.at[feature], sem).start()

    group = min(feats, 8)

    def one_group(at):
        for member in range(group):
            one_feature(at * group + member)

    if not last:
        lax.fori_loop(0, feats // group, lambda at, carry: (one_group(at), carry)[1], 0)
        return

    def beside(at, best):
        one_group(at)
        return group_gains(hist_held, at - 1, group, best)

    one_group(0)
    best = lax.fori_loop(1, feats // group, beside, jnp.zeros((NODES, LANES), F32))
    best = group_gains(hist_held, feats // group - 1, group, best)
    best = best.T
    width = LANES // NODES
    packed = jnp.concatenate(
        [best[at * (feats // width) : (at + 1) * (feats // width)] for at in range(width)], axis=1
    )
    for target in range(best_ref.shape[0]):
        best_ref[target] = packed
    pltpu.make_async_copy(hist_held, hist_ref, sem).wait()


def group_gains(hist_held, at, group, best):
    below = lax.broadcasted_iota(jnp.int32, (BINS, BINS), 0) <= lax.broadcasted_iota(
        jnp.int32, (BINS, BINS), 1
    )
    below = jnp.where(below, 1.0, 0.0).astype(BF16)
    feature_at = lax.broadcasted_iota(jnp.int32, (NODES, LANES), 1)
    last_bin = lax.broadcasted_iota(jnp.int32, (NODES, BINS), 1) == BINS - 1
    hist = hist_held[pl.ds(at * group, group)].reshape(group * 2 * NODES, BINS)
    high = hist.astype(BF16)
    low = (hist - high.astype(F32)).astype(BF16)
    left = jnp.dot(high, below, preferred_element_type=F32) + jnp.dot(
        low, below, preferred_element_type=F32
    )
    left = left.reshape(group, 2, NODES, BINS)
    for member in range(group):
        grad, hess = left[member, 0], left[member, 1]
        all_grad, all_hess = grad[:, BINS - 1 :], hess[:, BINS - 1 :]
        over_grad, over_hess = all_grad - grad, all_hess - hess
        gain = grad * grad / (hess + 1.0) + over_grad * over_grad / (over_hess + 1.0)
        gain = jnp.max(jnp.where(last_bin, -jnp.inf, gain), axis=1, keepdims=True)
        gain = gain - all_grad * all_grad / (all_hess + 1.0)
        best = jnp.where(feature_at == at * group + member, gain, best)
    return best


def shards(daily_unit_counts, region_ids, node_ids, bin_ids, quant_index, filter_kernels):
    rows = lax.axis_size("rows")
    feat_count = lax.axis_size("feat")
    series = daily_unit_counts.shape[0]
    feats = bin_ids.shape[1] // rows
    pad = max(feats, 16)
    height = pad + DAYS
    vmem = pl.BlockSpec(memory_space=pltpu.VMEM)
    smem = pl.BlockSpec(memory_space=pltpu.SMEM)
    hbm = pl.BlockSpec(memory_space=pl.ANY)
    params = pltpu.CompilerParams(vmem_limit_bytes=VMEM_LIMIT)
    regions = region_ids.reshape(1, series)
    nodes = node_ids.reshape(1, series)

    def exchange(array, step):
        pairs = [(at, partner(at, step, rows)) for at in range(rows)]
        return lax.ppermute(array, "rows", pairs)

    sums, *outgoing = pl.pallas_call(
        functools.partial(prepare, rows),
        out_shape=[jax.ShapeDtypeStruct((DAYS, LANES), BF16)]
        + [jax.ShapeDtypeStruct((series // LANES * height, LANES), BF16)] * rows,
        in_specs=[hbm] * 5,
        out_specs=[vmem] * (1 + rows),
        scratch_shapes=[
            pltpu.VMEM(daily_unit_counts.shape, BF16),
            pltpu.VMEM((1, series), jnp.int32),
            pltpu.VMEM((1, series), jnp.int32),
            pltpu.VMEM(bin_ids.shape, jnp.int32),
            pltpu.VMEM((TAPS, CHANNELS), F32),
            pltpu.VMEM((rows, pad, series), BF16),
            pltpu.SemaphoreType.DMA((5,)),
        ],
        compiler_params=params,
        name="prepare",
    )(
        *(
            pltpu.with_memory_space_constraint(array, pltpu.HBM)
            for array in (daily_unit_counts, regions, nodes, bin_ids, filter_kernels.T)
        )
    )
    sums = [sums] + [exchange(sums, step) for step in range(1, rows)]
    arrived = [outgoing[0]]
    for step in range(1, rows):
        block = outgoing[step]
        if step == rows - 1:
            block, sums[1:] = lax.optimization_barrier((block, sums[1:]))
        arrived.append(exchange(block, step))

    targets = rows * feat_count
    packed_rows = feats * NODES // LANES
    hist_shape = jax.ShapeDtypeStruct((feats, 2 * NODES, BINS), F32)
    steps = [arrived[at : at + 1] for at in range(min(rows, 4) - 1)]
    steps.append(arrived[len(steps) :])
    histogram = None
    for at, blocks in enumerate(steps):
        first, last = at == 0, at == len(steps) - 1
        count = len(blocks)
        held = [
            pltpu.VMEM((count, feats, series), jnp.int32),
            pltpu.VMEM((count, 4 * NODES, series), F8),
        ]
        operands = [quant_index, *sums, *blocks] + ([] if first else [histogram])
        if last:
            held += [pltpu.VMEM(hist_shape.shape, F32), pltpu.SemaphoreType.DMA]
            out_shape = [hist_shape, jax.ShapeDtypeStruct((targets, packed_rows, LANES), F32)]
            out_specs = [hbm, vmem]
        else:
            out_shape, out_specs = hist_shape, vmem
        histogram = pl.pallas_call(
            functools.partial(accumulate, rows, count, feats, first, last),
            out_shape=out_shape,
            in_specs=[smem] + [vmem] * (len(operands) - 1),
            out_specs=out_specs,
            scratch_shapes=held,
            input_output_aliases={} if first or last else {len(operands) - 1: 0},
            compiler_params=params,
            name=f"accumulate_{at}",
        )(*operands)
    histogram, best = histogram

    gathered = lax.all_to_all(best, ("feat", "rows"), 0, 0, tiled=True)
    width = LANES // NODES
    feature_best = (
        gathered.reshape(feat_count, rows, packed_rows, width, NODES)
        .transpose(0, 1, 3, 2, 4)
        .reshape(feat_count, rows, feats, NODES)
    )
    return histogram.reshape(1, 1, feats, 2, NODES, BINS), feature_best


def solution(mesh):
    in_specs = (
        P(("groups", "rows"), None),
        P(("groups", "rows")),
        P(("groups", "rows")),
        P(("groups", "rows"), "feat"),
        P("groups"),
        P(),
    )
    out_specs = (
        P(("groups", "feat"), "rows", None, None, None, None),
        P("groups", None, None, None),
    )
    return jax.shard_map(shards, mesh=mesh, in_specs=in_specs, out_specs=out_specs, check_vma=False)
```

```python
import functools

import jax
import jax.numpy as jnp
from jax import lax
from jax.experimental import pallas as pl
from jax.experimental.pallas import tpu as pltpu
from jax.sharding import PartitionSpec as P

BINS = 256
NODES = 32
HIST = 512
HORIZON = 28
FIRST_DAY = HIST - HORIZON
REGIONS = 10
CHANNELS = 8
TAPS = 4
DILATE = (1, 7, 14, 28)
LEVELS = (0.005, 0.025, 0.165, 0.25, 0.5, 0.75, 0.835, 0.975, 0.995)

LANES = 128
DAYS = 32
REGION_ROW = HORIZON
NODE_ROW = HORIZON + 1
TOTAL_ROW = HORIZON
LEVEL_ROW = HORIZON + 1
STORES = 16
PIECES = 3
SCALE = 256.0
BF16 = jnp.bfloat16
F32 = jnp.float32
F8 = jnp.float8_e4m3fn
ROW_BY_ROW = (((1,), (1,)), ((), ()))
VMEM_LIMIT = 24 * 2**20


def partner(position, step, count):
    if count & (count - 1) == 0:
        return position ^ step
    return (position + step) % count


def split_parts(values):
    parts = []
    rest = values
    for _ in range(PIECES):
        part = rest.astype(BF16)
        parts.append(part)
        rest = rest - part.astype(F32)
    return parts


def tap_matrix(taps_ref, parity):
    gap = lax.broadcasted_iota(jnp.int32, (DAYS, LANES), 1) - lax.broadcasted_iota(
        jnp.int32, (DAYS, LANES), 0
    )
    first = FIRST_DAY - (HIST - LANES)
    matrix = jnp.zeros((DAYS, LANES), F32)
    for channel in range(parity, CHANNELS, 2):
        for lag in range(TAPS):
            offset = first - 1 - lag * DILATE[(channel // 2) % 4]
            matrix = matrix + jnp.where(
                gap == offset, taps_ref[lag : lag + 1, channel : channel + 1], 0.0
            )
    if parity == 0:
        matrix = matrix - jnp.where(gap == first, 1.0, 0.0)
    day = lax.broadcasted_iota(jnp.int32, (DAYS, LANES), 0)
    return jnp.where(day < HORIZON, matrix, 0.0)


def prepare(rows, *refs):
    given, refs = refs[:5], refs[5:]
    sums_ref, out_refs, refs = refs[0], refs[1 : 1 + rows], refs[1 + rows :]
    taken, (held, sems) = refs[:5], refs[5:]
    counts_ref, region_ref, node_ref, bins_ref, taps_ref = taken
    copies = [
        pltpu.make_async_copy(source, target, sems.at[at])
        for at, (source, target) in enumerate(zip(given, taken))
    ]
    for at in (4, 3, 0, 1, 2):
        copies[at].start()
    series = counts_ref.shape[0]
    feats = bins_ref.shape[1] // rows
    pad = held.shape[1]
    height = pad + DAYS
    me = lax.axis_index("rows")

    copies[4].wait()
    own_taps = jnp.concatenate(split_parts(tap_matrix(taps_ref, 0)), axis=0)
    store_taps = tap_matrix(taps_ref, 1)

    copies[3].wait()
    turned = bins_ref[...].astype(F32).T
    for row_block in range(rows):
        part = turned[row_block * feats : (row_block + 1) * feats]
        if pad > feats:
            part = jnp.concatenate([part, jnp.zeros((pad - feats, series), F32)], axis=0)
        held[row_block] = part.astype(BF16)
    for step in range(rows):
        bins = held[partner(me, step, rows)]
        for block in range(series // LANES):
            lanes = slice(block * LANES, (block + 1) * LANES)
            out_refs[step][block * height : block * height + pad] = bins[:, lanes]

    for at in (0, 1, 2):
        copies[at].wait()
    counts = counts_ref[...]
    recent = counts_ref[:, HIST - LANES :]
    store = lax.broadcasted_iota(jnp.int32, (STORES, series), 0)
    pick = jnp.where(store == region_ref[...], 1.0, 0.0).astype(BF16)
    totals = jnp.dot(pick, counts, preferred_element_type=F32)
    forecast = lax.dot_general(
        store_taps,
        totals[:, HIST - LANES :],
        ROW_BY_ROW,
        precision=lax.Precision.HIGHEST,
        preferred_element_type=F32,
    )
    over_days = lax.dot_general(
        jnp.ones((DAYS, HIST), F32),
        totals,
        ROW_BY_ROW,
        precision=lax.Precision.HIGHEST,
        preferred_element_type=F32,
    )
    row = lax.broadcasted_iota(jnp.int32, (DAYS, STORES), 0)
    forecast = jnp.where(row == TOTAL_ROW, over_days, forecast)
    sums_ref[...] = jnp.concatenate(
        split_parts(forecast) + [jnp.zeros((DAYS, LANES - PIECES * STORES), BF16)], axis=1
    )

    own = lax.dot_general(own_taps, recent, ROW_BY_ROW, preferred_element_type=F32)
    own = own[:DAYS] + own[DAYS : 2 * DAYS] + own[2 * DAYS :]
    ones = jnp.ones((8, HIST), BF16)
    level = lax.dot_general(ones, counts, ROW_BY_ROW, preferred_element_type=F32)[:1] / HIST
    own = own / level
    day = lax.broadcasted_iota(jnp.int32, (DAYS, series), 0)
    own = jnp.where(day == REGION_ROW, region_ref[...].astype(F32), own)
    own = jnp.where(day == NODE_ROW, node_ref[...].astype(F32), own)
    own = own.astype(BF16)
    for step in range(rows):
        for block in range(series // LANES):
            lanes = slice(block * LANES, (block + 1) * LANES)
            out_refs[step][block * height + pad : (block + 1) * height] = own[:, lanes]


def leader(position, count):
    return position | 1 if position | 1 < count else position


def combine(rows, quant_ref, *refs):
    sums_refs, shared_ref = refs[:rows], refs[rows]
    level = F32(0.0)
    for index, value in enumerate(LEVELS):
        level = jnp.where(quant_ref[:, :1] == index, F32(value), level)
    sums = jnp.zeros((DAYS, STORES), F32)
    for ref in sums_refs:
        parts = ref[...].astype(F32)
        for piece in range(PIECES):
            sums = sums + parts[:, piece * STORES : (piece + 1) * STORES]
    shared = sums / (sums[TOTAL_ROW : TOTAL_ROW + 1] / HIST + 1.0)
    row = lax.broadcasted_iota(jnp.int32, (DAYS, STORES), 0)
    shared = jnp.where(row == LEVEL_ROW, level, shared)
    shared_ref[...] = jnp.concatenate(
        split_parts(shared) + [jnp.zeros((DAYS, LANES - PIECES * STORES), BF16)], axis=1
    )


def series_columns(own, shared, cols_ref):
    series = own.shape[1]
    day = lax.broadcasted_iota(jnp.int32, (DAYS, series), 0)
    store = lax.broadcasted_iota(jnp.int32, (PIECES * STORES, series), 0) % STORES
    region = own[REGION_ROW : REGION_ROW + 1].astype(jnp.int32)
    node = own[NODE_ROW : NODE_ROW + 1].astype(jnp.int32)
    pick = jnp.where(store == region, 1.0, 0.0).astype(BF16)
    shared = shared[:, : PIECES * STORES]
    regional = jnp.dot(shared, pick, preferred_element_type=F32)
    level = shared[LEVEL_ROW : LEVEL_ROW + 1].astype(F32)
    level = sum(level[:, piece * STORES : piece * STORES + 1] for piece in range(PIECES))
    wave = jnp.where(day < HORIZON, jnp.tanh(own + regional), 0.0)
    mean = jnp.sum(wave, axis=0, keepdims=True) / HORIZON
    square = jnp.sum(wave * wave, axis=0, keepdims=True) / HORIZON
    gradient = 0.5 + 0.5 * mean - level
    hessian = 0.5 * (1.0 - square)
    here_node = lax.broadcasted_iota(jnp.int32, (NODES, series), 0) == node
    for part, value in enumerate((gradient, hessian)):
        value = value.astype(BF16).astype(F32) * SCALE
        high = value.astype(F8).astype(F32)
        for offset, piece in ((0, high), (2, value - high)):
            at = (part + offset) * NODES
            cols_ref[at : at + NODES] = jnp.where(here_node, piece, 0.0).astype(F8)


def accumulate(sources, feats, first, last, led, leader_ref, own_ref, *refs):
    block_refs, refs = refs[:sources], refs[sources:]
    if not first:
        before_ref, refs = refs[0], refs[1:]
    if last:
        hist_ref, best_ref, bins_held, cols_held, hist_held, sem = refs
    else:
        left_ref, bins_held, cols_held = refs
    series = bins_held.shape[2]
    pad = max(feats, 16)
    height = pad + DAYS
    shared = jnp.where(led(lax.axis_index("feat")), leader_ref[...], own_ref[...])
    for source, ref in enumerate(block_refs):
        both = jnp.concatenate(
            [ref[block * height : (block + 1) * height] for block in range(series // LANES)],
            axis=1,
        ).astype(F32)
        bins_held[source] = (both[:feats] - 128.0).astype(jnp.int32)
        series_columns(both[pad:], shared, cols_held.at[source])

    bin_at = lax.broadcasted_iota(jnp.int32, (32, series), 0)

    def products(source, feature):
        bins = jnp.broadcast_to(bins_held[source, pl.ds(feature, 1)], (32, series)).astype(jnp.int8)
        upto = jnp.concatenate(
            [
                jnp.where(
                    bins <= (bin_at + (32 * part - 128)).astype(jnp.int8),
                    jnp.ones((), F8),
                    jnp.zeros((), F8),
                )
                for part in range(BINS // 32)
            ],
            axis=0,
        )
        return lax.dot_general(cols_held[source], upto, ROW_BY_ROW, preferred_element_type=F32)

    def one_feature(feature):
        product = products(0, feature)
        if sources > 1:
            product = lax.fori_loop(
                1, sources, lambda at, total: total + products(at, feature), product
            )
        left = product[: 2 * NODES] + product[2 * NODES :]
        return left if first else left + before_ref[feature]

    group = min(feats, 32 if last else 16)

    if not last:

        def one_group(at, carry):
            for member in range(group):
                feature = at * group + member
                left_ref[feature] = one_feature(feature)
            return carry

        lax.fori_loop(0, feats // group, one_group, 0)
        return

    feature_at = lax.broadcasted_iota(jnp.int32, (NODES, LANES), 1)
    bin_lane = lax.broadcasted_iota(jnp.int32, (2 * NODES, BINS), 1)
    last_bin = bin_lane[:NODES] == BINS - 1

    chunk = min(group, 8)

    def histogram(feature):
        left = one_feature(feature) * (1.0 / SCALE)
        before = jnp.where(bin_lane == 0, 0.0, pltpu.roll(left, 1, axis=1))
        hist_held[feature] = left - before
        return left

    def gains(feature, left, best):
        grad, hess = left[:NODES], left[NODES:]
        all_grad, all_hess = grad[:, BINS - 1 :], hess[:, BINS - 1 :]
        over_grad, over_hess = all_grad - grad, all_hess - hess
        gain = grad * grad / (hess + 1.0) + over_grad * over_grad / (over_hess + 1.0)
        gain = jnp.max(jnp.where(last_bin, -jnp.inf, gain), axis=1, keepdims=True)
        gain = gain - all_grad * all_grad / (all_hess + 1.0)
        return jnp.where(feature_at == feature, gain, best)

    def final_group(at, best):
        waiting = []
        for member in range(group):
            feature = at * group + member
            waiting.append((feature, histogram(feature)))
            if member % chunk == chunk - 1:
                here = pl.ds(feature - chunk + 1, chunk)
                pltpu.make_async_copy(hist_held.at[here], hist_ref.at[here], sem).start()
                for feature, left in waiting:
                    best = gains(feature, left, best)
                waiting = []
        return best

    best = lax.fori_loop(0, feats // group, final_group, jnp.zeros((NODES, LANES), F32))
    best = best.T
    width = LANES // NODES
    packed = jnp.concatenate(
        [best[at * (feats // width) : (at + 1) * (feats // width)] for at in range(width)], axis=1
    )
    for target in range(best_ref.shape[0]):
        best_ref[target] = packed
    pltpu.make_async_copy(hist_held, hist_ref, sem).wait()


def shards(daily_unit_counts, region_ids, node_ids, bin_ids, quant_index, filter_kernels):
    rows = lax.axis_size("rows")
    feat_count = lax.axis_size("feat")
    series = daily_unit_counts.shape[0]
    feats = bin_ids.shape[1] // rows
    pad = max(feats, 16)
    height = pad + DAYS
    vmem = pl.BlockSpec(memory_space=pltpu.VMEM)
    hbm = pl.BlockSpec(memory_space=pl.ANY)
    params = pltpu.CompilerParams(vmem_limit_bytes=VMEM_LIMIT)
    regions = region_ids.reshape(1, series)
    nodes = node_ids.reshape(1, series)

    def exchange(array, step):
        pairs = [(at, partner(at, step, rows)) for at in range(rows)]
        return lax.ppermute(array, "rows", pairs)

    sums, *outgoing = pl.pallas_call(
        functools.partial(prepare, rows),
        out_shape=[jax.ShapeDtypeStruct((DAYS, LANES), BF16)]
        + [jax.ShapeDtypeStruct((series // LANES * height, LANES), BF16)] * rows,
        in_specs=[hbm] * 5,
        out_specs=[vmem] * (1 + rows),
        scratch_shapes=[
            pltpu.VMEM(daily_unit_counts.shape, BF16),
            pltpu.VMEM((1, series), jnp.int32),
            pltpu.VMEM((1, series), jnp.int32),
            pltpu.VMEM(bin_ids.shape, jnp.int32),
            pltpu.VMEM((TAPS, CHANNELS), F32),
            pltpu.VMEM((rows, pad, series), BF16),
            pltpu.SemaphoreType.DMA((5,)),
        ],
        compiler_params=params,
        name="prepare",
    )(
        *(
            pltpu.with_memory_space_constraint(array, pltpu.HBM)
            for array in (daily_unit_counts, regions, nodes, bin_ids, filter_kernels.T)
        )
    )
    leads = sorted({leader(at, feat_count) for at in range(feat_count)})
    sums = [sums]
    for step in range(1, rows):
        pairs = [
            (at * feat_count + lead, partner(at, step, rows) * feat_count + lead)
            for at in range(rows)
            for lead in leads
        ]
        sums.append(lax.ppermute(sums[0], ("rows", "feat"), pairs))
    arrived = [outgoing[0]]
    quant = lax.pad(quant_index, jnp.int32(0), [(0, LANES - 1, 0)]).reshape(1, LANES)
    for step in range(1, rows):
        block = outgoing[step]
        if step == rows - 1:
            block, sums[1:] = lax.optimization_barrier((block, sums[1:]))
        arrived.append(exchange(block, step))

    shared = pl.pallas_call(
        functools.partial(combine, rows),
        out_shape=jax.ShapeDtypeStruct((DAYS, LANES), BF16),
        in_specs=[vmem] * (1 + rows),
        out_specs=vmem,
        compiler_params=params,
        name="combine",
    )(quant, *sums)
    followers = [at for at in range(feat_count) if leader(at, feat_count) != at]
    pairs = [(leader(at, feat_count), at) for at in followers]
    leaders_shared = lax.ppermute(shared, "feat", pairs)

    def led(position):
        return sum((position == at).astype(jnp.int32) for at in followers) > 0

    targets = rows * feat_count
    packed_rows = feats * NODES // LANES
    hist_shape = jax.ShapeDtypeStruct((feats, 2 * NODES, BINS), F32)
    steps = [arrived[at : at + 1] for at in range(min(rows, 4) - 1)]
    steps.append(arrived[len(steps) :])
    histogram = None
    for at, blocks in enumerate(steps):
        first, last = at == 0, at == len(steps) - 1
        count = len(blocks)
        held = [
            pltpu.VMEM((count, feats, series), jnp.int32),
            pltpu.VMEM((count, 4 * NODES, series), F8),
        ]
        operands = [leaders_shared, shared, *blocks] + ([] if first else [histogram])
        if last:
            held += [pltpu.VMEM(hist_shape.shape, F32), pltpu.SemaphoreType.DMA]
            out_shape = [hist_shape, jax.ShapeDtypeStruct((targets, packed_rows, LANES), F32)]
            out_specs = [hbm, vmem]
        else:
            out_shape, out_specs = hist_shape, vmem
        histogram = pl.pallas_call(
            functools.partial(accumulate, count, feats, first, last, led),
            out_shape=out_shape,
            in_specs=[vmem] * len(operands),
            out_specs=out_specs,
            scratch_shapes=held,
            input_output_aliases={} if first or last else {len(operands) - 1: 0},
            compiler_params=params,
            name=f"accumulate_{at}",
        )(*operands)
    histogram, best = histogram

    gathered = lax.all_to_all(best, ("feat", "rows"), 0, 0, tiled=True)
    width = LANES // NODES
    feature_best = (
        gathered.reshape(feat_count, rows, packed_rows, width, NODES)
        .transpose(0, 1, 3, 2, 4)
        .reshape(feat_count, rows, feats, NODES)
    )
    return histogram.reshape(1, 1, feats, 2, NODES, BINS), feature_best


def solution(mesh):
    in_specs = (
        P(("groups", "rows"), None),
        P(("groups", "rows")),
        P(("groups", "rows")),
        P(("groups", "rows"), "feat"),
        P("groups"),
        P(),
    )
    out_specs = (
        P(("groups", "feat"), "rows", None, None, None, None),
        P("groups", None, None, None),
    )
    return jax.shard_map(shards, mesh=mesh, in_specs=in_specs, out_specs=out_specs, check_vma=False)
```

```python
import functools

import jax
import jax.numpy as jnp
from jax import lax
from jax.experimental import pallas as pl
from jax.experimental.pallas import tpu as pltpu
from jax.sharding import PartitionSpec as P

BINS = 256
NODES = 32
HIST = 512
HORIZON = 28
FIRST_DAY = HIST - HORIZON
REGIONS = 10
CHANNELS = 8
TAPS = 4
DILATE = (1, 7, 14, 28)
LEVELS = (0.005, 0.025, 0.165, 0.25, 0.5, 0.75, 0.835, 0.975, 0.995)

LANES = 128
DAYS = 32
REGION_ROW = HORIZON
NODE_ROW = HORIZON + 1
TOTAL_ROW = HORIZON
STORES = 16
PIECES = 3
SCALE = 256.0
BF16 = jnp.bfloat16
F32 = jnp.float32
F8 = jnp.float8_e4m3fn
ROW_BY_ROW = (((1,), (1,)), ((), ()))
VMEM_LIMIT = 24 * 2**20


def partner(position, step, count):
    if count & (count - 1) == 0:
        return position ^ step
    return (position + step) % count


def split_parts(values):
    parts = []
    rest = values
    for _ in range(PIECES):
        part = rest.astype(BF16)
        parts.append(part)
        rest = rest - part.astype(F32)
    return parts


def tap_matrix(taps_ref, parity):
    gap = lax.broadcasted_iota(jnp.int32, (DAYS, LANES), 1) - lax.broadcasted_iota(
        jnp.int32, (DAYS, LANES), 0
    )
    first = FIRST_DAY - (HIST - LANES)
    matrix = jnp.zeros((DAYS, LANES), F32)
    for channel in range(parity, CHANNELS, 2):
        for lag in range(TAPS):
            offset = first - 1 - lag * DILATE[(channel // 2) % 4]
            matrix = matrix + jnp.where(
                gap == offset, taps_ref[lag : lag + 1, channel : channel + 1], 0.0
            )
    if parity == 0:
        matrix = matrix - jnp.where(gap == first, 1.0, 0.0)
    day = lax.broadcasted_iota(jnp.int32, (DAYS, LANES), 0)
    return jnp.where(day < HORIZON, matrix, 0.0)


def prepare(rows, *refs):
    given, refs = refs[:5], refs[5:]
    sums_ref, own_ref, out_refs, refs = refs[0], refs[1], refs[2 : 2 + rows], refs[2 + rows :]
    taken, (held, sems) = refs[:5], refs[5:]
    counts_ref, region_ref, node_ref, bins_ref, taps_ref = taken
    copies = [
        pltpu.make_async_copy(source, target, sems.at[at])
        for at, (source, target) in enumerate(zip(given, taken))
    ]
    for at in (4, 3, 0, 1, 2):
        copies[at].start()
    series = counts_ref.shape[0]
    feats = bins_ref.shape[1] // rows
    pad = held.shape[1]
    me = lax.axis_index("rows")

    copies[4].wait()
    own_taps = jnp.concatenate(split_parts(tap_matrix(taps_ref, 0)), axis=0)
    store_taps = tap_matrix(taps_ref, 1)

    copies[3].wait()
    turned = bins_ref[...].astype(F32).T
    for row_block in range(rows):
        part = turned[row_block * feats : (row_block + 1) * feats]
        if pad > feats:
            part = jnp.concatenate([part, jnp.zeros((pad - feats, series), F32)], axis=0)
        held[row_block] = part.astype(BF16)
    for step in range(rows):
        bins = held[partner(me, step, rows)]
        for block in range(series // LANES):
            lanes = slice(block * LANES, (block + 1) * LANES)
            out_refs[step][block * pad : (block + 1) * pad] = bins[:, lanes]

    for at in (0, 1, 2):
        copies[at].wait()
    counts = counts_ref[...]
    recent = counts_ref[:, HIST - LANES :]
    store = lax.broadcasted_iota(jnp.int32, (STORES, series), 0)
    pick = jnp.where(store == region_ref[...], 1.0, 0.0).astype(BF16)
    totals = jnp.dot(pick, counts, preferred_element_type=F32)
    forecast = lax.dot_general(
        store_taps,
        totals[:, HIST - LANES :],
        ROW_BY_ROW,
        precision=lax.Precision.HIGHEST,
        preferred_element_type=F32,
    )
    over_days = lax.dot_general(
        jnp.ones((DAYS, HIST), F32),
        totals,
        ROW_BY_ROW,
        precision=lax.Precision.HIGHEST,
        preferred_element_type=F32,
    )
    row = lax.broadcasted_iota(jnp.int32, (DAYS, STORES), 0)
    forecast = jnp.where(row == TOTAL_ROW, over_days, forecast)
    sums_ref[...] = jnp.concatenate(
        split_parts(forecast) + [jnp.zeros((DAYS, LANES - PIECES * STORES), BF16)], axis=1
    )

    own = lax.dot_general(own_taps, recent, ROW_BY_ROW, preferred_element_type=F32)
    own = own[:DAYS] + own[DAYS : 2 * DAYS] + own[2 * DAYS :]
    ones = jnp.ones((8, HIST), BF16)
    level = lax.dot_general(ones, counts, ROW_BY_ROW, preferred_element_type=F32)[:1] / HIST
    own = own / level
    day = lax.broadcasted_iota(jnp.int32, (DAYS, series), 0)
    own = jnp.where(day == REGION_ROW, region_ref[...].astype(F32), own)
    own = jnp.where(day == NODE_ROW, node_ref[...].astype(F32), own)
    own_ref[...] = own


def columns(rows, quant_ref, *refs):
    sums_refs, own_ref, refs = refs[:rows], refs[rows], refs[rows + 1 :]
    bins_refs, out_refs = refs[:rows], refs[rows:]
    series = own_ref.shape[1]
    behind = bins_refs[0].shape[0]
    level = F32(0.0)
    for index, value in enumerate(LEVELS):
        level = jnp.where(quant_ref[0] == index, F32(value), level)
    sums = jnp.zeros((DAYS, STORES), F32)
    for ref in sums_refs:
        parts = ref[...].astype(F32)
        for piece in range(PIECES):
            sums = sums + parts[:, piece * STORES : (piece + 1) * STORES]
    shared = sums / (sums[TOTAL_ROW : TOTAL_ROW + 1] / HIST + 1.0)
    shared = jnp.concatenate(split_parts(shared), axis=1)

    own = own_ref[...]
    day = lax.broadcasted_iota(jnp.int32, (DAYS, series), 0)
    store = lax.broadcasted_iota(jnp.int32, (PIECES * STORES, series), 0) % STORES
    region = own[REGION_ROW : REGION_ROW + 1].astype(jnp.int32)
    pick = jnp.where(store == region, 1.0, 0.0).astype(BF16)
    regional = jnp.dot(shared, pick, preferred_element_type=F32)
    wave = jnp.where(day < HORIZON, jnp.tanh(own + regional), 0.0)
    mean = jnp.sum(wave, axis=0, keepdims=True) / HORIZON
    square = jnp.sum(wave * wave, axis=0, keepdims=True) / HORIZON
    gradient = 0.5 + 0.5 * mean - level
    hessian = 0.5 * (1.0 - square)
    rows_of = [
        value[:, block * LANES : (block + 1) * LANES]
        for value in (gradient, hessian, own[NODE_ROW : NODE_ROW + 1])
        for block in range(series // LANES)
    ]
    spare = jnp.zeros((out_refs[0].shape[0] - behind - len(rows_of), LANES), F32)
    tail = jnp.concatenate(rows_of + [spare], axis=0).astype(BF16)
    for bins_ref, out_ref in zip(bins_refs, out_refs):
        out_ref[:behind] = bins_ref[...]
        out_ref[behind:] = tail


def place(tail, cols_ref):
    blocks = cols_ref.shape[1] // LANES
    gradient, hessian, node = (
        jnp.concatenate(
            [tail[at * blocks + block : at * blocks + block + 1] for block in range(blocks)], axis=1
        )
        for at in range(3)
    )
    node_at = lax.broadcasted_iota(jnp.int32, (NODES, cols_ref.shape[1]), 0)
    here_node = node_at == node.astype(jnp.int32)
    for part, value in enumerate((gradient, hessian)):
        value = value * SCALE
        high = value.astype(F8).astype(F32)
        for offset, piece in ((0, high), (2, value - high)):
            at = (part + offset) * NODES
            cols_ref[at : at + NODES] = jnp.where(here_node, piece, 0.0).astype(F8)


def accumulate(sources, feats, first, last, *refs):
    block_refs, refs = refs[:sources], refs[sources:]
    if not first:
        before_ref, refs = refs[0], refs[1:]
    if last:
        hist_ref, best_ref, bins_held, cols_held, hist_held, sem = refs
    else:
        left_ref, bins_held, cols_held = refs
    series = bins_held.shape[2]
    pad = max(feats, 16)
    behind = series // LANES * pad
    for source, ref in enumerate(block_refs):
        bins = jnp.concatenate(
            [ref[block * pad : (block + 1) * pad] for block in range(series // LANES)], axis=1
        )
        bins_held[source] = (bins[:feats].astype(F32) - 128.0).astype(jnp.int32)
        place(ref[behind:].astype(F32), cols_held.at[source])

    bin_at = lax.broadcasted_iota(jnp.int32, (32, series), 0)

    def products(source, feature):
        bins = jnp.broadcast_to(bins_held[source, pl.ds(feature, 1)], (32, series)).astype(jnp.int8)
        upto = jnp.concatenate(
            [
                jnp.where(
                    bins <= (bin_at + (32 * part - 128)).astype(jnp.int8),
                    jnp.ones((), F8),
                    jnp.zeros((), F8),
                )
                for part in range(BINS // 32)
            ],
            axis=0,
        )
        return lax.dot_general(cols_held[source], upto, ROW_BY_ROW, preferred_element_type=F32)

    def one_feature(feature):
        product = products(0, feature)
        if sources > 1:
            product = lax.fori_loop(
                1, sources, lambda at, total: total + products(at, feature), product
            )
        left = product[: 2 * NODES] + product[2 * NODES :]
        return left if first else left + before_ref[feature]

    group = min(feats, 32 if last else 16)

    if not last:

        def one_group(at, carry):
            for member in range(group):
                feature = at * group + member
                left_ref[feature] = one_feature(feature)
            return carry

        lax.fori_loop(0, feats // group, one_group, 0)
        return

    feature_at = lax.broadcasted_iota(jnp.int32, (NODES, LANES), 1)
    bin_lane = lax.broadcasted_iota(jnp.int32, (2 * NODES, BINS), 1)
    last_bin = bin_lane[:NODES] == BINS - 1

    chunk = min(group, 8)

    def histogram(feature):
        left = one_feature(feature) * (1.0 / SCALE)
        before = jnp.where(bin_lane == 0, 0.0, pltpu.roll(left, 1, axis=1))
        hist_held[feature] = left - before
        return left

    def gains(feature, left, best):
        grad, hess = left[:NODES], left[NODES:]
        all_grad, all_hess = grad[:, BINS - 1 :], hess[:, BINS - 1 :]
        over_grad, over_hess = all_grad - grad, all_hess - hess
        gain = grad * grad / (hess + 1.0) + over_grad * over_grad / (over_hess + 1.0)
        gain = jnp.max(jnp.where(last_bin, -jnp.inf, gain), axis=1, keepdims=True)
        gain = gain - all_grad * all_grad / (all_hess + 1.0)
        return jnp.where(feature_at == feature, gain, best)

    def final_group(at, best):
        waiting = []
        for member in range(group):
            feature = at * group + member
            waiting.append((feature, histogram(feature)))
            if member % chunk == chunk - 1:
                here = pl.ds(feature - chunk + 1, chunk)
                pltpu.make_async_copy(hist_held.at[here], hist_ref.at[here], sem).start()
                for feature, left in waiting:
                    best = gains(feature, left, best)
                waiting = []
        return best

    best = lax.fori_loop(0, feats // group, final_group, jnp.zeros((NODES, LANES), F32))
    best = best.T
    width = LANES // NODES
    packed = jnp.concatenate(
        [best[at * (feats // width) : (at + 1) * (feats // width)] for at in range(width)], axis=1
    )
    for target in range(best_ref.shape[0]):
        best_ref[target] = packed
    pltpu.make_async_copy(hist_held, hist_ref, sem).wait()


def shards(daily_unit_counts, region_ids, node_ids, bin_ids, quant_index, filter_kernels):
    rows = lax.axis_size("rows")
    feat_count = lax.axis_size("feat")
    series = daily_unit_counts.shape[0]
    feats = bin_ids.shape[1] // rows
    pad = max(feats, 16)
    blocks = series // LANES
    vmem = pl.BlockSpec(memory_space=pltpu.VMEM)
    smem = pl.BlockSpec(memory_space=pltpu.SMEM)
    hbm = pl.BlockSpec(memory_space=pl.ANY)
    params = pltpu.CompilerParams(vmem_limit_bytes=VMEM_LIMIT)
    regions = region_ids.reshape(1, series)
    nodes = node_ids.reshape(1, series)

    def exchange(array, step):
        pairs = [(at, partner(at, step, rows)) for at in range(rows)]
        return lax.ppermute(array, "rows", pairs)

    sums, own, *bins = pl.pallas_call(
        functools.partial(prepare, rows),
        out_shape=[jax.ShapeDtypeStruct((DAYS, LANES), BF16)]
        + [jax.ShapeDtypeStruct((DAYS, series), F32)]
        + [jax.ShapeDtypeStruct((blocks * pad, LANES), BF16)] * rows,
        in_specs=[hbm] * 5,
        out_specs=[vmem] * (2 + rows),
        scratch_shapes=[
            pltpu.VMEM(daily_unit_counts.shape, BF16),
            pltpu.VMEM((1, series), jnp.int32),
            pltpu.VMEM((1, series), jnp.int32),
            pltpu.VMEM(bin_ids.shape, jnp.int32),
            pltpu.VMEM((TAPS, CHANNELS), F32),
            pltpu.VMEM((rows, pad, series), BF16),
            pltpu.SemaphoreType.DMA((5,)),
        ],
        compiler_params=params,
        name="prepare",
    )(
        *(
            pltpu.with_memory_space_constraint(array, pltpu.HBM)
            for array in (daily_unit_counts, regions, nodes, bin_ids, filter_kernels.T)
        )
    )
    sums = [sums] + [exchange(sums, step) for step in range(1, rows)]
    outgoing = pl.pallas_call(
        functools.partial(columns, rows),
        out_shape=[jax.ShapeDtypeStruct((blocks * pad + 4 * blocks, LANES), BF16)] * rows,
        in_specs=[smem] + [vmem] * (2 * rows + 1),
        out_specs=[vmem] * rows,
        compiler_params=params,
        name="columns",
    )(quant_index, *sums, own, *bins)
    arrived = [outgoing[0]] + [exchange(outgoing[step], step) for step in range(1, rows)]

    targets = rows * feat_count
    packed_rows = feats * NODES // LANES
    hist_shape = jax.ShapeDtypeStruct((feats, 2 * NODES, BINS), F32)
    steps = [arrived[at : at + 1] for at in range(min(rows, 4) - 1)]
    steps.append(arrived[len(steps) :])
    histogram = None
    for at, sources in enumerate(steps):
        first, last = at == 0, at == len(steps) - 1
        count = len(sources)
        held = [
            pltpu.VMEM((count, feats, series), jnp.int32),
            pltpu.VMEM((count, 4 * NODES, series), F8),
        ]
        operands = sources + ([] if first else [histogram])
        if last:
            held += [pltpu.VMEM(hist_shape.shape, F32), pltpu.SemaphoreType.DMA]
            out_shape = [hist_shape, jax.ShapeDtypeStruct((targets, packed_rows, LANES), F32)]
            out_specs = [hbm, vmem]
        else:
            out_shape, out_specs = hist_shape, vmem
        histogram = pl.pallas_call(
            functools.partial(accumulate, count, feats, first, last),
            out_shape=out_shape,
            in_specs=[vmem] * len(operands),
            out_specs=out_specs,
            scratch_shapes=held,
            input_output_aliases={} if first or last else {len(operands) - 1: 0},
            compiler_params=params,
            name=f"accumulate_{at}",
        )(*operands)
    histogram, best = histogram

    gathered = lax.all_to_all(best, ("feat", "rows"), 0, 0, tiled=True)
    width = LANES // NODES
    feature_best = (
        gathered.reshape(feat_count, rows, packed_rows, width, NODES)
        .transpose(0, 1, 3, 2, 4)
        .reshape(feat_count, rows, feats, NODES)
    )
    return histogram.reshape(1, 1, feats, 2, NODES, BINS), feature_best


def solution(mesh):
    in_specs = (
        P(("groups", "rows"), None),
        P(("groups", "rows")),
        P(("groups", "rows")),
        P(("groups", "rows"), "feat"),
        P("groups"),
        P(),
    )
    out_specs = (
        P(("groups", "feat"), "rows", None, None, None, None),
        P("groups", None, None, None),
    )
    return jax.shard_map(shards, mesh=mesh, in_specs=in_specs, out_specs=out_specs, check_vma=False)
```

```python
import functools

import jax
import jax.numpy as jnp
from jax import lax
from jax.experimental import pallas as pl
from jax.experimental.pallas import tpu as pltpu
from jax.sharding import PartitionSpec as P

BINS = 256
HALF = BINS // 2
NODES = 32
HIST = 512
HORIZON = 28
FIRST_DAY = HIST - HORIZON
REGIONS = 10
CHANNELS = 8
TAPS = 4
DILATE = (1, 7, 14, 28)
LEVELS = (0.005, 0.025, 0.165, 0.25, 0.5, 0.75, 0.835, 0.975, 0.995)

LANES = 128
DAYS = 32
REGION_ROW = HORIZON
NODE_ROW = HORIZON + 1
TOTAL_ROW = HORIZON
STORES = 16
PIECES = 3
SCALE = 256.0
BF16 = jnp.bfloat16
F32 = jnp.float32
F8 = jnp.float8_e4m3fn
ROW_BY_ROW = (((1,), (1,)), ((), ()))
VMEM_LIMIT = 24 * 2**20


def partner(position, step, count):
    if count & (count - 1) == 0:
        return position ^ step
    return (position + step) % count


def split_parts(values):
    parts = []
    rest = values
    for _ in range(PIECES):
        part = rest.astype(BF16)
        parts.append(part)
        rest = rest - part.astype(F32)
    return parts


def tap_matrix(taps_ref, parity):
    gap = lax.broadcasted_iota(jnp.int32, (DAYS, LANES), 1) - lax.broadcasted_iota(
        jnp.int32, (DAYS, LANES), 0
    )
    first = FIRST_DAY - (HIST - LANES)
    matrix = jnp.zeros((DAYS, LANES), F32)
    for channel in range(parity, CHANNELS, 2):
        for lag in range(TAPS):
            offset = first - 1 - lag * DILATE[(channel // 2) % 4]
            matrix = matrix + jnp.where(
                gap == offset, taps_ref[lag : lag + 1, channel : channel + 1], 0.0
            )
    if parity == 0:
        matrix = matrix - jnp.where(gap == first, 1.0, 0.0)
    day = lax.broadcasted_iota(jnp.int32, (DAYS, LANES), 0)
    return jnp.where(day < HORIZON, matrix, 0.0)


def prepare(rows, *refs):
    given, refs = refs[:5], refs[5:]
    sums_ref, own_ref, out_refs, refs = refs[0], refs[1], refs[2 : 2 + rows], refs[2 + rows :]
    taken, (held, sems) = refs[:5], refs[5:]
    counts_ref, region_ref, node_ref, bins_ref, taps_ref = taken
    copies = [
        pltpu.make_async_copy(source, target, sems.at[at])
        for at, (source, target) in enumerate(zip(given, taken))
    ]
    for at in (4, 3, 0, 1, 2):
        copies[at].start()
    series = counts_ref.shape[0]
    feats = bins_ref.shape[1] // rows
    pad = held.shape[1]
    me = lax.axis_index("rows")

    copies[4].wait()
    own_taps = jnp.concatenate(split_parts(tap_matrix(taps_ref, 0)), axis=0)
    store_taps = tap_matrix(taps_ref, 1)

    copies[3].wait()
    turned = bins_ref[...].astype(F32).T
    for row_block in range(rows):
        part = turned[row_block * feats : (row_block + 1) * feats]
        if pad > feats:
            part = jnp.concatenate([part, jnp.zeros((pad - feats, series), F32)], axis=0)
        held[row_block] = part.astype(BF16)
    for step in range(rows):
        bins = held[partner(me, step, rows)]
        for block in range(series // LANES):
            lanes = slice(block * LANES, (block + 1) * LANES)
            out_refs[step][block * pad : (block + 1) * pad] = bins[:, lanes]

    for at in (0, 1, 2):
        copies[at].wait()
    counts = counts_ref[...]
    recent = counts_ref[:, HIST - LANES :]
    store = lax.broadcasted_iota(jnp.int32, (STORES, series), 0)
    pick = jnp.where(store == region_ref[...], 1.0, 0.0).astype(BF16)
    totals = jnp.dot(pick, counts, preferred_element_type=F32)
    forecast = lax.dot_general(
        store_taps,
        totals[:, HIST - LANES :],
        ROW_BY_ROW,
        precision=lax.Precision.HIGHEST,
        preferred_element_type=F32,
    )
    over_days = lax.dot_general(
        jnp.ones((DAYS, HIST), F32),
        totals,
        ROW_BY_ROW,
        precision=lax.Precision.HIGHEST,
        preferred_element_type=F32,
    )
    row = lax.broadcasted_iota(jnp.int32, (DAYS, STORES), 0)
    forecast = jnp.where(row == TOTAL_ROW, over_days, forecast)
    sums_ref[...] = jnp.concatenate(
        split_parts(forecast) + [jnp.zeros((DAYS, LANES - PIECES * STORES), BF16)], axis=1
    )

    own = lax.dot_general(own_taps, recent, ROW_BY_ROW, preferred_element_type=F32)
    own = own[:DAYS] + own[DAYS : 2 * DAYS] + own[2 * DAYS :]
    ones = jnp.ones((8, HIST), BF16)
    level = lax.dot_general(ones, counts, ROW_BY_ROW, preferred_element_type=F32)[:1] / HIST
    own = own / level
    day = lax.broadcasted_iota(jnp.int32, (DAYS, series), 0)
    own = jnp.where(day == REGION_ROW, region_ref[...].astype(F32), own)
    own = jnp.where(day == NODE_ROW, node_ref[...].astype(F32), own)
    own_ref[...] = own


def columns(rows, quant_ref, *refs):
    sums_refs, own_ref, refs = refs[:rows], refs[rows], refs[rows + 1 :]
    bins_refs, out_refs = refs[:rows], refs[rows:]
    series = own_ref.shape[1]
    behind = bins_refs[0].shape[0]
    level = F32(0.0)
    for index, value in enumerate(LEVELS):
        level = jnp.where(quant_ref[0] == index, F32(value), level)
    sums = jnp.zeros((DAYS, STORES), F32)
    for ref in sums_refs:
        parts = ref[...].astype(F32)
        for piece in range(PIECES):
            sums = sums + parts[:, piece * STORES : (piece + 1) * STORES]
    shared = sums / (sums[TOTAL_ROW : TOTAL_ROW + 1] / HIST + 1.0)
    shared = jnp.concatenate(split_parts(shared), axis=1)

    own = own_ref[...]
    day = lax.broadcasted_iota(jnp.int32, (DAYS, series), 0)
    store = lax.broadcasted_iota(jnp.int32, (PIECES * STORES, series), 0) % STORES
    region = own[REGION_ROW : REGION_ROW + 1].astype(jnp.int32)
    pick = jnp.where(store == region, 1.0, 0.0).astype(BF16)
    regional = jnp.dot(shared, pick, preferred_element_type=F32)
    wave = jnp.where(day < HORIZON, jnp.tanh(own + regional), 0.0)
    mean = jnp.sum(wave, axis=0, keepdims=True) / HORIZON
    square = jnp.sum(wave * wave, axis=0, keepdims=True) / HORIZON
    gradient = 0.5 + 0.5 * mean - level
    hessian = 0.5 * (1.0 - square)
    rows_of = [
        value[:, block * LANES : (block + 1) * LANES]
        for value in (gradient, hessian, own[NODE_ROW : NODE_ROW + 1])
        for block in range(series // LANES)
    ]
    spare = jnp.zeros((out_refs[0].shape[0] - behind - len(rows_of), LANES), F32)
    tail = jnp.concatenate(rows_of + [spare], axis=0).astype(BF16)
    for bins_ref, out_ref in zip(bins_refs, out_refs):
        out_ref[:behind] = bins_ref[...]
        out_ref[behind:] = tail


def place(tail, cols_ref):
    blocks = cols_ref.shape[1] // LANES
    gradient, hessian, node = (
        jnp.concatenate(
            [tail[at * blocks + block : at * blocks + block + 1] for block in range(blocks)], axis=1
        )
        for at in range(3)
    )
    node_at = lax.broadcasted_iota(jnp.int32, (NODES, cols_ref.shape[1]), 0)
    here_node = node_at == node.astype(jnp.int32)
    for part, value in enumerate((gradient, hessian)):
        value = value * SCALE
        high = value.astype(F8).astype(F32)
        for offset, piece in ((0, high), (2, value - high)):
            at = (part + offset) * NODES
            cols_ref[at : at + NODES] = jnp.where(here_node, piece, 0.0).astype(F8)


def accumulate(sources, feats, first, last, *refs):
    block_refs, refs = refs[:sources], refs[sources:]
    if not first:
        before_ref, refs = refs[0], refs[1:]
    if last:
        hist_ref, best_ref, bins_held, cols_held, hist_held, sem = refs
    else:
        left_ref, bins_held, cols_held = refs
    series = bins_held.shape[3]
    pad = max(feats, 16)
    behind = series // LANES * pad
    for source, ref in enumerate(block_refs):
        bins = jnp.concatenate(
            [ref[block * pad : (block + 1) * pad] for block in range(series // LANES)], axis=1
        )
        bins = bins[:feats].astype(jnp.int32)
        bins_held[source, 0] = jnp.bitwise_and(bins, HALF - 1)
        bins_held[source, 1] = jnp.where(bins >= HALF, 1, 0)
        place(ref[behind:].astype(F32), cols_held.at[source])

    bin_at = lax.broadcasted_iota(jnp.int32, (32, series), 0)

    def spread(source, part, feature):
        row = bins_held[source, part, pl.ds(feature, 1)]
        return jnp.broadcast_to(row, (32, series)).astype(jnp.int8)

    def products(source, pair):
        every = cols_held[source]
        uptos, sets = [], [every]
        for feature in pair:
            within = spread(source, 0, feature)
            uptos += [
                jnp.where(
                    within <= (bin_at + at).astype(jnp.int8), jnp.ones((), F8), jnp.zeros((), F8)
                )
                for at in range(0, HALF, 32)
            ]
            upper = spread(source, 1, feature) == jnp.int8(1)
            sets += [
                jnp.where(upper, every[at : at + 32], jnp.zeros((), F8))
                for at in range(0, every.shape[0], 32)
            ]
        product = lax.dot_general(
            jnp.concatenate(sets, axis=0),
            jnp.concatenate(uptos, axis=0),
            ROW_BY_ROW,
            preferred_element_type=F32,
        )
        count = every.shape[0]
        found = []
        for at in range(len(pair)):
            mine = product[:, at * HALF : (at + 1) * HALF]
            both, upper = mine[:count], mine[(at + 1) * count : (at + 2) * count]
            both = both[: count // 2] + both[count // 2 :]
            upper = upper[: count // 2] + upper[count // 2 :]
            found.append(jnp.concatenate([both - upper, upper], axis=1))
        return found

    def two_features(feature):
        pair = (feature, feature + 1)
        found = products(0, pair)
        if sources > 1:
            found = lax.fori_loop(
                1,
                sources,
                lambda at, total: [a + b for a, b in zip(total, products(at, pair))],
                found,
            )
        if not first:
            found = [value + before_ref[at] for at, value in zip(pair, found)]
        return found

    group = min(feats, 32 if last else 16)

    if not last:

        def one_group(at, carry):
            for member in range(0, group, 2):
                feature = at * group + member
                left_ref[feature], left_ref[feature + 1] = two_features(feature)
            return carry

        lax.fori_loop(0, feats // group, one_group, 0)
        return

    feature_at = lax.broadcasted_iota(jnp.int32, (NODES, LANES), 1)
    last_bin = lax.broadcasted_iota(jnp.int32, (NODES, BINS), 1) == BINS - 1

    chunk = min(group, 8)

    def histogram(feature, halves):
        halves = halves * (1.0 / SCALE)
        parts = [halves[:, :HALF], halves[:, HALF:]]
        first_bin = lax.broadcasted_iota(jnp.int32, parts[0].shape, 1) == 0
        hist_held[feature] = jnp.concatenate(
            [part - jnp.where(first_bin, 0.0, pltpu.roll(part, 1, axis=1)) for part in parts],
            axis=1,
        )
        return jnp.concatenate([parts[0], parts[1] + parts[0][:, HALF - 1 :]], axis=1)

    def gains(feature, left, best):
        grad, hess = left[:NODES], left[NODES:]
        all_grad, all_hess = grad[:, BINS - 1 :], hess[:, BINS - 1 :]
        over_grad, over_hess = all_grad - grad, all_hess - hess
        gain = grad * grad / (hess + 1.0) + over_grad * over_grad / (over_hess + 1.0)
        gain = jnp.max(jnp.where(last_bin, -jnp.inf, gain), axis=1, keepdims=True)
        gain = gain - all_grad * all_grad / (all_hess + 1.0)
        return jnp.where(feature_at == feature, gain, best)

    def final_group(at, best):
        waiting = []
        for member in range(0, group, 2):
            feature = at * group + member
            for offset, halves in enumerate(two_features(feature)):
                waiting.append((feature + offset, histogram(feature + offset, halves)))
            if (member + 2) % chunk == 0:
                here = pl.ds(feature + 2 - chunk, chunk)
                pltpu.make_async_copy(hist_held.at[here], hist_ref.at[here], sem).start()
                for feature, left in waiting:
                    best = gains(feature, left, best)
                waiting = []
        return best

    best = lax.fori_loop(0, feats // group, final_group, jnp.zeros((NODES, LANES), F32))
    best = best.T
    width = LANES // NODES
    packed = jnp.concatenate(
        [best[at * (feats // width) : (at + 1) * (feats // width)] for at in range(width)], axis=1
    )
    for target in range(best_ref.shape[0]):
        best_ref[target] = packed
    pltpu.make_async_copy(hist_held, hist_ref, sem).wait()


def shards(daily_unit_counts, region_ids, node_ids, bin_ids, quant_index, filter_kernels):
    rows = lax.axis_size("rows")
    feat_count = lax.axis_size("feat")
    series = daily_unit_counts.shape[0]
    feats = bin_ids.shape[1] // rows
    pad = max(feats, 16)
    blocks = series // LANES
    vmem = pl.BlockSpec(memory_space=pltpu.VMEM)
    smem = pl.BlockSpec(memory_space=pltpu.SMEM)
    hbm = pl.BlockSpec(memory_space=pl.ANY)
    params = pltpu.CompilerParams(vmem_limit_bytes=VMEM_LIMIT)
    regions = region_ids.reshape(1, series)
    nodes = node_ids.reshape(1, series)

    def exchange(array, step):
        pairs = [(at, partner(at, step, rows)) for at in range(rows)]
        return lax.ppermute(array, "rows", pairs)

    sums, own, *bins = pl.pallas_call(
        functools.partial(prepare, rows),
        out_shape=[jax.ShapeDtypeStruct((DAYS, LANES), BF16)]
        + [jax.ShapeDtypeStruct((DAYS, series), F32)]
        + [jax.ShapeDtypeStruct((blocks * pad, LANES), BF16)] * rows,
        in_specs=[hbm] * 5,
        out_specs=[vmem] * (2 + rows),
        scratch_shapes=[
            pltpu.VMEM(daily_unit_counts.shape, BF16),
            pltpu.VMEM((1, series), jnp.int32),
            pltpu.VMEM((1, series), jnp.int32),
            pltpu.VMEM(bin_ids.shape, jnp.int32),
            pltpu.VMEM((TAPS, CHANNELS), F32),
            pltpu.VMEM((rows, pad, series), BF16),
            pltpu.SemaphoreType.DMA((5,)),
        ],
        compiler_params=params,
        name="prepare",
    )(
        *(
            pltpu.with_memory_space_constraint(array, pltpu.HBM)
            for array in (daily_unit_counts, regions, nodes, bin_ids, filter_kernels.T)
        )
    )
    sums = [sums] + [exchange(sums, step) for step in range(1, rows)]
    outgoing = pl.pallas_call(
        functools.partial(columns, rows),
        out_shape=[jax.ShapeDtypeStruct((blocks * pad + 4 * blocks, LANES), BF16)] * rows,
        in_specs=[smem] + [vmem] * (2 * rows + 1),
        out_specs=[vmem] * rows,
        compiler_params=params,
        name="columns",
    )(quant_index, *sums, own, *bins)
    arrived = [outgoing[0]] + [exchange(outgoing[step], step) for step in range(1, rows)]

    targets = rows * feat_count
    packed_rows = feats * NODES // LANES
    hist_shape = jax.ShapeDtypeStruct((feats, 2 * NODES, BINS), F32)
    steps = [arrived[at : at + 1] for at in range(min(rows, 4) - 1)]
    steps.append(arrived[len(steps) :])
    histogram = None
    for at, sources in enumerate(steps):
        first, last = at == 0, at == len(steps) - 1
        count = len(sources)
        held = [
            pltpu.VMEM((count, 2, feats, series), jnp.int32),
            pltpu.VMEM((count, 4 * NODES, series), F8),
        ]
        operands = sources + ([] if first else [histogram])
        if last:
            held += [pltpu.VMEM(hist_shape.shape, F32), pltpu.SemaphoreType.DMA]
            out_shape = [hist_shape, jax.ShapeDtypeStruct((targets, packed_rows, LANES), F32)]
            out_specs = [hbm, vmem]
        else:
            out_shape, out_specs = hist_shape, vmem
        histogram = pl.pallas_call(
            functools.partial(accumulate, count, feats, first, last),
            out_shape=out_shape,
            in_specs=[vmem] * len(operands),
            out_specs=out_specs,
            scratch_shapes=held,
            input_output_aliases={} if first or last else {len(operands) - 1: 0},
            compiler_params=params,
            name=f"accumulate_{at}",
        )(*operands)
    histogram, best = histogram

    gathered = lax.all_to_all(best, ("feat", "rows"), 0, 0, tiled=True)
    width = LANES // NODES
    feature_best = (
        gathered.reshape(feat_count, rows, packed_rows, width, NODES)
        .transpose(0, 1, 3, 2, 4)
        .reshape(feat_count, rows, feats, NODES)
    )
    return histogram.reshape(1, 1, feats, 2, NODES, BINS), feature_best


def solution(mesh):
    in_specs = (
        P(("groups", "rows"), None),
        P(("groups", "rows")),
        P(("groups", "rows")),
        P(("groups", "rows"), "feat"),
        P("groups"),
        P(),
    )
    out_specs = (
        P(("groups", "feat"), "rows", None, None, None, None),
        P("groups", None, None, None),
    )
    return jax.shard_map(shards, mesh=mesh, in_specs=in_specs, out_specs=out_specs, check_vma=False)
```

```python
import functools

import jax
import jax.numpy as jnp
from jax import lax
from jax.experimental import pallas as pl
from jax.experimental.pallas import tpu as pltpu
from jax.sharding import PartitionSpec as P

BINS = 256
HALF = BINS // 2
NODES = 32
HIST = 512
HORIZON = 28
FIRST_DAY = HIST - HORIZON
REGIONS = 10
CHANNELS = 8
TAPS = 4
DILATE = (1, 7, 14, 28)
LEVELS = (0.005, 0.025, 0.165, 0.25, 0.5, 0.75, 0.835, 0.975, 0.995)

LANES = 128
DAYS = 32
REGION_ROW = HORIZON
NODE_ROW = HORIZON + 1
TOTAL_ROW = HORIZON
STORES = 16
PIECES = 3
SCALE = 256.0
BF16 = jnp.bfloat16
F32 = jnp.float32
F8 = jnp.float8_e4m3fn
ROW_BY_ROW = (((1,), (1,)), ((), ()))
VMEM_LIMIT = 24 * 2**20


def partner(position, step, count):
    if count & (count - 1) == 0:
        return position ^ step
    return (position + step) % count


def split_parts(values):
    parts = []
    rest = values
    for _ in range(PIECES):
        part = rest.astype(BF16)
        parts.append(part)
        rest = rest - part.astype(F32)
    return parts


def tap_matrix(taps_ref, parity):
    gap = lax.broadcasted_iota(jnp.int32, (DAYS, LANES), 1) - lax.broadcasted_iota(
        jnp.int32, (DAYS, LANES), 0
    )
    first = FIRST_DAY - (HIST - LANES)
    matrix = jnp.zeros((DAYS, LANES), F32)
    for channel in range(parity, CHANNELS, 2):
        for lag in range(TAPS):
            offset = first - 1 - lag * DILATE[(channel // 2) % 4]
            matrix = matrix + jnp.where(
                gap == offset, taps_ref[lag : lag + 1, channel : channel + 1], 0.0
            )
    if parity == 0:
        matrix = matrix - jnp.where(gap == first, 1.0, 0.0)
    day = lax.broadcasted_iota(jnp.int32, (DAYS, LANES), 0)
    return jnp.where(day < HORIZON, matrix, 0.0)


def prepare(rows, *refs):
    given, refs = refs[:5], refs[5:]
    sums_ref, own_ref, out_refs, refs = refs[0], refs[1], refs[2 : 2 + rows], refs[2 + rows :]
    taken, (held, sems) = refs[:5], refs[5:]
    counts_ref, region_ref, node_ref, bins_ref, taps_ref = taken
    copies = [
        pltpu.make_async_copy(source, target, sems.at[at])
        for at, (source, target) in enumerate(zip(given, taken))
    ]
    for at in (4, 3, 0, 1, 2):
        copies[at].start()
    series = counts_ref.shape[0]
    feats = bins_ref.shape[1] // rows
    pad = held.shape[1]
    me = lax.axis_index("rows")

    copies[4].wait()
    own_taps = jnp.concatenate(split_parts(tap_matrix(taps_ref, 0)), axis=0)
    store_taps = tap_matrix(taps_ref, 1)

    copies[3].wait()
    turned = bins_ref[...].astype(F32).T
    for row_block in range(rows):
        part = turned[row_block * feats : (row_block + 1) * feats]
        if pad > feats:
            part = jnp.concatenate([part, jnp.zeros((pad - feats, series), F32)], axis=0)
        held[row_block] = part.astype(BF16)
    for step in range(rows):
        bins = held[partner(me, step, rows)]
        for block in range(series // LANES):
            lanes = slice(block * LANES, (block + 1) * LANES)
            out_refs[step][block * pad : (block + 1) * pad] = bins[:, lanes]

    for at in (0, 1, 2):
        copies[at].wait()
    counts = counts_ref[...]
    recent = counts_ref[:, HIST - LANES :]
    store = lax.broadcasted_iota(jnp.int32, (STORES, series), 0)
    pick = jnp.where(store == region_ref[...], 1.0, 0.0).astype(BF16)
    totals = jnp.dot(pick, counts, preferred_element_type=F32)
    forecast = lax.dot_general(
        store_taps,
        totals[:, HIST - LANES :],
        ROW_BY_ROW,
        precision=lax.Precision.HIGHEST,
        preferred_element_type=F32,
    )
    over_days = lax.dot_general(
        jnp.ones((DAYS, HIST), F32),
        totals,
        ROW_BY_ROW,
        precision=lax.Precision.HIGHEST,
        preferred_element_type=F32,
    )
    row = lax.broadcasted_iota(jnp.int32, (DAYS, STORES), 0)
    forecast = jnp.where(row == TOTAL_ROW, over_days, forecast)
    sums_ref[...] = jnp.concatenate(
        split_parts(forecast) + [jnp.zeros((DAYS, LANES - PIECES * STORES), BF16)], axis=1
    )

    own = lax.dot_general(own_taps, recent, ROW_BY_ROW, preferred_element_type=F32)
    own = own[:DAYS] + own[DAYS : 2 * DAYS] + own[2 * DAYS :]
    ones = jnp.ones((8, HIST), BF16)
    level = lax.dot_general(ones, counts, ROW_BY_ROW, preferred_element_type=F32)[:1] / HIST
    own = own / level
    day = lax.broadcasted_iota(jnp.int32, (DAYS, series), 0)
    own = jnp.where(day == REGION_ROW, region_ref[...].astype(F32), own)
    own = jnp.where(day == NODE_ROW, node_ref[...].astype(F32), own)
    own_ref[...] = own


def columns(rows, quant_ref, *refs):
    sums_refs, own_ref, refs = refs[:rows], refs[rows], refs[rows + 1 :]
    bins_refs, out_refs = refs[:rows], refs[rows:]
    series = own_ref.shape[1]
    behind = bins_refs[0].shape[0]
    level = F32(0.0)
    for index, value in enumerate(LEVELS):
        level = jnp.where(quant_ref[0] == index, F32(value), level)
    sums = jnp.zeros((DAYS, STORES), F32)
    for ref in sums_refs:
        parts = ref[...].astype(F32)
        for piece in range(PIECES):
            sums = sums + parts[:, piece * STORES : (piece + 1) * STORES]
    shared = sums / (sums[TOTAL_ROW : TOTAL_ROW + 1] / HIST + 1.0)
    shared = jnp.concatenate(split_parts(shared), axis=1)

    own = own_ref[...]
    day = lax.broadcasted_iota(jnp.int32, (DAYS, series), 0)
    store = lax.broadcasted_iota(jnp.int32, (PIECES * STORES, series), 0) % STORES
    region = own[REGION_ROW : REGION_ROW + 1].astype(jnp.int32)
    pick = jnp.where(store == region, 1.0, 0.0).astype(BF16)
    regional = jnp.dot(shared, pick, preferred_element_type=F32)
    wave = jnp.where(day < HORIZON, jnp.tanh(own + regional), 0.0)
    mean = jnp.sum(wave, axis=0, keepdims=True) / HORIZON
    square = jnp.sum(wave * wave, axis=0, keepdims=True) / HORIZON
    gradient = 0.5 + 0.5 * mean - level
    hessian = 0.5 * (1.0 - square)
    rows_of = [
        value[:, block * LANES : (block + 1) * LANES]
        for value in (gradient, hessian, own[NODE_ROW : NODE_ROW + 1])
        for block in range(series // LANES)
    ]
    spare = jnp.zeros((out_refs[0].shape[0] - behind - len(rows_of), LANES), F32)
    tail = jnp.concatenate(rows_of + [spare], axis=0).astype(BF16)
    for bins_ref, out_ref in zip(bins_refs, out_refs):
        out_ref[:behind] = bins_ref[...]
        out_ref[behind:] = tail


def place(tail, cols_ref):
    blocks = cols_ref.shape[1] // LANES
    gradient, hessian, node = (
        jnp.concatenate(
            [tail[at * blocks + block : at * blocks + block + 1] for block in range(blocks)], axis=1
        )
        for at in range(3)
    )
    node_at = lax.broadcasted_iota(jnp.int32, (NODES, cols_ref.shape[1]), 0)
    here_node = node_at == node.astype(jnp.int32)
    for part, value in enumerate((gradient, hessian)):
        value = value * SCALE
        high = value.astype(F8).astype(F32)
        for offset, piece in ((0, high), (2, value - high)):
            at = (part + offset) * NODES
            cols_ref[at : at + NODES] = jnp.where(here_node, piece, 0.0).astype(F8)


def accumulate(sources, feats, first, last, *refs):
    block_refs, refs = refs[:sources], refs[sources:]
    if not first:
        before_ref, refs = refs[0], refs[1:]
    if last:
        hist_ref, best_ref, bins_held, cols_held, hist_held, sem = refs
    else:
        left_ref, bins_held, cols_held = refs
    series = bins_held.shape[3]
    pad = max(feats, 16)
    behind = series // LANES * pad
    for source, ref in enumerate(block_refs):
        bins = jnp.concatenate(
            [ref[block * pad : (block + 1) * pad] for block in range(series // LANES)], axis=1
        )
        bins = bins[:feats].astype(jnp.int32)
        bins_held[source, 0] = jnp.bitwise_and(bins, HALF - 1)
        bins_held[source, 1] = jnp.where(bins >= HALF, 1, 0)
        place(ref[behind:].astype(F32), cols_held.at[source])

    bin_at = lax.broadcasted_iota(jnp.int32, (32, series), 0)

    def spread(source, part, feature):
        row = bins_held[source, part, pl.ds(feature, 1)]
        return jnp.broadcast_to(row, (32, series)).astype(jnp.int8)

    def products(source, pair):
        every = cols_held[source]
        uptos, sets = [], [every]
        for feature in pair:
            within = spread(source, 0, feature)
            uptos += [
                jnp.where(
                    within <= (bin_at + at).astype(jnp.int8), jnp.ones((), F8), jnp.zeros((), F8)
                )
                for at in range(0, HALF, 32)
            ]
            upper = spread(source, 1, feature) == jnp.int8(1)
            sets += [
                jnp.where(upper, every[at : at + 32], jnp.zeros((), F8))
                for at in range(0, every.shape[0], 32)
            ]
        product = lax.dot_general(
            jnp.concatenate(sets, axis=0),
            jnp.concatenate(uptos, axis=0),
            ROW_BY_ROW,
            preferred_element_type=F32,
        )
        count = every.shape[0]
        found = []
        for at in range(len(pair)):
            mine = product[:, at * HALF : (at + 1) * HALF]
            both, upper = mine[:count], mine[(at + 1) * count : (at + 2) * count]
            both = both[: count // 2] + both[count // 2 :]
            upper = upper[: count // 2] + upper[count // 2 :]
            found.append(jnp.concatenate([both - upper, upper], axis=1))
        return found

    def two_features(feature):
        pair = (feature, feature + 1)
        found = products(0, pair)
        if sources > 1:
            found = lax.fori_loop(
                1,
                sources,
                lambda at, total: [a + b for a, b in zip(total, products(at, pair))],
                found,
            )
        if not first:
            found = [value + before_ref[at] for at, value in zip(pair, found)]
        return found

    group = min(feats, 16)

    if not last:

        def one_group(at, carry):
            for member in range(0, group, 2):
                feature = at * group + member
                left_ref[feature], left_ref[feature + 1] = two_features(feature)
            return carry

        lax.fori_loop(0, feats // group, one_group, 0)
        return

    feature_at = lax.broadcasted_iota(jnp.int32, (NODES, LANES), 1)
    last_bin = lax.broadcasted_iota(jnp.int32, (NODES, BINS), 1) == BINS - 1

    chunk = min(group, 4)

    def histogram(feature, halves):
        halves = halves * (1.0 / SCALE)
        parts = [halves[:, :HALF], halves[:, HALF:]]
        first_bin = lax.broadcasted_iota(jnp.int32, parts[0].shape, 1) == 0
        hist_held[feature] = jnp.concatenate(
            [part - jnp.where(first_bin, 0.0, pltpu.roll(part, 1, axis=1)) for part in parts],
            axis=1,
        )
        return jnp.concatenate([parts[0], parts[1] + parts[0][:, HALF - 1 :]], axis=1)

    def gains(feature, left, best):
        grad, hess = left[:NODES], left[NODES:]
        all_grad, all_hess = grad[:, BINS - 1 :], hess[:, BINS - 1 :]
        over_grad, over_hess = all_grad - grad, all_hess - hess
        gain = grad * grad / (hess + 1.0) + over_grad * over_grad / (over_hess + 1.0)
        gain = jnp.max(jnp.where(last_bin, -jnp.inf, gain), axis=1, keepdims=True)
        gain = gain - all_grad * all_grad / (all_hess + 1.0)
        return jnp.where(feature_at == feature, gain, best)

    def final_group(at, best):
        waiting = []
        for member in range(0, group, 2):
            feature = at * group + member
            for offset, halves in enumerate(two_features(feature)):
                waiting.append((feature + offset, histogram(feature + offset, halves)))
            if (member + 2) % chunk == 0:
                here = pl.ds(feature + 2 - chunk, chunk)
                pltpu.make_async_copy(hist_held.at[here], hist_ref.at[here], sem).start()
                for feature, left in waiting:
                    best = gains(feature, left, best)
                waiting = []
        return best

    best = lax.fori_loop(0, feats // group, final_group, jnp.zeros((NODES, LANES), F32))
    best = best.T
    width = LANES // NODES
    packed = jnp.concatenate(
        [best[at * (feats // width) : (at + 1) * (feats // width)] for at in range(width)], axis=1
    )
    for target in range(best_ref.shape[0]):
        best_ref[target] = packed
    pltpu.make_async_copy(hist_held, hist_ref, sem).wait()


def shards(daily_unit_counts, region_ids, node_ids, bin_ids, quant_index, filter_kernels):
    rows = lax.axis_size("rows")
    feat_count = lax.axis_size("feat")
    series = daily_unit_counts.shape[0]
    feats = bin_ids.shape[1] // rows
    pad = max(feats, 16)
    blocks = series // LANES
    vmem = pl.BlockSpec(memory_space=pltpu.VMEM)
    smem = pl.BlockSpec(memory_space=pltpu.SMEM)
    hbm = pl.BlockSpec(memory_space=pl.ANY)
    params = pltpu.CompilerParams(vmem_limit_bytes=VMEM_LIMIT)
    regions = region_ids.reshape(1, series)
    nodes = node_ids.reshape(1, series)

    def exchange(array, step):
        pairs = [(at, partner(at, step, rows)) for at in range(rows)]
        return lax.ppermute(array, "rows", pairs)

    sums, own, *bins = pl.pallas_call(
        functools.partial(prepare, rows),
        out_shape=[jax.ShapeDtypeStruct((DAYS, LANES), BF16)]
        + [jax.ShapeDtypeStruct((DAYS, series), F32)]
        + [jax.ShapeDtypeStruct((blocks * pad, LANES), BF16)] * rows,
        in_specs=[hbm] * 5,
        out_specs=[vmem] * (2 + rows),
        scratch_shapes=[
            pltpu.VMEM(daily_unit_counts.shape, BF16),
            pltpu.VMEM((1, series), jnp.int32),
            pltpu.VMEM((1, series), jnp.int32),
            pltpu.VMEM(bin_ids.shape, jnp.int32),
            pltpu.VMEM((TAPS, CHANNELS), F32),
            pltpu.VMEM((rows, pad, series), BF16),
            pltpu.SemaphoreType.DMA((5,)),
        ],
        compiler_params=params,
        name="prepare",
    )(
        *(
            pltpu.with_memory_space_constraint(array, pltpu.HBM)
            for array in (daily_unit_counts, regions, nodes, bin_ids, filter_kernels.T)
        )
    )
    sums = [sums] + [exchange(sums, step) for step in range(1, rows)]
    outgoing = pl.pallas_call(
        functools.partial(columns, rows),
        out_shape=[jax.ShapeDtypeStruct((blocks * pad + 4 * blocks, LANES), BF16)] * rows,
        in_specs=[smem] + [vmem] * (2 * rows + 1),
        out_specs=[vmem] * rows,
        compiler_params=params,
        name="columns",
    )(quant_index, *sums, own, *bins)
    arrived = [outgoing[0]] + [exchange(outgoing[step], step) for step in range(1, rows)]

    targets = rows * feat_count
    packed_rows = feats * NODES // LANES
    hist_shape = jax.ShapeDtypeStruct((feats, 2 * NODES, BINS), F32)
    steps = [arrived[at : at + 1] for at in range(min(rows, 4) - 1)]
    steps.append(arrived[len(steps) :])
    histogram = None
    for at, sources in enumerate(steps):
        first, last = at == 0, at == len(steps) - 1
        count = len(sources)
        held = [
            pltpu.VMEM((count, 2, feats, series), jnp.int32),
            pltpu.VMEM((count, 4 * NODES, series), F8),
        ]
        operands = sources + ([] if first else [histogram])
        if last:
            held += [pltpu.VMEM(hist_shape.shape, F32), pltpu.SemaphoreType.DMA]
            out_shape = [hist_shape, jax.ShapeDtypeStruct((targets, packed_rows, LANES), F32)]
            out_specs = [hbm, vmem]
        else:
            out_shape, out_specs = hist_shape, vmem
        histogram = pl.pallas_call(
            functools.partial(accumulate, count, feats, first, last),
            out_shape=out_shape,
            in_specs=[vmem] * len(operands),
            out_specs=out_specs,
            scratch_shapes=held,
            input_output_aliases={} if first or last else {len(operands) - 1: 0},
            compiler_params=params,
            name=f"accumulate_{at}",
        )(*operands)
    histogram, best = histogram

    gathered = lax.all_to_all(best, ("feat", "rows"), 0, 0, tiled=True)
    width = LANES // NODES
    feature_best = (
        gathered.reshape(feat_count, rows, packed_rows, width, NODES)
        .transpose(0, 1, 3, 2, 4)
        .reshape(feat_count, rows, feats, NODES)
    )
    return histogram.reshape(1, 1, feats, 2, NODES, BINS), feature_best


def solution(mesh):
    in_specs = (
        P(("groups", "rows"), None),
        P(("groups", "rows")),
        P(("groups", "rows")),
        P(("groups", "rows"), "feat"),
        P("groups"),
        P(),
    )
    out_specs = (
        P(("groups", "feat"), "rows", None, None, None, None),
        P("groups", None, None, None),
    )
    return jax.shard_map(shards, mesh=mesh, in_specs=in_specs, out_specs=out_specs, check_vma=False)
```

```python
import functools

import jax
import jax.numpy as jnp
from jax import lax
from jax.experimental import pallas as pl
from jax.experimental.pallas import tpu as pltpu
from jax.sharding import PartitionSpec as P

BINS = 256
HALF = BINS // 2
NODES = 32
HIST = 512
HORIZON = 28
FIRST_DAY = HIST - HORIZON
REGIONS = 10
CHANNELS = 8
TAPS = 4
DILATE = (1, 7, 14, 28)
LEVELS = (0.005, 0.025, 0.165, 0.25, 0.5, 0.75, 0.835, 0.975, 0.995)

LANES = 128
DAYS = 32
REGION_ROW = HORIZON
NODE_ROW = HORIZON + 1
TOTAL_ROW = HORIZON
STORES = 16
PIECES = 3
SCALE = 256.0
BF16 = jnp.bfloat16
F32 = jnp.float32
F8 = jnp.float8_e4m3fn
ROW_BY_ROW = (((1,), (1,)), ((), ()))
VMEM_LIMIT = 24 * 2**20


def partner(position, step, count):
    if count & (count - 1) == 0:
        return position ^ step
    return (position + step) % count


def split_parts(values):
    parts = []
    rest = values
    for _ in range(PIECES):
        part = rest.astype(BF16)
        parts.append(part)
        rest = rest - part.astype(F32)
    return parts


def tap_matrix(taps_ref, parity):
    gap = lax.broadcasted_iota(jnp.int32, (DAYS, LANES), 1) - lax.broadcasted_iota(
        jnp.int32, (DAYS, LANES), 0
    )
    first = FIRST_DAY - (HIST - LANES)
    matrix = jnp.zeros((DAYS, LANES), F32)
    for channel in range(parity, CHANNELS, 2):
        for lag in range(TAPS):
            offset = first - 1 - lag * DILATE[(channel // 2) % 4]
            matrix = matrix + jnp.where(
                gap == offset, taps_ref[lag : lag + 1, channel : channel + 1], 0.0
            )
    if parity == 0:
        matrix = matrix - jnp.where(gap == first, 1.0, 0.0)
    day = lax.broadcasted_iota(jnp.int32, (DAYS, LANES), 0)
    return jnp.where(day < HORIZON, matrix, 0.0)


def prepare(rows, *refs):
    given, refs = refs[:5], refs[5:]
    sums_ref, own_ref, out_refs, refs = refs[0], refs[1], refs[2 : 2 + rows], refs[2 + rows :]
    taken, (held, sems) = refs[:5], refs[5:]
    counts_ref, region_ref, node_ref, bins_ref, taps_ref = taken
    copies = [
        pltpu.make_async_copy(source, target, sems.at[at])
        for at, (source, target) in enumerate(zip(given, taken))
    ]
    for at in (4, 3, 0, 1, 2):
        copies[at].start()
    series = counts_ref.shape[0]
    feats = bins_ref.shape[1] // rows
    pad = held.shape[1]
    me = lax.axis_index("rows")

    copies[4].wait()
    own_taps = jnp.concatenate(split_parts(tap_matrix(taps_ref, 0)), axis=0)
    store_taps = tap_matrix(taps_ref, 1)

    copies[3].wait()
    turned = bins_ref[...].astype(F32).T
    for row_block in range(rows):
        part = turned[row_block * feats : (row_block + 1) * feats]
        if pad > feats:
            part = jnp.concatenate([part, jnp.zeros((pad - feats, series), F32)], axis=0)
        held[row_block] = part.astype(BF16)
    for step in range(rows):
        bins = held[partner(me, step, rows)]
        for block in range(series // LANES):
            lanes = slice(block * LANES, (block + 1) * LANES)
            out_refs[step][block * pad : (block + 1) * pad] = bins[:, lanes]

    for at in (0, 1, 2):
        copies[at].wait()
    counts = counts_ref[...]
    recent = counts_ref[:, HIST - LANES :]
    store = lax.broadcasted_iota(jnp.int32, (STORES, series), 0)
    pick = jnp.where(store == region_ref[...], 1.0, 0.0).astype(BF16)
    totals = jnp.dot(pick, counts, preferred_element_type=F32)
    forecast = lax.dot_general(
        store_taps,
        totals[:, HIST - LANES :],
        ROW_BY_ROW,
        precision=lax.Precision.HIGHEST,
        preferred_element_type=F32,
    )
    over_days = lax.dot_general(
        jnp.ones((DAYS, HIST), F32),
        totals,
        ROW_BY_ROW,
        precision=lax.Precision.HIGHEST,
        preferred_element_type=F32,
    )
    row = lax.broadcasted_iota(jnp.int32, (DAYS, STORES), 0)
    forecast = jnp.where(row == TOTAL_ROW, over_days, forecast)
    sums_ref[...] = jnp.concatenate(
        split_parts(forecast) + [jnp.zeros((DAYS, LANES - PIECES * STORES), BF16)], axis=1
    )

    own = lax.dot_general(own_taps, recent, ROW_BY_ROW, preferred_element_type=F32)
    own = own[:DAYS] + own[DAYS : 2 * DAYS] + own[2 * DAYS :]
    ones = jnp.ones((8, HIST), BF16)
    level = lax.dot_general(ones, counts, ROW_BY_ROW, preferred_element_type=F32)[:1] / HIST
    own = own / level
    day = lax.broadcasted_iota(jnp.int32, (DAYS, series), 0)
    own = jnp.where(day == REGION_ROW, region_ref[...].astype(F32), own)
    own = jnp.where(day == NODE_ROW, node_ref[...].astype(F32), own)
    own_ref[...] = own


def columns(rows, quant_ref, *refs):
    sums_refs, own_ref, refs = refs[:rows], refs[rows], refs[rows + 1 :]
    bins_refs, out_refs = refs[:rows], refs[rows:]
    series = own_ref.shape[1]
    behind = bins_refs[0].shape[0]
    level = F32(0.0)
    for index, value in enumerate(LEVELS):
        level = jnp.where(quant_ref[0] == index, F32(value), level)
    sums = jnp.zeros((DAYS, STORES), F32)
    for ref in sums_refs:
        parts = ref[...].astype(F32)
        for piece in range(PIECES):
            sums = sums + parts[:, piece * STORES : (piece + 1) * STORES]
    shared = sums / (sums[TOTAL_ROW : TOTAL_ROW + 1] / HIST + 1.0)
    shared = jnp.concatenate(split_parts(shared), axis=1)

    own = own_ref[...]
    day = lax.broadcasted_iota(jnp.int32, (DAYS, series), 0)
    store = lax.broadcasted_iota(jnp.int32, (PIECES * STORES, series), 0) % STORES
    region = own[REGION_ROW : REGION_ROW + 1].astype(jnp.int32)
    pick = jnp.where(store == region, 1.0, 0.0).astype(BF16)
    regional = jnp.dot(shared, pick, preferred_element_type=F32)
    wave = jnp.where(day < HORIZON, jnp.tanh(own + regional), 0.0)
    mean = jnp.sum(wave, axis=0, keepdims=True) / HORIZON
    square = jnp.sum(wave * wave, axis=0, keepdims=True) / HORIZON
    gradient = 0.5 + 0.5 * mean - level
    hessian = 0.5 * (1.0 - square)
    rows_of = [
        value[:, block * LANES : (block + 1) * LANES]
        for value in (gradient, hessian, own[NODE_ROW : NODE_ROW + 1])
        for block in range(series // LANES)
    ]
    spare = jnp.zeros((out_refs[0].shape[0] - behind - len(rows_of), LANES), F32)
    tail = jnp.concatenate(rows_of + [spare], axis=0).astype(BF16)
    for bins_ref, out_ref in zip(bins_refs, out_refs):
        out_ref[:behind] = bins_ref[...]
        out_ref[behind:] = tail


def place(tail, cols_ref):
    blocks = cols_ref.shape[1] // LANES
    gradient, hessian, node = (
        jnp.concatenate(
            [tail[at * blocks + block : at * blocks + block + 1] for block in range(blocks)], axis=1
        )
        for at in range(3)
    )
    node_at = lax.broadcasted_iota(jnp.int32, (NODES, cols_ref.shape[1]), 0)
    here_node = node_at == node.astype(jnp.int32)
    for part, value in enumerate((gradient, hessian)):
        value = value * SCALE
        high = value.astype(F8).astype(F32)
        for offset, piece in ((0, high), (2, value - high)):
            at = (part + offset) * NODES
            cols_ref[at : at + NODES] = jnp.where(here_node, piece, 0.0).astype(F8)


def accumulate(sources, feats, first, last, *refs):
    block_refs, refs = refs[:sources], refs[sources:]
    if not first:
        before_ref, refs = refs[0], refs[1:]
    left_ref, refs = refs[0], refs[1:]
    if last:
        best_ref, refs = refs[0], refs[1:]
    bins_held, cols_held = refs
    series = bins_held.shape[3]
    pad = max(feats, 16)
    behind = series // LANES * pad
    for source, ref in enumerate(block_refs):
        bins = jnp.concatenate(
            [ref[block * pad : (block + 1) * pad] for block in range(series // LANES)], axis=1
        )
        bins = bins[:feats].astype(jnp.int32)
        bins_held[source, 0] = jnp.bitwise_and(bins, HALF - 1)
        bins_held[source, 1] = jnp.where(bins >= HALF, 1, 0)
        place(ref[behind:].astype(F32), cols_held.at[source])

    bin_at = lax.broadcasted_iota(jnp.int32, (32, series), 0)

    def spread(source, part, feature):
        row = bins_held[source, part, pl.ds(feature, 1)]
        return jnp.broadcast_to(row, (32, series)).astype(jnp.int8)

    def products(source, pair):
        every = cols_held[source]
        uptos, sets = [], [every]
        for feature in pair:
            within = spread(source, 0, feature)
            uptos += [
                jnp.where(
                    within <= (bin_at + at).astype(jnp.int8), jnp.ones((), F8), jnp.zeros((), F8)
                )
                for at in range(0, HALF, 32)
            ]
            upper = spread(source, 1, feature) == jnp.int8(1)
            sets += [
                jnp.where(upper, every[at : at + 32], jnp.zeros((), F8))
                for at in range(0, every.shape[0], 32)
            ]
        product = lax.dot_general(
            jnp.concatenate(sets, axis=0),
            jnp.concatenate(uptos, axis=0),
            ROW_BY_ROW,
            preferred_element_type=F32,
        )
        count = every.shape[0]
        found = []
        for at in range(len(pair)):
            mine = product[:, at * HALF : (at + 1) * HALF]
            both, upper = mine[:count], mine[(at + 1) * count : (at + 2) * count]
            both = both[: count // 2] + both[count // 2 :]
            upper = upper[: count // 2] + upper[count // 2 :]
            found.append(jnp.concatenate([both - upper, upper], axis=1))
        return found

    def two_features(feature):
        pair = (feature, feature + 1)
        found = products(0, pair)
        if sources > 1:
            found = lax.fori_loop(
                1,
                sources,
                lambda at, total: [a + b for a, b in zip(total, products(at, pair))],
                found,
            )
        if not first:
            found = [value + before_ref[at] for at, value in zip(pair, found)]
        return found

    group = min(feats, 32 if last else 16)

    if not last:

        def one_group(at, carry):
            for member in range(0, group, 2):
                feature = at * group + member
                left_ref[feature], left_ref[feature + 1] = two_features(feature)
            return carry

        lax.fori_loop(0, feats // group, one_group, 0)
        return

    feature_at = lax.broadcasted_iota(jnp.int32, (NODES, LANES), 1)
    last_bin = lax.broadcasted_iota(jnp.int32, (NODES, BINS), 1) == BINS - 1


    def over_all(halves):
        lower, upper = halves[:, :HALF], halves[:, HALF:]
        return jnp.concatenate([lower, upper + lower[:, HALF - 1 :]], axis=1) * (1.0 / SCALE)

    def gains(feature, left, best):
        grad, hess = left[:NODES], left[NODES:]
        all_grad, all_hess = grad[:, BINS - 1 :], hess[:, BINS - 1 :]
        over_grad, over_hess = all_grad - grad, all_hess - hess
        gain = grad * grad / (hess + 1.0) + over_grad * over_grad / (over_hess + 1.0)
        gain = jnp.max(jnp.where(last_bin, -jnp.inf, gain), axis=1, keepdims=True)
        gain = gain - all_grad * all_grad / (all_hess + 1.0)
        return jnp.where(feature_at == feature, gain, best)

    def final_group(at, best):
        for member in range(0, group, 2):
            feature = at * group + member
            for offset, halves in enumerate(two_features(feature)):
                left_ref[feature + offset] = halves
                best = gains(feature + offset, over_all(halves), best)
        return best

    best = lax.fori_loop(0, feats // group, final_group, jnp.zeros((NODES, LANES), F32))
    best = best.T
    width = LANES // NODES
    packed = jnp.concatenate(
        [best[at * (feats // width) : (at + 1) * (feats // width)] for at in range(width)], axis=1
    )
    for target in range(best_ref.shape[0]):
        best_ref[target] = packed


def results(left_ref, packed_ref, hist_ref, best_ref, hist_held, best_held, sems):
    feats = left_ref.shape[0]
    targets, packed_rows, _ = packed_ref.shape
    for target in range(targets):
        packed = packed_ref[target]
        for at in range(LANES // NODES):
            best_held[target, at * packed_rows : (at + 1) * packed_rows] = packed[
                :, at * NODES : (at + 1) * NODES
            ]
    best_copy = pltpu.make_async_copy(best_held, best_ref, sems.at[1])
    best_copy.start()
    first_bin = lax.broadcasted_iota(jnp.int32, (2 * NODES, HALF), 1) == 0
    group = min(feats, 4)

    def one_group(at, carry):
        for member in range(group):
            feature = at * group + member
            for half in range(2):
                lanes = slice(half * HALF, (half + 1) * HALF)
                left = left_ref[feature, :, lanes] * (1.0 / SCALE)
                before = jnp.where(first_bin, 0.0, pltpu.roll(left, 1, axis=1))
                hist_held[feature, :, lanes] = left - before
        here = pl.ds(at * group, group)
        pltpu.make_async_copy(hist_held.at[here], hist_ref.at[here], sems.at[0]).start()
        return carry

    lax.fori_loop(0, feats // group, one_group, 0)
    pltpu.make_async_copy(hist_held, hist_ref, sems.at[0]).wait()
    best_copy.wait()


def shards(daily_unit_counts, region_ids, node_ids, bin_ids, quant_index, filter_kernels):
    rows = lax.axis_size("rows")
    feat_count = lax.axis_size("feat")
    series = daily_unit_counts.shape[0]
    feats = bin_ids.shape[1] // rows
    pad = max(feats, 16)
    blocks = series // LANES
    vmem = pl.BlockSpec(memory_space=pltpu.VMEM)
    smem = pl.BlockSpec(memory_space=pltpu.SMEM)
    hbm = pl.BlockSpec(memory_space=pl.ANY)
    params = pltpu.CompilerParams(vmem_limit_bytes=VMEM_LIMIT)
    regions = region_ids.reshape(1, series)
    nodes = node_ids.reshape(1, series)

    def exchange(array, step):
        pairs = [(at, partner(at, step, rows)) for at in range(rows)]
        return lax.ppermute(array, "rows", pairs)

    sums, own, *bins = pl.pallas_call(
        functools.partial(prepare, rows),
        out_shape=[jax.ShapeDtypeStruct((DAYS, LANES), BF16)]
        + [jax.ShapeDtypeStruct((DAYS, series), F32)]
        + [jax.ShapeDtypeStruct((blocks * pad, LANES), BF16)] * rows,
        in_specs=[hbm] * 5,
        out_specs=[vmem] * (2 + rows),
        scratch_shapes=[
            pltpu.VMEM(daily_unit_counts.shape, BF16),
            pltpu.VMEM((1, series), jnp.int32),
            pltpu.VMEM((1, series), jnp.int32),
            pltpu.VMEM(bin_ids.shape, jnp.int32),
            pltpu.VMEM((TAPS, CHANNELS), F32),
            pltpu.VMEM((rows, pad, series), BF16),
            pltpu.SemaphoreType.DMA((5,)),
        ],
        compiler_params=params,
        name="prepare",
    )(
        *(
            pltpu.with_memory_space_constraint(array, pltpu.HBM)
            for array in (daily_unit_counts, regions, nodes, bin_ids, filter_kernels.T)
        )
    )
    sums = [sums] + [exchange(sums, step) for step in range(1, rows)]
    outgoing = pl.pallas_call(
        functools.partial(columns, rows),
        out_shape=[jax.ShapeDtypeStruct((blocks * pad + 4 * blocks, LANES), BF16)] * rows,
        in_specs=[smem] + [vmem] * (2 * rows + 1),
        out_specs=[vmem] * rows,
        compiler_params=params,
        name="columns",
    )(quant_index, *sums, own, *bins)
    arrived = [outgoing[0]] + [exchange(outgoing[step], step) for step in range(1, rows)]

    targets = rows * feat_count
    packed_rows = feats * NODES // LANES
    hist_shape = jax.ShapeDtypeStruct((feats, 2 * NODES, BINS), F32)
    steps = [arrived[at : at + 1] for at in range(min(rows, 4) - 1)]
    steps.append(arrived[len(steps) :])
    histogram = None
    for at, sources in enumerate(steps):
        first, last = at == 0, at == len(steps) - 1
        count = len(sources)
        held = [
            pltpu.VMEM((count, 2, feats, series), jnp.int32),
            pltpu.VMEM((count, 4 * NODES, series), F8),
        ]
        operands = sources + ([] if first else [histogram])
        if last:
            out_shape = [hist_shape, jax.ShapeDtypeStruct((targets, packed_rows, LANES), F32)]
            out_specs = [vmem, vmem]
        else:
            out_shape, out_specs = hist_shape, vmem
        histogram = pl.pallas_call(
            functools.partial(accumulate, count, feats, first, last),
            out_shape=out_shape,
            in_specs=[vmem] * len(operands),
            out_specs=out_specs,
            scratch_shapes=held,
            input_output_aliases={} if first else {len(operands) - 1: 0},
            compiler_params=params,
            name=f"accumulate_{at}",
        )(*operands)
    left, best = histogram

    gathered = lax.all_to_all(best, ("feat", "rows"), 0, 0, tiled=True)
    best_shape = jax.ShapeDtypeStruct((targets, feats, NODES), F32)
    histogram, feature_best = pl.pallas_call(
        results,
        out_shape=[hist_shape, best_shape],
        in_specs=[vmem] * 2,
        out_specs=[hbm] * 2,
        scratch_shapes=[
            pltpu.VMEM(hist_shape.shape, F32),
            pltpu.VMEM(best_shape.shape, F32),
            pltpu.SemaphoreType.DMA((2,)),
        ],
        compiler_params=params,
        name="results",
    )(left, gathered)
    return (
        histogram.reshape(1, 1, feats, 2, NODES, BINS),
        feature_best.reshape(feat_count, rows, feats, NODES),
    )


def solution(mesh):
    in_specs = (
        P(("groups", "rows"), None),
        P(("groups", "rows")),
        P(("groups", "rows")),
        P(("groups", "rows"), "feat"),
        P("groups"),
        P(),
    )
    out_specs = (
        P(("groups", "feat"), "rows", None, None, None, None),
        P("groups", None, None, None),
    )
    return jax.shard_map(shards, mesh=mesh, in_specs=in_specs, out_specs=out_specs, check_vma=False)
```

```python
import functools

import jax
import jax.numpy as jnp
from jax import lax
from jax.experimental import pallas as pl
from jax.experimental.pallas import tpu as pltpu
from jax.sharding import PartitionSpec as P

BINS = 256
HALF = BINS // 2
NODES = 32
HIST = 512
HORIZON = 28
FIRST_DAY = HIST - HORIZON
REGIONS = 10
CHANNELS = 8
TAPS = 4
DILATE = (1, 7, 14, 28)
LEVELS = (0.005, 0.025, 0.165, 0.25, 0.5, 0.75, 0.835, 0.975, 0.995)

LANES = 128
DAYS = 32
REGION_ROW = HORIZON
NODE_ROW = HORIZON + 1
TOTAL_ROW = HORIZON
STORES = 16
PIECES = 3
SCALE = 256.0
BF16 = jnp.bfloat16
F32 = jnp.float32
F8 = jnp.float8_e4m3fn
ROW_BY_ROW = (((1,), (1,)), ((), ()))
VMEM_LIMIT = 24 * 2**20


def partner(position, step, count):
    if count & (count - 1) == 0:
        return position ^ step
    return (position + step) % count


def split_parts(values):
    parts = []
    rest = values
    for _ in range(PIECES):
        part = rest.astype(BF16)
        parts.append(part)
        rest = rest - part.astype(F32)
    return parts


def tap_matrix(taps_ref, parity):
    gap = lax.broadcasted_iota(jnp.int32, (DAYS, LANES), 1) - lax.broadcasted_iota(
        jnp.int32, (DAYS, LANES), 0
    )
    first = FIRST_DAY - (HIST - LANES)
    matrix = jnp.zeros((DAYS, LANES), F32)
    for channel in range(parity, CHANNELS, 2):
        for lag in range(TAPS):
            offset = first - 1 - lag * DILATE[(channel // 2) % 4]
            matrix = matrix + jnp.where(
                gap == offset, taps_ref[lag : lag + 1, channel : channel + 1], 0.0
            )
    if parity == 0:
        matrix = matrix - jnp.where(gap == first, 1.0, 0.0)
    day = lax.broadcasted_iota(jnp.int32, (DAYS, LANES), 0)
    return jnp.where(day < HORIZON, matrix, 0.0)


def prepare(rows, *refs):
    given, refs = refs[:5], refs[5:]
    sums_ref, out_refs, refs = refs[0], refs[1 : 1 + rows], refs[1 + rows :]
    counts_ref, region_ref, node_ref, own_taps_ref, bins_ref, taps_ref, held, sems = refs
    taken = (counts_ref, region_ref, node_ref, bins_ref, taps_ref)
    copies = [
        pltpu.make_async_copy(source, target, sems.at[at])
        for at, (source, target) in enumerate(zip(given, taken))
    ]
    for at in (4, 3, 0, 1, 2):
        copies[at].start()
    series = counts_ref.shape[0]
    feats = bins_ref.shape[1] // rows
    pad = held.shape[1]
    me = lax.axis_index("rows")

    copies[4].wait()
    own_taps_ref[...] = jnp.concatenate(split_parts(tap_matrix(taps_ref, 0)), axis=0)
    store_taps = tap_matrix(taps_ref, 1)

    copies[3].wait()
    turned = bins_ref[...].astype(F32).T
    for row_block in range(rows):
        part = turned[row_block * feats : (row_block + 1) * feats]
        if pad > feats:
            part = jnp.concatenate([part, jnp.zeros((pad - feats, series), F32)], axis=0)
        held[row_block] = part.astype(BF16)
    for step in range(rows):
        bins = held[partner(me, step, rows)]
        for block in range(series // LANES):
            lanes = slice(block * LANES, (block + 1) * LANES)
            out_refs[step][block * pad : (block + 1) * pad] = bins[:, lanes]

    for at in (0, 1, 2):
        copies[at].wait()
    counts = counts_ref[...]
    store = lax.broadcasted_iota(jnp.int32, (STORES, series), 0)
    pick = jnp.where(store == region_ref[...], 1.0, 0.0).astype(BF16)
    totals = jnp.dot(pick, counts, preferred_element_type=F32)
    forecast = lax.dot_general(
        store_taps,
        totals[:, HIST - LANES :],
        ROW_BY_ROW,
        precision=lax.Precision.HIGHEST,
        preferred_element_type=F32,
    )
    over_days = lax.dot_general(
        jnp.ones((DAYS, HIST), F32),
        totals,
        ROW_BY_ROW,
        precision=lax.Precision.HIGHEST,
        preferred_element_type=F32,
    )
    row = lax.broadcasted_iota(jnp.int32, (DAYS, STORES), 0)
    forecast = jnp.where(row == TOTAL_ROW, over_days, forecast)
    sums_ref[...] = jnp.concatenate(
        split_parts(forecast) + [jnp.zeros((DAYS, LANES - PIECES * STORES), BF16)], axis=1
    )


def own_terms(counts_ref, region_ref, node_ref, taps_ref, own_ref):
    counts = counts_ref[...]
    series = counts.shape[0]
    own = lax.dot_general(
        taps_ref[...], counts[:, HIST - LANES :], ROW_BY_ROW, preferred_element_type=F32
    )
    own = own[:DAYS] + own[DAYS : 2 * DAYS] + own[2 * DAYS :]
    ones = jnp.ones((8, HIST), BF16)
    mean = lax.dot_general(ones, counts, ROW_BY_ROW, preferred_element_type=F32)[:1] / HIST
    own = own / mean
    day = lax.broadcasted_iota(jnp.int32, (DAYS, series), 0)
    own = jnp.where(day == REGION_ROW, region_ref[...].astype(F32), own)
    own_ref[...] = jnp.where(day == NODE_ROW, node_ref[...].astype(F32), own)


def columns(rows, quant_ref, *refs):
    sums_refs, own_ref, refs = refs[:rows], refs[rows], refs[rows + 1 :]
    bins_refs, out_refs = refs[:rows], refs[rows:]
    series = own_ref.shape[1]
    behind = bins_refs[0].shape[0]
    level = F32(0.0)
    for index, value in enumerate(LEVELS):
        level = jnp.where(quant_ref[0] == index, F32(value), level)
    sums = jnp.zeros((DAYS, STORES), F32)
    for ref in sums_refs:
        parts = ref[...].astype(F32)
        for piece in range(PIECES):
            sums = sums + parts[:, piece * STORES : (piece + 1) * STORES]
    shared = sums / (sums[TOTAL_ROW : TOTAL_ROW + 1] / HIST + 1.0)
    shared = jnp.concatenate(split_parts(shared), axis=1)

    own = own_ref[...]
    day = lax.broadcasted_iota(jnp.int32, (DAYS, series), 0)
    store = lax.broadcasted_iota(jnp.int32, (PIECES * STORES, series), 0) % STORES
    region = own[REGION_ROW : REGION_ROW + 1].astype(jnp.int32)
    pick = jnp.where(store == region, 1.0, 0.0).astype(BF16)
    regional = jnp.dot(shared, pick, preferred_element_type=F32)
    wave = jnp.where(day < HORIZON, jnp.tanh(own + regional), 0.0)
    mean = jnp.sum(wave, axis=0, keepdims=True) / HORIZON
    square = jnp.sum(wave * wave, axis=0, keepdims=True) / HORIZON
    gradient = 0.5 + 0.5 * mean - level
    hessian = 0.5 * (1.0 - square)
    rows_of = [
        value[:, block * LANES : (block + 1) * LANES]
        for value in (gradient, hessian, own[NODE_ROW : NODE_ROW + 1])
        for block in range(series // LANES)
    ]
    spare = jnp.zeros((out_refs[0].shape[0] - behind - len(rows_of), LANES), F32)
    tail = jnp.concatenate(rows_of + [spare], axis=0).astype(BF16)
    for bins_ref, out_ref in zip(bins_refs, out_refs):
        out_ref[:behind] = bins_ref[...]
        out_ref[behind:] = tail


def place(tail, cols_ref):
    blocks = cols_ref.shape[1] // LANES
    gradient, hessian, node = (
        jnp.concatenate(
            [tail[at * blocks + block : at * blocks + block + 1] for block in range(blocks)], axis=1
        )
        for at in range(3)
    )
    node_at = lax.broadcasted_iota(jnp.int32, (NODES, cols_ref.shape[1]), 0)
    here_node = node_at == node.astype(jnp.int32)
    for part, value in enumerate((gradient, hessian)):
        value = value * SCALE
        high = value.astype(F8).astype(F32)
        for offset, piece in ((0, high), (2, value - high)):
            at = (part + offset) * NODES
            cols_ref[at : at + NODES] = jnp.where(here_node, piece, 0.0).astype(F8)


def accumulate(sources, feats, first, last, *refs):
    block_refs, refs = refs[:sources], refs[sources:]
    if not first:
        before_ref, refs = refs[0], refs[1:]
    left_ref, refs = refs[0], refs[1:]
    if last:
        best_ref, refs = refs[0], refs[1:]
    bins_held, cols_held = refs
    series = bins_held.shape[3]
    pad = max(feats, 16)
    behind = series // LANES * pad
    for source, ref in enumerate(block_refs):
        bins = jnp.concatenate(
            [ref[block * pad : (block + 1) * pad] for block in range(series // LANES)], axis=1
        )
        bins = bins[:feats].astype(jnp.int32)
        bins_held[source, 0] = jnp.bitwise_and(bins, HALF - 1)
        bins_held[source, 1] = jnp.where(bins >= HALF, 1, 0)
        place(ref[behind:].astype(F32), cols_held.at[source])

    bin_at = lax.broadcasted_iota(jnp.int32, (32, series), 0)

    def spread(source, part, feature):
        row = bins_held[source, part, pl.ds(feature, 1)]
        return jnp.broadcast_to(row, (32, series)).astype(jnp.int8)

    def products(source, pair):
        every = cols_held[source]
        uptos, sets = [], [every]
        for feature in pair:
            within = spread(source, 0, feature)
            uptos += [
                jnp.where(
                    within <= (bin_at + at).astype(jnp.int8), jnp.ones((), F8), jnp.zeros((), F8)
                )
                for at in range(0, HALF, 32)
            ]
            upper = spread(source, 1, feature) == jnp.int8(1)
            sets += [
                jnp.where(upper, every[at : at + 32], jnp.zeros((), F8))
                for at in range(0, every.shape[0], 32)
            ]
        product = lax.dot_general(
            jnp.concatenate(sets, axis=0),
            jnp.concatenate(uptos, axis=0),
            ROW_BY_ROW,
            preferred_element_type=F32,
        )
        count = every.shape[0]
        found = []
        for at in range(len(pair)):
            mine = product[:, at * HALF : (at + 1) * HALF]
            both, upper = mine[:count], mine[(at + 1) * count : (at + 2) * count]
            both = both[: count // 2] + both[count // 2 :]
            upper = upper[: count // 2] + upper[count // 2 :]
            found.append(jnp.concatenate([both - upper, upper], axis=1))
        return found

    def two_features(feature):
        pair = (feature, feature + 1)
        found = products(0, pair)
        if sources > 1:
            found = lax.fori_loop(
                1,
                sources,
                lambda at, total: [a + b for a, b in zip(total, products(at, pair))],
                found,
            )
        if not first:
            found = [value + before_ref[at] for at, value in zip(pair, found)]
        return found

    group = min(feats, 32 if last else 16)

    if not last:

        def one_group(at, carry):
            for member in range(0, group, 2):
                feature = at * group + member
                left_ref[feature], left_ref[feature + 1] = two_features(feature)
            return carry

        lax.fori_loop(0, feats // group, one_group, 0)
        return

    feature_at = lax.broadcasted_iota(jnp.int32, (NODES, LANES), 1)
    last_bin = lax.broadcasted_iota(jnp.int32, (NODES, BINS), 1) == BINS - 1


    def over_all(halves):
        lower, upper = halves[:, :HALF], halves[:, HALF:]
        return jnp.concatenate([lower, upper + lower[:, HALF - 1 :]], axis=1) * (1.0 / SCALE)

    def gains(feature, left, best):
        grad, hess = left[:NODES], left[NODES:]
        all_grad, all_hess = grad[:, BINS - 1 :], hess[:, BINS - 1 :]
        over_grad, over_hess = all_grad - grad, all_hess - hess
        gain = grad * grad / (hess + 1.0) + over_grad * over_grad / (over_hess + 1.0)
        gain = jnp.max(jnp.where(last_bin, -jnp.inf, gain), axis=1, keepdims=True)
        gain = gain - all_grad * all_grad / (all_hess + 1.0)
        return jnp.where(feature_at == feature, gain, best)

    def final_group(at, best):
        for member in range(0, group, 2):
            feature = at * group + member
            for offset, halves in enumerate(two_features(feature)):
                left_ref[feature + offset] = halves
                best = gains(feature + offset, over_all(halves), best)
        return best

    best = lax.fori_loop(0, feats // group, final_group, jnp.zeros((NODES, LANES), F32))
    best = best.T
    width = LANES // NODES
    packed = jnp.concatenate(
        [best[at * (feats // width) : (at + 1) * (feats // width)] for at in range(width)], axis=1
    )
    for target in range(best_ref.shape[0]):
        best_ref[target] = packed


def results(left_ref, packed_ref, hist_ref, best_ref, hist_held, best_held, sems):
    feats = left_ref.shape[0]
    targets, packed_rows, _ = packed_ref.shape
    first_bin = lax.broadcasted_iota(jnp.int32, (2 * NODES, HALF), 1) == 0
    group = min(feats, 8)

    def one_group(at, carry):
        for member in range(group):
            feature = at * group + member
            for half in range(2):
                lanes = slice(half * HALF, (half + 1) * HALF)
                left = left_ref[feature, :, lanes] * (1.0 / SCALE)
                before = jnp.where(first_bin, 0.0, pltpu.roll(left, 1, axis=1))
                hist_held[feature, :, lanes] = left - before
        here = pl.ds(at * group, group)
        pltpu.make_async_copy(hist_held.at[here], hist_ref.at[here], sems.at[0]).start()
        return carry

    lax.fori_loop(0, feats // group, one_group, 0)
    for target in range(targets):
        packed = packed_ref[target]
        for at in range(LANES // NODES):
            best_held[target, at * packed_rows : (at + 1) * packed_rows] = packed[
                :, at * NODES : (at + 1) * NODES
            ]
    best_copy = pltpu.make_async_copy(best_held, best_ref, sems.at[1])
    best_copy.start()
    pltpu.make_async_copy(hist_held, hist_ref, sems.at[0]).wait()
    best_copy.wait()


def shards(daily_unit_counts, region_ids, node_ids, bin_ids, quant_index, filter_kernels):
    rows = lax.axis_size("rows")
    feat_count = lax.axis_size("feat")
    series = daily_unit_counts.shape[0]
    feats = bin_ids.shape[1] // rows
    pad = max(feats, 16)
    blocks = series // LANES
    vmem = pl.BlockSpec(memory_space=pltpu.VMEM)
    smem = pl.BlockSpec(memory_space=pltpu.SMEM)
    hbm = pl.BlockSpec(memory_space=pl.ANY)
    params = pltpu.CompilerParams(vmem_limit_bytes=VMEM_LIMIT)
    regions = region_ids.reshape(1, series)
    nodes = node_ids.reshape(1, series)

    def exchange(array, step):
        pairs = [(at, partner(at, step, rows)) for at in range(rows)]
        return lax.ppermute(array, "rows", pairs)

    sums, *bins = pl.pallas_call(
        functools.partial(prepare, rows),
        out_shape=[jax.ShapeDtypeStruct((DAYS, LANES), BF16)]
        + [jax.ShapeDtypeStruct((blocks * pad, LANES), BF16)] * rows
        + [
            jax.ShapeDtypeStruct(daily_unit_counts.shape, BF16),
            jax.ShapeDtypeStruct((1, series), jnp.int32),
            jax.ShapeDtypeStruct((1, series), jnp.int32),
            jax.ShapeDtypeStruct((PIECES * DAYS, LANES), BF16),
        ],
        in_specs=[hbm] * 5,
        out_specs=[vmem] * (5 + rows),
        scratch_shapes=[
            pltpu.VMEM(bin_ids.shape, jnp.int32),
            pltpu.VMEM((TAPS, CHANNELS), F32),
            pltpu.VMEM((rows, pad, series), BF16),
            pltpu.SemaphoreType.DMA((5,)),
        ],
        compiler_params=params,
        name="prepare",
    )(
        *(
            pltpu.with_memory_space_constraint(array, pltpu.HBM)
            for array in (daily_unit_counts, regions, nodes, bin_ids, filter_kernels.T)
        )
    )
    bins, passed = bins[:rows], bins[rows:]
    own = pl.pallas_call(
        own_terms,
        out_shape=jax.ShapeDtypeStruct((DAYS, series), F32),
        in_specs=[vmem] * 4,
        out_specs=vmem,
        compiler_params=params,
        name="own_terms",
    )(*passed)
    sums = [sums] + [exchange(sums, step) for step in range(1, rows)]
    outgoing = pl.pallas_call(
        functools.partial(columns, rows),
        out_shape=[jax.ShapeDtypeStruct((blocks * pad + 4 * blocks, LANES), BF16)] * rows,
        in_specs=[smem] + [vmem] * (2 * rows + 1),
        out_specs=[vmem] * rows,
        compiler_params=params,
        name="columns",
    )(quant_index, *sums, own, *bins)
    arrived = [outgoing[0]] + [exchange(outgoing[step], step) for step in range(1, rows)]

    targets = rows * feat_count
    packed_rows = feats * NODES // LANES
    hist_shape = jax.ShapeDtypeStruct((feats, 2 * NODES, BINS), F32)
    steps = [arrived[at : at + 1] for at in range(min(rows, 4) - 1)]
    steps.append(arrived[len(steps) :])
    histogram = None
    for at, sources in enumerate(steps):
        first, last = at == 0, at == len(steps) - 1
        count = len(sources)
        held = [
            pltpu.VMEM((count, 2, feats, series), jnp.int32),
            pltpu.VMEM((count, 4 * NODES, series), F8),
        ]
        operands = sources + ([] if first else [histogram])
        if last:
            out_shape = [hist_shape, jax.ShapeDtypeStruct((targets, packed_rows, LANES), F32)]
            out_specs = [vmem, vmem]
        else:
            out_shape, out_specs = hist_shape, vmem
        histogram = pl.pallas_call(
            functools.partial(accumulate, count, feats, first, last),
            out_shape=out_shape,
            in_specs=[vmem] * len(operands),
            out_specs=out_specs,
            scratch_shapes=held,
            input_output_aliases={} if first else {len(operands) - 1: 0},
            compiler_params=params,
            name=f"accumulate_{at}",
        )(*operands)
    left, best = histogram

    gathered = lax.all_to_all(best, ("feat", "rows"), 0, 0, tiled=True)
    best_shape = jax.ShapeDtypeStruct((targets, feats, NODES), F32)
    histogram, feature_best = pl.pallas_call(
        results,
        out_shape=[hist_shape, best_shape],
        in_specs=[vmem] * 2,
        out_specs=[hbm] * 2,
        scratch_shapes=[
            pltpu.VMEM(hist_shape.shape, F32),
            pltpu.VMEM(best_shape.shape, F32),
            pltpu.SemaphoreType.DMA((2,)),
        ],
        compiler_params=params,
        name="results",
    )(left, gathered)
    return (
        histogram.reshape(1, 1, feats, 2, NODES, BINS),
        feature_best.reshape(feat_count, rows, feats, NODES),
    )


def solution(mesh):
    in_specs = (
        P(("groups", "rows"), None),
        P(("groups", "rows")),
        P(("groups", "rows")),
        P(("groups", "rows"), "feat"),
        P("groups"),
        P(),
    )
    out_specs = (
        P(("groups", "feat"), "rows", None, None, None, None),
        P("groups", None, None, None),
    )
    return jax.shard_map(shards, mesh=mesh, in_specs=in_specs, out_specs=out_specs, check_vma=False)
```

```python
import functools

import jax
import jax.numpy as jnp
from jax import lax
from jax.experimental import pallas as pl
from jax.experimental.pallas import tpu as pltpu
from jax.sharding import PartitionSpec as P

BINS = 256
HALF = BINS // 2
NODES = 32
HIST = 512
HORIZON = 28
FIRST_DAY = HIST - HORIZON
REGIONS = 10
CHANNELS = 8
TAPS = 4
DILATE = (1, 7, 14, 28)
LEVELS = (0.005, 0.025, 0.165, 0.25, 0.5, 0.75, 0.835, 0.975, 0.995)

LANES = 128
DAYS = 32
REGION_ROW = HORIZON
NODE_ROW = HORIZON + 1
TOTAL_ROW = HORIZON
STORES = 16
PIECES = 3
SCALE = 256.0
BF16 = jnp.bfloat16
F32 = jnp.float32
F8 = jnp.float8_e4m3fn
ROW_BY_ROW = (((1,), (1,)), ((), ()))
VMEM_LIMIT = 24 * 2**20


def partner(position, step, count):
    if count & (count - 1) == 0:
        return position ^ step
    return (position + step) % count


def split_parts(values):
    parts = []
    rest = values
    for _ in range(PIECES):
        part = rest.astype(BF16)
        parts.append(part)
        rest = rest - part.astype(F32)
    return parts


def tap_matrix(taps_ref, parity):
    gap = lax.broadcasted_iota(jnp.int32, (DAYS, LANES), 1) - lax.broadcasted_iota(
        jnp.int32, (DAYS, LANES), 0
    )
    first = FIRST_DAY - (HIST - LANES)
    matrix = jnp.zeros((DAYS, LANES), F32)
    for channel in range(parity, CHANNELS, 2):
        for lag in range(TAPS):
            offset = first - 1 - lag * DILATE[(channel // 2) % 4]
            matrix = matrix + jnp.where(
                gap == offset, taps_ref[lag : lag + 1, channel : channel + 1], 0.0
            )
    if parity == 0:
        matrix = matrix - jnp.where(gap == first, 1.0, 0.0)
    day = lax.broadcasted_iota(jnp.int32, (DAYS, LANES), 0)
    return jnp.where(day < HORIZON, matrix, 0.0)


def prepare(*refs):
    given, sums_ref, refs = refs[:5], refs[5], refs[6:]
    counts_ref, region_ref, node_ref, bins_ref, own_taps_ref, taps_ref, sems = refs
    taken = (counts_ref, region_ref, node_ref, bins_ref, taps_ref)
    copies = [
        pltpu.make_async_copy(source, target, sems.at[at])
        for at, (source, target) in enumerate(zip(given, taken))
    ]
    for at in (4, 0, 1, 2, 3):
        copies[at].start()
    series = counts_ref.shape[0]
    copies[4].wait()
    own_taps_ref[...] = jnp.concatenate(split_parts(tap_matrix(taps_ref, 0)), axis=0)
    store_taps = tap_matrix(taps_ref, 1)

    for at in (0, 1, 2):
        copies[at].wait()
    counts = counts_ref[...]
    store = lax.broadcasted_iota(jnp.int32, (STORES, series), 0)
    pick = jnp.where(store == region_ref[...], 1.0, 0.0).astype(BF16)
    totals = jnp.dot(pick, counts, preferred_element_type=F32)
    forecast = lax.dot_general(
        store_taps,
        totals[:, HIST - LANES :],
        ROW_BY_ROW,
        precision=lax.Precision.HIGHEST,
        preferred_element_type=F32,
    )
    over_days = lax.dot_general(
        jnp.ones((DAYS, HIST), F32),
        totals,
        ROW_BY_ROW,
        precision=lax.Precision.HIGHEST,
        preferred_element_type=F32,
    )
    row = lax.broadcasted_iota(jnp.int32, (DAYS, STORES), 0)
    forecast = jnp.where(row == TOTAL_ROW, over_days, forecast)
    sums_ref[...] = jnp.concatenate(
        split_parts(forecast) + [jnp.zeros((DAYS, LANES - PIECES * STORES), BF16)], axis=1
    )
    copies[3].wait()


def local_terms(rows, counts_ref, region_ref, node_ref, bins_ref, taps_ref, own_ref, *refs):
    out_refs, held = refs[:rows], refs[rows]
    counts = counts_ref[...]
    series = counts.shape[0]
    feats = bins_ref.shape[1] // rows
    pad = held.shape[1]
    me = lax.axis_index("rows")
    own = lax.dot_general(
        taps_ref[...], counts[:, HIST - LANES :], ROW_BY_ROW, preferred_element_type=F32
    )
    own = own[:DAYS] + own[DAYS : 2 * DAYS] + own[2 * DAYS :]
    ones = jnp.ones((8, HIST), BF16)
    mean = lax.dot_general(ones, counts, ROW_BY_ROW, preferred_element_type=F32)[:1] / HIST
    own = own / mean
    day = lax.broadcasted_iota(jnp.int32, (DAYS, series), 0)
    own = jnp.where(day == REGION_ROW, region_ref[...].astype(F32), own)
    own_ref[...] = jnp.where(day == NODE_ROW, node_ref[...].astype(F32), own)

    turned = bins_ref[...].astype(F32).T
    for row_block in range(rows):
        part = turned[row_block * feats : (row_block + 1) * feats]
        if pad > feats:
            part = jnp.concatenate([part, jnp.zeros((pad - feats, series), F32)], axis=0)
        held[row_block] = part.astype(BF16)
    for step in range(rows):
        bins = held[partner(me, step, rows)]
        for block in range(series // LANES):
            lanes = slice(block * LANES, (block + 1) * LANES)
            out_refs[step][block * pad : (block + 1) * pad] = bins[:, lanes]


def columns(rows, quant_ref, *refs):
    sums_refs, own_ref, refs = refs[:rows], refs[rows], refs[rows + 1 :]
    bins_refs, out_refs = refs[:rows], refs[rows:]
    series = own_ref.shape[1]
    behind = bins_refs[0].shape[0]
    level = F32(0.0)
    for index, value in enumerate(LEVELS):
        level = jnp.where(quant_ref[0] == index, F32(value), level)
    sums = jnp.zeros((DAYS, STORES), F32)
    for ref in sums_refs:
        parts = ref[...].astype(F32)
        for piece in range(PIECES):
            sums = sums + parts[:, piece * STORES : (piece + 1) * STORES]
    shared = sums / (sums[TOTAL_ROW : TOTAL_ROW + 1] / HIST + 1.0)
    shared = jnp.concatenate(split_parts(shared), axis=1)

    own = own_ref[...]
    day = lax.broadcasted_iota(jnp.int32, (DAYS, series), 0)
    store = lax.broadcasted_iota(jnp.int32, (PIECES * STORES, series), 0) % STORES
    region = own[REGION_ROW : REGION_ROW + 1].astype(jnp.int32)
    pick = jnp.where(store == region, 1.0, 0.0).astype(BF16)
    regional = jnp.dot(shared, pick, preferred_element_type=F32)
    wave = jnp.where(day < HORIZON, jnp.tanh(own + regional), 0.0)
    mean = jnp.sum(wave, axis=0, keepdims=True) / HORIZON
    square = jnp.sum(wave * wave, axis=0, keepdims=True) / HORIZON
    gradient = 0.5 + 0.5 * mean - level
    hessian = 0.5 * (1.0 - square)
    rows_of = [
        value[:, block * LANES : (block + 1) * LANES]
        for value in (gradient, hessian, own[NODE_ROW : NODE_ROW + 1])
        for block in range(series // LANES)
    ]
    spare = jnp.zeros((out_refs[0].shape[0] - behind - len(rows_of), LANES), F32)
    tail = jnp.concatenate(rows_of + [spare], axis=0).astype(BF16)
    for bins_ref, out_ref in zip(bins_refs, out_refs):
        out_ref[:behind] = bins_ref[...]
        out_ref[behind:] = tail


def place(tail, cols_ref):
    blocks = cols_ref.shape[1] // LANES
    gradient, hessian, node = (
        jnp.concatenate(
            [tail[at * blocks + block : at * blocks + block + 1] for block in range(blocks)], axis=1
        )
        for at in range(3)
    )
    node_at = lax.broadcasted_iota(jnp.int32, (NODES, cols_ref.shape[1]), 0)
    here_node = node_at == node.astype(jnp.int32)
    for part, value in enumerate((gradient, hessian)):
        value = value * SCALE
        high = value.astype(F8).astype(F32)
        for offset, piece in ((0, high), (2, value - high)):
            at = (part + offset) * NODES
            cols_ref[at : at + NODES] = jnp.where(here_node, piece, 0.0).astype(F8)


def accumulate(sources, feats, first, last, *refs):
    block_refs, refs = refs[:sources], refs[sources:]
    if not first:
        before_ref, refs = refs[0], refs[1:]
    left_ref, refs = refs[0], refs[1:]
    if last:
        best_ref, refs = refs[0], refs[1:]
    bins_held, cols_held = refs
    series = bins_held.shape[3]
    pad = max(feats, 16)
    behind = series // LANES * pad
    for source, ref in enumerate(block_refs):
        bins = jnp.concatenate(
            [ref[block * pad : (block + 1) * pad] for block in range(series // LANES)], axis=1
        )
        bins = bins[:feats].astype(jnp.int32)
        bins_held[source, 0] = jnp.bitwise_and(bins, HALF - 1)
        bins_held[source, 1] = jnp.where(bins >= HALF, 1, 0)
        place(ref[behind:].astype(F32), cols_held.at[source])

    bin_at = lax.broadcasted_iota(jnp.int32, (32, series), 0)

    def spread(source, part, feature):
        row = bins_held[source, part, pl.ds(feature, 1)]
        return jnp.broadcast_to(row, (32, series)).astype(jnp.int8)

    def products(source, pair):
        every = cols_held[source]
        uptos, sets = [], [every]
        for feature in pair:
            within = spread(source, 0, feature)
            uptos += [
                jnp.where(
                    within <= (bin_at + at).astype(jnp.int8), jnp.ones((), F8), jnp.zeros((), F8)
                )
                for at in range(0, HALF, 32)
            ]
            upper = spread(source, 1, feature) == jnp.int8(1)
            sets += [
                jnp.where(upper, every[at : at + 32], jnp.zeros((), F8))
                for at in range(0, every.shape[0], 32)
            ]
        product = lax.dot_general(
            jnp.concatenate(sets, axis=0),
            jnp.concatenate(uptos, axis=0),
            ROW_BY_ROW,
            preferred_element_type=F32,
        )
        count = every.shape[0]
        found = []
        for at in range(len(pair)):
            mine = product[:, at * HALF : (at + 1) * HALF]
            both, upper = mine[:count], mine[(at + 1) * count : (at + 2) * count]
            both = both[: count // 2] + both[count // 2 :]
            upper = upper[: count // 2] + upper[count // 2 :]
            found.append(jnp.concatenate([both - upper, upper], axis=1))
        return found

    def two_features(feature):
        pair = (feature, feature + 1)
        found = products(0, pair)
        if sources > 1:
            found = lax.fori_loop(
                1,
                sources,
                lambda at, total: [a + b for a, b in zip(total, products(at, pair))],
                found,
            )
        if not first:
            found = [value + before_ref[at] for at, value in zip(pair, found)]
        return found

    group = min(feats, 32 if last else 16)

    if not last:

        def one_group(at, carry):
            for member in range(0, group, 2):
                feature = at * group + member
                left_ref[feature], left_ref[feature + 1] = two_features(feature)
            return carry

        lax.fori_loop(0, feats // group, one_group, 0)
        return

    feature_at = lax.broadcasted_iota(jnp.int32, (NODES, LANES), 1)
    last_bin = lax.broadcasted_iota(jnp.int32, (NODES, BINS), 1) == BINS - 1


    def over_all(halves):
        lower, upper = halves[:, :HALF], halves[:, HALF:]
        return jnp.concatenate([lower, upper + lower[:, HALF - 1 :]], axis=1) * (1.0 / SCALE)

    def gains(feature, left, best):
        grad, hess = left[:NODES], left[NODES:]
        all_grad, all_hess = grad[:, BINS - 1 :], hess[:, BINS - 1 :]
        over_grad, over_hess = all_grad - grad, all_hess - hess
        gain = grad * grad / (hess + 1.0) + over_grad * over_grad / (over_hess + 1.0)
        gain = jnp.max(jnp.where(last_bin, -jnp.inf, gain), axis=1, keepdims=True)
        gain = gain - all_grad * all_grad / (all_hess + 1.0)
        return jnp.where(feature_at == feature, gain, best)

    def final_group(at, best):
        for member in range(0, group, 2):
            feature = at * group + member
            for offset, halves in enumerate(two_features(feature)):
                left_ref[feature + offset] = halves
                best = gains(feature + offset, over_all(halves), best)
        return best

    best = lax.fori_loop(0, feats // group, final_group, jnp.zeros((NODES, LANES), F32))
    best = best.T
    width = LANES // NODES
    packed = jnp.concatenate(
        [best[at * (feats // width) : (at + 1) * (feats // width)] for at in range(width)], axis=1
    )
    for target in range(best_ref.shape[0]):
        best_ref[target] = packed


def results(left_ref, packed_ref, hist_ref, best_ref, hist_held, best_held, sems):
    feats = left_ref.shape[0]
    targets, packed_rows, _ = packed_ref.shape
    first_bin = lax.broadcasted_iota(jnp.int32, (2 * NODES, HALF), 1) == 0
    group = min(feats, 4)

    def one_group(at, carry):
        for member in range(group):
            feature = at * group + member
            for half in range(2):
                lanes = slice(half * HALF, (half + 1) * HALF)
                left = left_ref[feature, :, lanes] * (1.0 / SCALE)
                before = jnp.where(first_bin, 0.0, pltpu.roll(left, 1, axis=1))
                hist_held[feature, :, lanes] = left - before
        here = pl.ds(at * group, group)
        pltpu.make_async_copy(hist_held.at[here], hist_ref.at[here], sems.at[0]).start()
        return carry

    for step in range(feats // group):
        one_group(step, 0)
    for target in range(targets):
        packed = packed_ref[target]
        for at in range(LANES // NODES):
            best_held[target, at * packed_rows : (at + 1) * packed_rows] = packed[
                :, at * NODES : (at + 1) * NODES
            ]
    best_copy = pltpu.make_async_copy(best_held, best_ref, sems.at[1])
    best_copy.start()
    pltpu.make_async_copy(hist_held, hist_ref, sems.at[0]).wait()
    best_copy.wait()


def shards(daily_unit_counts, region_ids, node_ids, bin_ids, quant_index, filter_kernels):
    rows = lax.axis_size("rows")
    feat_count = lax.axis_size("feat")
    series = daily_unit_counts.shape[0]
    feats = bin_ids.shape[1] // rows
    pad = max(feats, 16)
    blocks = series // LANES
    vmem = pl.BlockSpec(memory_space=pltpu.VMEM)
    smem = pl.BlockSpec(memory_space=pltpu.SMEM)
    hbm = pl.BlockSpec(memory_space=pl.ANY)
    params = pltpu.CompilerParams(vmem_limit_bytes=VMEM_LIMIT)
    regions = region_ids.reshape(1, series)
    nodes = node_ids.reshape(1, series)

    def exchange(array, step):
        pairs = [(at, partner(at, step, rows)) for at in range(rows)]
        return lax.ppermute(array, "rows", pairs)

    sums, *passed = pl.pallas_call(
        prepare,
        out_shape=[
            jax.ShapeDtypeStruct((DAYS, LANES), BF16),
            jax.ShapeDtypeStruct(daily_unit_counts.shape, BF16),
            jax.ShapeDtypeStruct((1, series), jnp.int32),
            jax.ShapeDtypeStruct((1, series), jnp.int32),
            jax.ShapeDtypeStruct(bin_ids.shape, jnp.int32),
            jax.ShapeDtypeStruct((PIECES * DAYS, LANES), BF16),
        ],
        in_specs=[hbm] * 5,
        out_specs=[vmem] * 6,
        scratch_shapes=[pltpu.VMEM((TAPS, CHANNELS), F32), pltpu.SemaphoreType.DMA((5,))],
        compiler_params=params,
        name="prepare",
    )(
        *(
            pltpu.with_memory_space_constraint(array, pltpu.HBM)
            for array in (daily_unit_counts, regions, nodes, bin_ids, filter_kernels.T)
        )
    )
    own, *bins = pl.pallas_call(
        functools.partial(local_terms, rows),
        out_shape=[jax.ShapeDtypeStruct((DAYS, series), F32)]
        + [jax.ShapeDtypeStruct((blocks * pad, LANES), BF16)] * rows,
        in_specs=[vmem] * 5,
        out_specs=[vmem] * (1 + rows),
        scratch_shapes=[pltpu.VMEM((rows, pad, series), BF16)],
        compiler_params=params,
        name="local_terms",
    )(*passed)
    sums = [sums] + [exchange(sums, step) for step in range(1, rows)]
    outgoing = pl.pallas_call(
        functools.partial(columns, rows),
        out_shape=[jax.ShapeDtypeStruct((blocks * pad + 4 * blocks, LANES), BF16)] * rows,
        in_specs=[smem] + [vmem] * (2 * rows + 1),
        out_specs=[vmem] * rows,
        compiler_params=params,
        name="columns",
    )(quant_index, *sums, own, *bins)
    arrived = [outgoing[0]] + [exchange(outgoing[step], step) for step in range(1, rows)]

    targets = rows * feat_count
    packed_rows = feats * NODES // LANES
    hist_shape = jax.ShapeDtypeStruct((feats, 2 * NODES, BINS), F32)
    steps = [arrived[at : at + 1] for at in range(min(rows, 4) - 1)]
    steps.append(arrived[len(steps) :])
    histogram = None
    for at, sources in enumerate(steps):
        first, last = at == 0, at == len(steps) - 1
        count = len(sources)
        held = [
            pltpu.VMEM((count, 2, feats, series), jnp.int32),
            pltpu.VMEM((count, 4 * NODES, series), F8),
        ]
        operands = sources + ([] if first else [histogram])
        if last:
            out_shape = [hist_shape, jax.ShapeDtypeStruct((targets, packed_rows, LANES), F32)]
            out_specs = [vmem, vmem]
        else:
            out_shape, out_specs = hist_shape, vmem
        histogram = pl.pallas_call(
            functools.partial(accumulate, count, feats, first, last),
            out_shape=out_shape,
            in_specs=[vmem] * len(operands),
            out_specs=out_specs,
            scratch_shapes=held,
            input_output_aliases={} if first else {len(operands) - 1: 0},
            compiler_params=params,
            name=f"accumulate_{at}",
        )(*operands)
    left, best = histogram

    gathered = lax.all_to_all(best, ("feat", "rows"), 0, 0, tiled=True)
    best_shape = jax.ShapeDtypeStruct((targets, feats, NODES), F32)
    histogram, feature_best = pl.pallas_call(
        results,
        out_shape=[hist_shape, best_shape],
        in_specs=[vmem] * 2,
        out_specs=[hbm] * 2,
        scratch_shapes=[
            pltpu.VMEM(hist_shape.shape, F32),
            pltpu.VMEM(best_shape.shape, F32),
            pltpu.SemaphoreType.DMA((2,)),
        ],
        compiler_params=params,
        name="results",
    )(left, gathered)
    return (
        histogram.reshape(1, 1, feats, 2, NODES, BINS),
        feature_best.reshape(feat_count, rows, feats, NODES),
    )


def solution(mesh):
    in_specs = (
        P(("groups", "rows"), None),
        P(("groups", "rows")),
        P(("groups", "rows")),
        P(("groups", "rows"), "feat"),
        P("groups"),
        P(),
    )
    out_specs = (
        P(("groups", "feat"), "rows", None, None, None, None),
        P("groups", None, None, None),
    )
    return jax.shard_map(shards, mesh=mesh, in_specs=in_specs, out_specs=out_specs, check_vma=False)
```

```python
import functools

import jax
import jax.numpy as jnp
from jax import lax
from jax.experimental import pallas as pl
from jax.experimental.pallas import tpu as pltpu
from jax.sharding import PartitionSpec as P

BINS = 256
HALF = BINS // 2
NODES = 32
HIST = 512
HORIZON = 28
FIRST_DAY = HIST - HORIZON
REGIONS = 10
CHANNELS = 8
TAPS = 4
DILATE = (1, 7, 14, 28)
LEVELS = (0.005, 0.025, 0.165, 0.25, 0.5, 0.75, 0.835, 0.975, 0.995)

LANES = 128
DAYS = 32
REGION_ROW = HORIZON
NODE_ROW = HORIZON + 1
TOTAL_ROW = HORIZON
STORES = 16
PIECES = 3
SCALE = 256.0
BF16 = jnp.bfloat16
F32 = jnp.float32
F8 = jnp.float8_e4m3fn
ROW_BY_ROW = (((1,), (1,)), ((), ()))
VMEM_LIMIT = 24 * 2**20


def partner(position, step, count):
    if count & (count - 1) == 0:
        return position ^ step
    return (position + step) % count


def split_parts(values):
    parts = []
    rest = values
    for _ in range(PIECES):
        part = rest.astype(BF16)
        parts.append(part)
        rest = rest - part.astype(F32)
    return parts


def tap_matrix(taps_ref, parity):
    gap = lax.broadcasted_iota(jnp.int32, (DAYS, LANES), 1) - lax.broadcasted_iota(
        jnp.int32, (DAYS, LANES), 0
    )
    first = FIRST_DAY - (HIST - LANES)
    matrix = jnp.zeros((DAYS, LANES), F32)
    for channel in range(parity, CHANNELS, 2):
        for lag in range(TAPS):
            offset = first - 1 - lag * DILATE[(channel // 2) % 4]
            matrix = matrix + jnp.where(
                gap == offset, taps_ref[lag : lag + 1, channel : channel + 1], 0.0
            )
    if parity == 0:
        matrix = matrix - jnp.where(gap == first, 1.0, 0.0)
    day = lax.broadcasted_iota(jnp.int32, (DAYS, LANES), 0)
    return jnp.where(day < HORIZON, matrix, 0.0)


def prepare(*refs):
    given, sums_ref, refs = refs[:5], refs[5], refs[6:]
    counts_ref, region_ref, node_ref, bins_ref, own_taps_ref, taps_ref, sems = refs
    taken = (counts_ref, region_ref, node_ref, bins_ref, taps_ref)
    copies = [
        pltpu.make_async_copy(source, target, sems.at[at])
        for at, (source, target) in enumerate(zip(given, taken))
    ]
    for at in (4, 0, 1, 2, 3):
        copies[at].start()
    series = counts_ref.shape[0]
    copies[4].wait()
    own_taps_ref[...] = jnp.concatenate(split_parts(tap_matrix(taps_ref, 0)), axis=0)
    store_taps = tap_matrix(taps_ref, 1)

    for at in (0, 1, 2):
        copies[at].wait()
    counts = counts_ref[...]
    store = lax.broadcasted_iota(jnp.int32, (STORES, series), 0)
    pick = jnp.where(store == region_ref[...], 1.0, 0.0).astype(BF16)
    totals = jnp.dot(pick, counts, preferred_element_type=F32)
    forecast = lax.dot_general(
        store_taps,
        totals[:, HIST - LANES :],
        ROW_BY_ROW,
        precision=lax.Precision.HIGHEST,
        preferred_element_type=F32,
    )
    over_days = lax.dot_general(
        jnp.ones((DAYS, HIST), F32),
        totals,
        ROW_BY_ROW,
        precision=lax.Precision.HIGHEST,
        preferred_element_type=F32,
    )
    row = lax.broadcasted_iota(jnp.int32, (DAYS, STORES), 0)
    forecast = jnp.where(row == TOTAL_ROW, over_days, forecast)
    sums_ref[...] = jnp.concatenate(
        split_parts(forecast) + [jnp.zeros((DAYS, LANES - PIECES * STORES), BF16)], axis=1
    )
    copies[3].wait()


def local_terms(rows, counts_ref, region_ref, node_ref, bins_ref, taps_ref, own_ref, *refs):
    out_refs, held = refs[:rows], refs[rows]
    counts = counts_ref[...]
    series = counts.shape[0]
    feats = bins_ref.shape[1] // rows
    pad = held.shape[1]
    me = lax.axis_index("rows")
    own = lax.dot_general(
        taps_ref[...], counts[:, HIST - LANES :], ROW_BY_ROW, preferred_element_type=F32
    )
    own = own[:DAYS] + own[DAYS : 2 * DAYS] + own[2 * DAYS :]
    ones = jnp.ones((8, HIST), BF16)
    mean = lax.dot_general(ones, counts, ROW_BY_ROW, preferred_element_type=F32)[:1] / HIST
    own = own / mean
    day = lax.broadcasted_iota(jnp.int32, (DAYS, series), 0)
    own = jnp.where(day == REGION_ROW, region_ref[...].astype(F32), own)
    own_ref[...] = jnp.where(day == NODE_ROW, node_ref[...].astype(F32), own)

    turned = bins_ref[...].astype(F32).T
    for row_block in range(rows):
        part = turned[row_block * feats : (row_block + 1) * feats]
        if pad > feats:
            part = jnp.concatenate([part, jnp.zeros((pad - feats, series), F32)], axis=0)
        held[row_block] = part.astype(BF16)
    for step in range(rows):
        bins = held[partner(me, step, rows)]
        for block in range(series // LANES):
            lanes = slice(block * LANES, (block + 1) * LANES)
            out_refs[step][block * pad : (block + 1) * pad] = bins[:, lanes]


def columns(rows, quant_ref, *refs):
    sums_refs, own_ref, refs = refs[:rows], refs[rows], refs[rows + 1 :]
    bins_refs, out_refs = refs[:rows], refs[rows:]
    series = own_ref.shape[1]
    behind = bins_refs[0].shape[0]
    level = F32(0.0)
    for index, value in enumerate(LEVELS):
        level = jnp.where(quant_ref[0] == index, F32(value), level)
    sums = jnp.zeros((DAYS, STORES), F32)
    for ref in sums_refs:
        parts = ref[...].astype(F32)
        for piece in range(PIECES):
            sums = sums + parts[:, piece * STORES : (piece + 1) * STORES]
    shared = sums / (sums[TOTAL_ROW : TOTAL_ROW + 1] / HIST + 1.0)
    shared = jnp.concatenate(split_parts(shared), axis=1)

    own = own_ref[...]
    day = lax.broadcasted_iota(jnp.int32, (DAYS, series), 0)
    store = lax.broadcasted_iota(jnp.int32, (PIECES * STORES, series), 0) % STORES
    region = own[REGION_ROW : REGION_ROW + 1].astype(jnp.int32)
    pick = jnp.where(store == region, 1.0, 0.0).astype(BF16)
    regional = jnp.dot(shared, pick, preferred_element_type=F32)
    wave = jnp.where(day < HORIZON, jnp.tanh(own + regional), 0.0)
    mean = jnp.sum(wave, axis=0, keepdims=True) / HORIZON
    square = jnp.sum(wave * wave, axis=0, keepdims=True) / HORIZON
    gradient = 0.5 + 0.5 * mean - level
    hessian = 0.5 * (1.0 - square)
    rows_of = [
        value[:, block * LANES : (block + 1) * LANES]
        for value in (gradient, hessian, own[NODE_ROW : NODE_ROW + 1])
        for block in range(series // LANES)
    ]
    spare = jnp.zeros((out_refs[0].shape[0] - behind - len(rows_of), LANES), F32)
    tail = jnp.concatenate(rows_of + [spare], axis=0).astype(BF16)
    for bins_ref, out_ref in zip(bins_refs, out_refs):
        out_ref[:behind] = bins_ref[...]
        out_ref[behind:] = tail


def place(tail, cols_ref):
    blocks = cols_ref.shape[1] // LANES
    gradient, hessian, node = (
        jnp.concatenate(
            [tail[at * blocks + block : at * blocks + block + 1] for block in range(blocks)], axis=1
        )
        for at in range(3)
    )
    node_at = lax.broadcasted_iota(jnp.int32, (NODES, cols_ref.shape[1]), 0)
    here_node = node_at == node.astype(jnp.int32)
    for part, value in enumerate((gradient, hessian)):
        value = value * SCALE
        high = value.astype(F8).astype(F32)
        for offset, piece in ((0, high), (2, value - high)):
            at = (part + offset) * NODES
            cols_ref[at : at + NODES] = jnp.where(here_node, piece, 0.0).astype(F8)


def accumulate(sources, feats, first, last, *refs):
    block_refs, refs = refs[:sources], refs[sources:]
    if not first:
        before_ref, refs = refs[0], refs[1:]
    left_ref, refs = refs[0], refs[1:]
    if last:
        best_ref, refs = refs[0], refs[1:]
    bins_held, cols_held = refs
    series = bins_held.shape[3]
    pad = max(feats, 16)
    behind = series // LANES * pad
    for source, ref in enumerate(block_refs):
        bins = jnp.concatenate(
            [ref[block * pad : (block + 1) * pad] for block in range(series // LANES)], axis=1
        )
        bins = bins[:feats].astype(jnp.int32)
        bins_held[source, 0] = jnp.bitwise_and(bins, HALF - 1)
        bins_held[source, 1] = jnp.where(bins >= HALF, 1, 0)
        place(ref[behind:].astype(F32), cols_held.at[source])

    bin_at = lax.broadcasted_iota(jnp.int32, (32, series), 0)

    def spread(source, part, feature):
        row = bins_held[source, part, pl.ds(feature, 1)]
        return jnp.broadcast_to(row, (32, series)).astype(jnp.int8)

    def products(source, pair):
        every = cols_held[source]
        uptos, sets = [], [every]
        for feature in pair:
            within = spread(source, 0, feature)
            uptos += [
                jnp.where(
                    within <= (bin_at + at).astype(jnp.int8), jnp.ones((), F8), jnp.zeros((), F8)
                )
                for at in range(0, HALF, 32)
            ]
            upper = spread(source, 1, feature) == jnp.int8(1)
            sets += [
                jnp.where(upper, every[at : at + 32], jnp.zeros((), F8))
                for at in range(0, every.shape[0], 32)
            ]
        product = lax.dot_general(
            jnp.concatenate(sets, axis=0),
            jnp.concatenate(uptos, axis=0),
            ROW_BY_ROW,
            preferred_element_type=F32,
        )
        count = every.shape[0]
        found = []
        for at in range(len(pair)):
            mine = product[:, at * HALF : (at + 1) * HALF]
            both, upper = mine[:count], mine[(at + 1) * count : (at + 2) * count]
            both = both[: count // 2] + both[count // 2 :]
            upper = upper[: count // 2] + upper[count // 2 :]
            found.append(jnp.concatenate([both - upper, upper], axis=1))
        return found

    def two_features(feature):
        pair = (feature, feature + 1)
        found = products(0, pair)
        if sources > 1:
            found = lax.fori_loop(
                1,
                sources,
                lambda at, total: [a + b for a, b in zip(total, products(at, pair))],
                found,
            )
        if not first:
            found = [value + before_ref[at] for at, value in zip(pair, found)]
        return found

    group = min(feats, 32 if last else 16)

    if not last:

        def one_group(at, carry):
            for member in range(0, group, 2):
                feature = at * group + member
                left_ref[feature], left_ref[feature + 1] = two_features(feature)
            return carry

        lax.fori_loop(0, feats // group, one_group, 0)
        return

    feature_at = lax.broadcasted_iota(jnp.int32, (NODES, LANES), 1)
    last_bin = lax.broadcasted_iota(jnp.int32, (NODES, BINS), 1) == BINS - 1


    def over_all(halves):
        lower, upper = halves[:, :HALF], halves[:, HALF:]
        return jnp.concatenate([lower, upper + lower[:, HALF - 1 :]], axis=1) * (1.0 / SCALE)

    def gains(feature, left, best):
        grad, hess = left[:NODES], left[NODES:]
        all_grad, all_hess = grad[:, BINS - 1 :], hess[:, BINS - 1 :]
        over_grad, over_hess = all_grad - grad, all_hess - hess
        gain = grad * grad / (hess + 1.0) + over_grad * over_grad / (over_hess + 1.0)
        gain = jnp.max(jnp.where(last_bin, -jnp.inf, gain), axis=1, keepdims=True)
        gain = gain - all_grad * all_grad / (all_hess + 1.0)
        return jnp.where(feature_at == feature, gain, best)

    def final_group(at, best):
        for member in range(0, group, 2):
            feature = at * group + member
            for offset, halves in enumerate(two_features(feature)):
                left_ref[feature + offset] = halves
                best = gains(feature + offset, over_all(halves), best)
        return best

    best = lax.fori_loop(0, feats // group, final_group, jnp.zeros((NODES, LANES), F32))
    best = best.T
    width = LANES // NODES
    packed = jnp.concatenate(
        [best[at * (feats // width) : (at + 1) * (feats // width)] for at in range(width)], axis=1
    )
    for target in range(best_ref.shape[0]):
        best_ref[target] = packed


def results(left_ref, packed_ref, hist_ref, best_ref, hist_held, best_held, sems):
    feats = left_ref.shape[0]
    targets, packed_rows, _ = packed_ref.shape
    first_bin = lax.broadcasted_iota(jnp.int32, (2 * NODES, HALF), 1) == 0
    group = min(feats, 4)

    def one_group(at, carry):
        for member in range(group):
            feature = at * group + member
            for half in range(2):
                lanes = slice(half * HALF, (half + 1) * HALF)
                left = left_ref[feature, :, lanes] * (1.0 / SCALE)
                before = jnp.where(first_bin, 0.0, pltpu.roll(left, 1, axis=1))
                hist_held[feature, :, lanes] = left - before
        here = pl.ds(at * group, group)
        pltpu.make_async_copy(hist_held.at[here], hist_ref.at[here], sems.at[0]).start()
        return carry

    for step in range(feats // group):
        one_group(step, 0)
    for target in range(targets):
        packed = packed_ref[target]
        for at in range(LANES // NODES):
            best_held[target, at * packed_rows : (at + 1) * packed_rows] = packed[
                :, at * NODES : (at + 1) * NODES
            ]
    best_copy = pltpu.make_async_copy(best_held, best_ref, sems.at[1])
    best_copy.start()
    pltpu.make_async_copy(hist_held, hist_ref, sems.at[0]).wait()
    best_copy.wait()


def shards(daily_unit_counts, region_ids, node_ids, bin_ids, quant_index, filter_kernels):
    rows = lax.axis_size("rows")
    feat_count = lax.axis_size("feat")
    series = daily_unit_counts.shape[0]
    feats = bin_ids.shape[1] // rows
    pad = max(feats, 16)
    blocks = series // LANES
    vmem = pl.BlockSpec(memory_space=pltpu.VMEM)
    smem = pl.BlockSpec(memory_space=pltpu.SMEM)
    hbm = pl.BlockSpec(memory_space=pl.ANY)
    params = pltpu.CompilerParams(vmem_limit_bytes=VMEM_LIMIT)
    regions = region_ids.reshape(1, series)
    nodes = node_ids.reshape(1, series)

    def exchange(array, step):
        pairs = [(at, partner(at, step, rows)) for at in range(rows)]
        return lax.ppermute(array, "rows", pairs)

    sums, *passed = pl.pallas_call(
        prepare,
        out_shape=[
            jax.ShapeDtypeStruct((DAYS, LANES), BF16),
            jax.ShapeDtypeStruct(daily_unit_counts.shape, BF16),
            jax.ShapeDtypeStruct((1, series), jnp.int32),
            jax.ShapeDtypeStruct((1, series), jnp.int32),
            jax.ShapeDtypeStruct(bin_ids.shape, jnp.int32),
            jax.ShapeDtypeStruct((PIECES * DAYS, LANES), BF16),
        ],
        in_specs=[hbm] * 5,
        out_specs=[vmem] * 6,
        scratch_shapes=[pltpu.VMEM((TAPS, CHANNELS), F32), pltpu.SemaphoreType.DMA((5,))],
        compiler_params=params,
        name="prepare",
    )(
        *(
            pltpu.with_memory_space_constraint(array, pltpu.HBM)
            for array in (daily_unit_counts, regions, nodes, bin_ids, filter_kernels.T)
        )
    )
    own, *bins = pl.pallas_call(
        functools.partial(local_terms, rows),
        out_shape=[jax.ShapeDtypeStruct((DAYS, series), F32)]
        + [jax.ShapeDtypeStruct((blocks * pad, LANES), BF16)] * rows,
        in_specs=[vmem] * 5,
        out_specs=[vmem] * (1 + rows),
        scratch_shapes=[pltpu.VMEM((rows, pad, series), BF16)],
        compiler_params=params,
        name="local_terms",
    )(*passed)

    def exchange_sums(step):
        pairs = [
            (at * feat_count + lane, partner(at, step, rows) * feat_count + beside(lane))
            for at in range(rows)
            for lane in range(feat_count)
        ]
        return lax.ppermute(sums, ("rows", "feat"), pairs)

    def beside(lane):
        return lane ^ 1 if lane ^ 1 < feat_count else lane

    every_sums = [sums] + [exchange_sums(step) for step in range(1, rows)]
    outgoing = pl.pallas_call(
        functools.partial(columns, rows),
        out_shape=[jax.ShapeDtypeStruct((blocks * pad + 4 * blocks, LANES), BF16)] * rows,
        in_specs=[smem] + [vmem] * (2 * rows + 1),
        out_specs=[vmem] * rows,
        compiler_params=params,
        name="columns",
    )(quant_index, *every_sums, own, *bins)
    arrived = [outgoing[0]] + [exchange(outgoing[step], step) for step in range(1, rows)]

    targets = rows * feat_count
    packed_rows = feats * NODES // LANES
    hist_shape = jax.ShapeDtypeStruct((feats, 2 * NODES, BINS), F32)
    steps = [arrived[at : at + 1] for at in range(min(rows, 4) - 1)]
    steps.append(arrived[len(steps) :])
    histogram = None
    for at, sources in enumerate(steps):
        first, last = at == 0, at == len(steps) - 1
        count = len(sources)
        held = [
            pltpu.VMEM((count, 2, feats, series), jnp.int32),
            pltpu.VMEM((count, 4 * NODES, series), F8),
        ]
        operands = sources + ([] if first else [histogram])
        if last:
            out_shape = [hist_shape, jax.ShapeDtypeStruct((targets, packed_rows, LANES), F32)]
            out_specs = [vmem, vmem]
        else:
            out_shape, out_specs = hist_shape, vmem
        histogram = pl.pallas_call(
            functools.partial(accumulate, count, feats, first, last),
            out_shape=out_shape,
            in_specs=[vmem] * len(operands),
            out_specs=out_specs,
            scratch_shapes=held,
            input_output_aliases={} if first else {len(operands) - 1: 0},
            compiler_params=params,
            name=f"accumulate_{at}",
        )(*operands)
    left, best = histogram

    gathered = lax.all_to_all(best, ("feat", "rows"), 0, 0, tiled=True)
    best_shape = jax.ShapeDtypeStruct((targets, feats, NODES), F32)
    histogram, feature_best = pl.pallas_call(
        results,
        out_shape=[hist_shape, best_shape],
        in_specs=[vmem] * 2,
        out_specs=[hbm] * 2,
        scratch_shapes=[
            pltpu.VMEM(hist_shape.shape, F32),
            pltpu.VMEM(best_shape.shape, F32),
            pltpu.SemaphoreType.DMA((2,)),
        ],
        compiler_params=params,
        name="results",
    )(left, gathered)
    return (
        histogram.reshape(1, 1, feats, 2, NODES, BINS),
        feature_best.reshape(feat_count, rows, feats, NODES),
    )


def solution(mesh):
    in_specs = (
        P(("groups", "rows"), None),
        P(("groups", "rows")),
        P(("groups", "rows")),
        P(("groups", "rows"), "feat"),
        P("groups"),
        P(),
    )
    out_specs = (
        P(("groups", "feat"), "rows", None, None, None, None),
        P("groups", None, None, None),
    )
    return jax.shard_map(shards, mesh=mesh, in_specs=in_specs, out_specs=out_specs, check_vma=False)
```

```python
import functools

import jax
import jax.numpy as jnp
from jax import lax
from jax.experimental import pallas as pl
from jax.experimental.pallas import tpu as pltpu
from jax.sharding import PartitionSpec as P

BINS = 256
HALF = BINS // 2
NODES = 32
HIST = 512
HORIZON = 28
FIRST_DAY = HIST - HORIZON
REGIONS = 10
CHANNELS = 8
TAPS = 4
DILATE = (1, 7, 14, 28)
LEVELS = (0.005, 0.025, 0.165, 0.25, 0.5, 0.75, 0.835, 0.975, 0.995)

LANES = 128
DAYS = 32
REGION_ROW = HORIZON
NODE_ROW = HORIZON + 1
TOTAL_ROW = HORIZON
STORES = 16
PIECES = 3
SCALE = 256.0
BF16 = jnp.bfloat16
F32 = jnp.float32
F8 = jnp.float8_e4m3fn
ROW_BY_ROW = (((1,), (1,)), ((), ()))
VMEM_LIMIT = 24 * 2**20


def partner(position, step, count):
    if count & (count - 1) == 0:
        return position ^ step
    return (position + step) % count


def split_parts(values):
    parts = []
    rest = values
    for _ in range(PIECES):
        part = rest.astype(BF16)
        parts.append(part)
        rest = rest - part.astype(F32)
    return parts


def tap_matrix(taps_ref, parity):
    gap = lax.broadcasted_iota(jnp.int32, (DAYS, LANES), 1) - lax.broadcasted_iota(
        jnp.int32, (DAYS, LANES), 0
    )
    first = FIRST_DAY - (HIST - LANES)
    matrix = jnp.zeros((DAYS, LANES), F32)
    for channel in range(parity, CHANNELS, 2):
        for lag in range(TAPS):
            offset = first - 1 - lag * DILATE[(channel // 2) % 4]
            matrix = matrix + jnp.where(
                gap == offset, taps_ref[lag : lag + 1, channel : channel + 1], 0.0
            )
    if parity == 0:
        matrix = matrix - jnp.where(gap == first, 1.0, 0.0)
    day = lax.broadcasted_iota(jnp.int32, (DAYS, LANES), 0)
    return jnp.where(day < HORIZON, matrix, 0.0)


def prepare(*refs):
    given, sums_ref, refs = refs[:5], refs[5], refs[6:]
    counts_ref, region_ref, node_ref, bins_ref, own_taps_ref, taps_ref, sems = refs
    taken = (counts_ref, region_ref, node_ref, bins_ref, taps_ref)
    copies = [
        pltpu.make_async_copy(source, target, sems.at[at])
        for at, (source, target) in enumerate(zip(given, taken))
    ]
    for at in (4, 0, 1, 2, 3):
        copies[at].start()
    series = counts_ref.shape[0]
    copies[4].wait()
    own_taps_ref[...] = jnp.concatenate(split_parts(tap_matrix(taps_ref, 0)), axis=0)
    store_taps = tap_matrix(taps_ref, 1)

    for at in (0, 1, 2):
        copies[at].wait()
    counts = counts_ref[...]
    store = lax.broadcasted_iota(jnp.int32, (STORES, series), 0)
    pick = jnp.where(store == region_ref[...], 1.0, 0.0).astype(BF16)
    totals = jnp.dot(pick, counts, preferred_element_type=F32)
    forecast = lax.dot_general(
        store_taps,
        totals[:, HIST - LANES :],
        ROW_BY_ROW,
        precision=lax.Precision.HIGHEST,
        preferred_element_type=F32,
    )
    over_days = lax.dot_general(
        jnp.ones((DAYS, HIST), F32),
        totals,
        ROW_BY_ROW,
        precision=lax.Precision.HIGHEST,
        preferred_element_type=F32,
    )
    row = lax.broadcasted_iota(jnp.int32, (DAYS, STORES), 0)
    forecast = jnp.where(row == TOTAL_ROW, over_days, forecast)
    sums_ref[...] = jnp.concatenate(
        split_parts(forecast) + [jnp.zeros((DAYS, LANES - PIECES * STORES), BF16)], axis=1
    )
    copies[3].wait()


def local_terms(rows, counts_ref, region_ref, node_ref, bins_ref, taps_ref, own_ref, *refs):
    out_refs, held = refs[:rows], refs[rows]
    counts = counts_ref[...]
    series = counts.shape[0]
    feats = bins_ref.shape[1] // rows
    pad = held.shape[1]
    me = lax.axis_index("rows")
    own = lax.dot_general(
        taps_ref[...], counts[:, HIST - LANES :], ROW_BY_ROW, preferred_element_type=F32
    )
    own = own[:DAYS] + own[DAYS : 2 * DAYS] + own[2 * DAYS :]
    ones = jnp.ones((8, HIST), BF16)
    mean = lax.dot_general(ones, counts, ROW_BY_ROW, preferred_element_type=F32)[:1] / HIST
    own = own / mean
    day = lax.broadcasted_iota(jnp.int32, (DAYS, series), 0)
    own = jnp.where(day == REGION_ROW, region_ref[...].astype(F32), own)
    own_ref[...] = jnp.where(day == NODE_ROW, node_ref[...].astype(F32), own)

    turned = bins_ref[...].astype(F32).T
    for row_block in range(rows):
        part = turned[row_block * feats : (row_block + 1) * feats]
        if pad > feats:
            part = jnp.concatenate([part, jnp.zeros((pad - feats, series), F32)], axis=0)
        held[row_block] = part.astype(BF16)
    for step in range(rows):
        bins = held[partner(me, step, rows)]
        for block in range(series // LANES):
            lanes = slice(block * LANES, (block + 1) * LANES)
            out_refs[step][block * pad : (block + 1) * pad] = bins[:, lanes]


def columns(rows, quant_ref, *refs):
    sums_refs, own_ref, refs = refs[:rows], refs[rows], refs[rows + 1 :]
    bins_refs, out_refs = refs[:rows], refs[rows:]
    series = own_ref.shape[1]
    behind = bins_refs[0].shape[0]
    level = F32(0.0)
    for index, value in enumerate(LEVELS):
        level = jnp.where(quant_ref[0] == index, F32(value), level)
    sums = jnp.zeros((DAYS, STORES), F32)
    for ref in sums_refs:
        parts = ref[...].astype(F32)
        for piece in range(PIECES):
            sums = sums + parts[:, piece * STORES : (piece + 1) * STORES]
    shared = sums / (sums[TOTAL_ROW : TOTAL_ROW + 1] / HIST + 1.0)
    shared = jnp.concatenate(split_parts(shared), axis=1)

    own = own_ref[...]
    day = lax.broadcasted_iota(jnp.int32, (DAYS, series), 0)
    store = lax.broadcasted_iota(jnp.int32, (PIECES * STORES, series), 0) % STORES
    region = own[REGION_ROW : REGION_ROW + 1].astype(jnp.int32)
    pick = jnp.where(store == region, 1.0, 0.0).astype(BF16)
    regional = jnp.dot(shared, pick, preferred_element_type=F32)
    wave = jnp.where(day < HORIZON, jnp.tanh(own + regional), 0.0)
    mean = jnp.sum(wave, axis=0, keepdims=True) / HORIZON
    square = jnp.sum(wave * wave, axis=0, keepdims=True) / HORIZON
    gradient = 0.5 + 0.5 * mean - level
    hessian = 0.5 * (1.0 - square)
    rows_of = [
        value[:, block * LANES : (block + 1) * LANES]
        for value in (gradient, hessian, own[NODE_ROW : NODE_ROW + 1])
        for block in range(series // LANES)
    ]
    spare = jnp.zeros((out_refs[0].shape[0] - behind - len(rows_of), LANES), F32)
    tail = jnp.concatenate(rows_of + [spare], axis=0).astype(BF16)
    for bins_ref, out_ref in zip(bins_refs, out_refs):
        out_ref[:behind] = bins_ref[...]
        out_ref[behind:] = tail


def place(tail, cols_ref):
    blocks = cols_ref.shape[1] // LANES
    gradient, hessian, node = (
        jnp.concatenate(
            [tail[at * blocks + block : at * blocks + block + 1] for block in range(blocks)], axis=1
        )
        for at in range(3)
    )
    node_at = lax.broadcasted_iota(jnp.int32, (NODES, cols_ref.shape[1]), 0)
    here_node = node_at == node.astype(jnp.int32)
    for part, value in enumerate((gradient, hessian)):
        value = value * SCALE
        high = value.astype(F8).astype(F32)
        for offset, piece in ((0, high), (2, value - high)):
            at = (part + offset) * NODES
            cols_ref[at : at + NODES] = jnp.where(here_node, piece, 0.0).astype(F8)


def accumulate(sources, feats, first, last, *refs):
    block_refs, refs = refs[:sources], refs[sources:]
    if not first:
        before_ref, refs = refs[0], refs[1:]
    left_ref, refs = refs[0], refs[1:]
    if last:
        best_ref, refs = refs[0], refs[1:]
    bins_held, cols_held = refs
    series = bins_held.shape[3]
    pad = max(feats, 16)
    behind = series // LANES * pad
    for source, ref in enumerate(block_refs):
        bins = jnp.concatenate(
            [ref[block * pad : (block + 1) * pad] for block in range(series // LANES)], axis=1
        )
        bins = bins[:feats].astype(jnp.int32)
        bins_held[source, 0] = jnp.bitwise_and(bins, HALF - 1)
        bins_held[source, 1] = jnp.where(bins >= HALF, 1, 0)
        place(ref[behind:].astype(F32), cols_held.at[source])

    bin_at = lax.broadcasted_iota(jnp.int32, (32, series), 0)

    def spread(source, part, feature):
        row = bins_held[source, part, pl.ds(feature, 1)]
        return jnp.broadcast_to(row, (32, series)).astype(jnp.int8)

    def products(source, pair):
        every = cols_held[source]
        uptos, sets = [], [every]
        for feature in pair:
            within = spread(source, 0, feature)
            uptos += [
                jnp.where(
                    within <= (bin_at + at).astype(jnp.int8), jnp.ones((), F8), jnp.zeros((), F8)
                )
                for at in range(0, HALF, 32)
            ]
            upper = spread(source, 1, feature) == jnp.int8(1)
            sets += [
                jnp.where(upper, every[at : at + 32], jnp.zeros((), F8))
                for at in range(0, every.shape[0], 32)
            ]
        product = lax.dot_general(
            jnp.concatenate(sets, axis=0),
            jnp.concatenate(uptos, axis=0),
            ROW_BY_ROW,
            preferred_element_type=F32,
        )
        count = every.shape[0]
        found = []
        for at in range(len(pair)):
            mine = product[:, at * HALF : (at + 1) * HALF]
            both, upper = mine[:count], mine[(at + 1) * count : (at + 2) * count]
            both = both[: count // 2] + both[count // 2 :]
            upper = upper[: count // 2] + upper[count // 2 :]
            found.append(jnp.concatenate([both - upper, upper], axis=1))
        return found

    def two_features(feature):
        pair = (feature, feature + 1)
        found = products(0, pair)
        if sources > 1:
            found = lax.fori_loop(
                1,
                sources,
                lambda at, total: [a + b for a, b in zip(total, products(at, pair))],
                found,
            )
        if not first:
            found = [value + before_ref[at] for at, value in zip(pair, found)]
        return found

    group = min(feats, 32 if last else 16)

    if not last:

        def one_group(at, carry):
            for member in range(0, group, 2):
                feature = at * group + member
                left_ref[feature], left_ref[feature + 1] = two_features(feature)
            return carry

        lax.fori_loop(0, feats // group, one_group, 0)
        return

    feature_at = lax.broadcasted_iota(jnp.int32, (NODES, LANES), 1)
    last_bin = lax.broadcasted_iota(jnp.int32, (NODES, BINS), 1) == BINS - 1


    def over_all(halves):
        lower, upper = halves[:, :HALF], halves[:, HALF:]
        return jnp.concatenate([lower, upper + lower[:, HALF - 1 :]], axis=1) * (1.0 / SCALE)

    def gains(feature, left, best):
        grad, hess = left[:NODES], left[NODES:]
        all_grad, all_hess = grad[:, BINS - 1 :], hess[:, BINS - 1 :]
        over_grad, over_hess = all_grad - grad, all_hess - hess
        gain = grad * grad / (hess + 1.0) + over_grad * over_grad / (over_hess + 1.0)
        gain = jnp.max(jnp.where(last_bin, -jnp.inf, gain), axis=1, keepdims=True)
        gain = gain - all_grad * all_grad / (all_hess + 1.0)
        return jnp.where(feature_at == feature, gain, best)

    def final_group(at, best):
        for member in range(0, group, 2):
            feature = at * group + member
            for offset, halves in enumerate(two_features(feature)):
                left_ref[feature + offset] = halves
                best = gains(feature + offset, over_all(halves), best)
        return best

    best = lax.fori_loop(0, feats // group, final_group, jnp.zeros((NODES, LANES), F32))
    best = best.T
    width = LANES // NODES
    packed = jnp.concatenate(
        [best[at * (feats // width) : (at + 1) * (feats // width)] for at in range(width)], axis=1
    )
    for target in range(best_ref.shape[0]):
        best_ref[target] = packed


def results(left_ref, packed_ref, hist_ref, best_ref, hist_held, best_held, sems):
    feats = left_ref.shape[0]
    targets, packed_rows, _ = packed_ref.shape
    first_bin = lax.broadcasted_iota(jnp.int32, (2 * NODES, HALF), 1) == 0
    group = min(feats, 4)

    def one_group(at, carry):
        for member in range(group):
            feature = at * group + member
            for half in range(2):
                lanes = slice(half * HALF, (half + 1) * HALF)
                left = left_ref[feature, :, lanes] * (1.0 / SCALE)
                before = jnp.where(first_bin, 0.0, pltpu.roll(left, 1, axis=1))
                hist_held[feature, :, lanes] = left - before
        here = pl.ds(at * group, group)
        pltpu.make_async_copy(hist_held.at[here], hist_ref.at[here], sems.at[0]).start()
        return carry

    for step in range(feats // group):
        one_group(step, 0)
    for target in range(targets):
        packed = packed_ref[target]
        for at in range(LANES // NODES):
            best_held[target, at * packed_rows : (at + 1) * packed_rows] = packed[
                :, at * NODES : (at + 1) * NODES
            ]
    best_copy = pltpu.make_async_copy(best_held, best_ref, sems.at[1])
    best_copy.start()
    pltpu.make_async_copy(hist_held, hist_ref, sems.at[0]).wait()
    best_copy.wait()


def shards(daily_unit_counts, region_ids, node_ids, bin_ids, quant_index, filter_kernels):
    rows = lax.axis_size("rows")
    feat_count = lax.axis_size("feat")
    series = daily_unit_counts.shape[0]
    feats = bin_ids.shape[1] // rows
    pad = max(feats, 16)
    blocks = series // LANES
    vmem = pl.BlockSpec(memory_space=pltpu.VMEM)
    smem = pl.BlockSpec(memory_space=pltpu.SMEM)
    hbm = pl.BlockSpec(memory_space=pl.ANY)
    params = pltpu.CompilerParams(vmem_limit_bytes=VMEM_LIMIT)
    regions = region_ids.reshape(1, series)
    nodes = node_ids.reshape(1, series)

    def exchange(array, step):
        pairs = [(at, partner(at, step, rows)) for at in range(rows)]
        return lax.ppermute(array, "rows", pairs)

    sums, *passed = pl.pallas_call(
        prepare,
        out_shape=[
            jax.ShapeDtypeStruct((DAYS, LANES), BF16),
            jax.ShapeDtypeStruct(daily_unit_counts.shape, BF16),
            jax.ShapeDtypeStruct((1, series), jnp.int32),
            jax.ShapeDtypeStruct((1, series), jnp.int32),
            jax.ShapeDtypeStruct(bin_ids.shape, jnp.int32),
            jax.ShapeDtypeStruct((PIECES * DAYS, LANES), BF16),
        ],
        in_specs=[hbm] * 5,
        out_specs=[vmem] * 6,
        scratch_shapes=[pltpu.VMEM((TAPS, CHANNELS), F32), pltpu.SemaphoreType.DMA((5,))],
        compiler_params=params,
        name="prepare",
    )(
        *(
            pltpu.with_memory_space_constraint(array, pltpu.HBM)
            for array in (daily_unit_counts, regions, nodes, bin_ids, filter_kernels.T)
        )
    )
    own, *bins = pl.pallas_call(
        functools.partial(local_terms, rows),
        out_shape=[jax.ShapeDtypeStruct((DAYS, series), F32)]
        + [jax.ShapeDtypeStruct((blocks * pad, LANES), BF16)] * rows,
        in_specs=[vmem] * 5,
        out_specs=[vmem] * (1 + rows),
        scratch_shapes=[pltpu.VMEM((rows, pad, series), BF16)],
        compiler_params=params,
        name="local_terms",
    )(*passed)

    def exchange_sums(step):
        pairs = [
            (at * feat_count + lane, partner(at, step, rows) * feat_count + beside(lane))
            for at in range(rows)
            for lane in range(feat_count)
        ]
        return lax.ppermute(sums, ("rows", "feat"), pairs)

    def beside(lane):
        return lane ^ 1 if lane ^ 1 < feat_count else lane

    every_sums = [sums] + [exchange_sums(step) for step in range(1, rows)]
    outgoing = pl.pallas_call(
        functools.partial(columns, rows),
        out_shape=[jax.ShapeDtypeStruct((blocks * pad + 4 * blocks, LANES), BF16)] * rows,
        in_specs=[smem] + [vmem] * (2 * rows + 1),
        out_specs=[vmem] * rows,
        compiler_params=params,
        name="columns",
    )(quant_index, *every_sums, own, *bins)
    order = [2, 1, *range(3, rows)] if rows > 2 else [*range(1, rows)]
    arrived = [outgoing[0]] + [exchange(outgoing[step], step) for step in order]

    targets = rows * feat_count
    packed_rows = feats * NODES // LANES
    hist_shape = jax.ShapeDtypeStruct((feats, 2 * NODES, BINS), F32)
    steps = [arrived[at : at + 1] for at in range(min(rows, 4) - 1)]
    steps.append(arrived[len(steps) :])
    histogram = None
    for at, sources in enumerate(steps):
        first, last = at == 0, at == len(steps) - 1
        count = len(sources)
        held = [
            pltpu.VMEM((count, 2, feats, series), jnp.int32),
            pltpu.VMEM((count, 4 * NODES, series), F8),
        ]
        operands = sources + ([] if first else [histogram])
        if last:
            out_shape = [hist_shape, jax.ShapeDtypeStruct((targets, packed_rows, LANES), F32)]
            out_specs = [vmem, vmem]
        else:
            out_shape, out_specs = hist_shape, vmem
        histogram = pl.pallas_call(
            functools.partial(accumulate, count, feats, first, last),
            out_shape=out_shape,
            in_specs=[vmem] * len(operands),
            out_specs=out_specs,
            scratch_shapes=held,
            input_output_aliases={} if first else {len(operands) - 1: 0},
            compiler_params=params,
            name=f"accumulate_{at}",
        )(*operands)
    left, best = histogram

    gathered = lax.all_to_all(best, ("feat", "rows"), 0, 0, tiled=True)
    best_shape = jax.ShapeDtypeStruct((targets, feats, NODES), F32)
    histogram, feature_best = pl.pallas_call(
        results,
        out_shape=[hist_shape, best_shape],
        in_specs=[vmem] * 2,
        out_specs=[hbm] * 2,
        scratch_shapes=[
            pltpu.VMEM(hist_shape.shape, F32),
            pltpu.VMEM(best_shape.shape, F32),
            pltpu.SemaphoreType.DMA((2,)),
        ],
        compiler_params=params,
        name="results",
    )(left, gathered)
    return (
        histogram.reshape(1, 1, feats, 2, NODES, BINS),
        feature_best.reshape(feat_count, rows, feats, NODES),
    )


def solution(mesh):
    in_specs = (
        P(("groups", "rows"), None),
        P(("groups", "rows")),
        P(("groups", "rows")),
        P(("groups", "rows"), "feat"),
        P("groups"),
        P(),
    )
    out_specs = (
        P(("groups", "feat"), "rows", None, None, None, None),
        P("groups", None, None, None),
    )
    return jax.shard_map(shards, mesh=mesh, in_specs=in_specs, out_specs=out_specs, check_vma=False)
```

```python
import functools

import jax
import jax.numpy as jnp
from jax import lax
from jax.experimental import pallas as pl
from jax.experimental.pallas import tpu as pltpu
from jax.sharding import PartitionSpec as P

BINS = 256
HALF = BINS // 2
NODES = 32
HIST = 512
HORIZON = 28
FIRST_DAY = HIST - HORIZON
REGIONS = 10
CHANNELS = 8
TAPS = 4
DILATE = (1, 7, 14, 28)
LEVELS = (0.005, 0.025, 0.165, 0.25, 0.5, 0.75, 0.835, 0.975, 0.995)

LANES = 128
DAYS = 32
REGION_ROW = HORIZON
NODE_ROW = HORIZON + 1
TOTAL_ROW = HORIZON
STORES = 16
PIECES = 3
SCALE = 256.0
BF16 = jnp.bfloat16
F32 = jnp.float32
F8 = jnp.float8_e4m3fn
ROW_BY_ROW = (((1,), (1,)), ((), ()))
VMEM_LIMIT = 24 * 2**20


def partner(position, step, count):
    if count & (count - 1) == 0:
        return position ^ step
    return (position + step) % count


def split_parts(values):
    parts = []
    rest = values
    for _ in range(PIECES):
        part = rest.astype(BF16)
        parts.append(part)
        rest = rest - part.astype(F32)
    return parts


def tap_matrix(taps_ref, parity):
    gap = lax.broadcasted_iota(jnp.int32, (DAYS, LANES), 1) - lax.broadcasted_iota(
        jnp.int32, (DAYS, LANES), 0
    )
    first = FIRST_DAY - (HIST - LANES)
    matrix = jnp.zeros((DAYS, LANES), F32)
    for channel in range(parity, CHANNELS, 2):
        for lag in range(TAPS):
            offset = first - 1 - lag * DILATE[(channel // 2) % 4]
            matrix = matrix + jnp.where(
                gap == offset, taps_ref[lag : lag + 1, channel : channel + 1], 0.0
            )
    if parity == 0:
        matrix = matrix - jnp.where(gap == first, 1.0, 0.0)
    day = lax.broadcasted_iota(jnp.int32, (DAYS, LANES), 0)
    return jnp.where(day < HORIZON, matrix, 0.0)


def prepare(*refs):
    given, sums_ref, refs = refs[:5], refs[5], refs[6:]
    counts_ref, region_ref, node_ref, bins_ref, own_taps_ref, taps_ref, sems = refs
    taken = (counts_ref, region_ref, node_ref, bins_ref, taps_ref)
    copies = [
        pltpu.make_async_copy(source, target, sems.at[at])
        for at, (source, target) in enumerate(zip(given, taken))
    ]
    for at in (4, 0, 1, 2, 3):
        copies[at].start()
    series = counts_ref.shape[0]
    copies[4].wait()
    own_taps_ref[...] = jnp.concatenate(split_parts(tap_matrix(taps_ref, 0)), axis=0)
    store_taps = tap_matrix(taps_ref, 1)

    for at in (0, 1, 2):
        copies[at].wait()
    counts = counts_ref[...]
    store = lax.broadcasted_iota(jnp.int32, (STORES, series), 0)
    pick = jnp.where(store == region_ref[...], 1.0, 0.0).astype(BF16)
    totals = jnp.dot(pick, counts, preferred_element_type=F32)
    forecast = lax.dot_general(
        store_taps,
        totals[:, HIST - LANES :],
        ROW_BY_ROW,
        precision=lax.Precision.HIGHEST,
        preferred_element_type=F32,
    )
    over_days = lax.dot_general(
        jnp.ones((DAYS, HIST), F32),
        totals,
        ROW_BY_ROW,
        precision=lax.Precision.HIGHEST,
        preferred_element_type=F32,
    )
    row = lax.broadcasted_iota(jnp.int32, (DAYS, STORES), 0)
    forecast = jnp.where(row == TOTAL_ROW, over_days, forecast)
    sums_ref[...] = jnp.concatenate(
        split_parts(forecast) + [jnp.zeros((DAYS, LANES - PIECES * STORES), BF16)], axis=1
    )
    copies[3].wait()


def local_terms(rows, counts_ref, region_ref, node_ref, bins_ref, taps_ref, own_ref, *refs):
    out_refs, held = refs[:rows], refs[rows]
    counts = counts_ref[...]
    series = counts.shape[0]
    feats = bins_ref.shape[1] // rows
    pad = held.shape[1]
    me = lax.axis_index("rows")
    own = lax.dot_general(
        taps_ref[...], counts[:, HIST - LANES :], ROW_BY_ROW, preferred_element_type=F32
    )
    own = own[:DAYS] + own[DAYS : 2 * DAYS] + own[2 * DAYS :]
    ones = jnp.ones((8, HIST), BF16)
    mean = lax.dot_general(ones, counts, ROW_BY_ROW, preferred_element_type=F32)[:1] / HIST
    own = own / mean
    day = lax.broadcasted_iota(jnp.int32, (DAYS, series), 0)
    own = jnp.where(day == REGION_ROW, region_ref[...].astype(F32), own)
    own_ref[...] = jnp.where(day == NODE_ROW, node_ref[...].astype(F32), own)

    turned = bins_ref[...].astype(F32).T
    for row_block in range(rows):
        part = turned[row_block * feats : (row_block + 1) * feats]
        if pad > feats:
            part = jnp.concatenate([part, jnp.zeros((pad - feats, series), F32)], axis=0)
        held[row_block] = part.astype(BF16)
    for step in range(rows):
        bins = held[partner(me, step, rows)]
        for block in range(series // LANES):
            lanes = slice(block * LANES, (block + 1) * LANES)
            out_refs[step][block * pad : (block + 1) * pad] = bins[:, lanes]


def columns(rows, quant_ref, *refs):
    sums_refs, own_ref, refs = refs[:rows], refs[rows], refs[rows + 1 :]
    bins_refs, out_refs = refs[:rows], refs[rows:]
    series = own_ref.shape[1]
    behind = bins_refs[0].shape[0]
    level = F32(0.0)
    for index, value in enumerate(LEVELS):
        level = jnp.where(quant_ref[0] == index, F32(value), level)
    sums = jnp.zeros((DAYS, STORES), F32)
    for ref in sums_refs:
        parts = ref[...].astype(F32)
        for piece in range(PIECES):
            sums = sums + parts[:, piece * STORES : (piece + 1) * STORES]
    shared = sums / (sums[TOTAL_ROW : TOTAL_ROW + 1] / HIST + 1.0)
    shared = jnp.concatenate(split_parts(shared), axis=1)

    own = own_ref[...]
    day = lax.broadcasted_iota(jnp.int32, (DAYS, series), 0)
    store = lax.broadcasted_iota(jnp.int32, (PIECES * STORES, series), 0) % STORES
    region = own[REGION_ROW : REGION_ROW + 1].astype(jnp.int32)
    pick = jnp.where(store == region, 1.0, 0.0).astype(BF16)
    regional = jnp.dot(shared, pick, preferred_element_type=F32)
    wave = jnp.where(day < HORIZON, jnp.tanh(own + regional), 0.0)
    mean = jnp.sum(wave, axis=0, keepdims=True) / HORIZON
    square = jnp.sum(wave * wave, axis=0, keepdims=True) / HORIZON
    gradient = 0.5 + 0.5 * mean - level
    hessian = 0.5 * (1.0 - square)
    rows_of = [
        value[:, block * LANES : (block + 1) * LANES]
        for value in (gradient, hessian, own[NODE_ROW : NODE_ROW + 1])
        for block in range(series // LANES)
    ]
    spare = jnp.zeros((out_refs[0].shape[0] - behind - len(rows_of), LANES), F32)
    tail = jnp.concatenate(rows_of + [spare], axis=0).astype(BF16)
    for bins_ref, out_ref in zip(bins_refs, out_refs):
        out_ref[:behind] = bins_ref[...]
        out_ref[behind:] = tail


def place(tail, cols_ref):
    blocks = cols_ref.shape[1] // LANES
    gradient, hessian, node = (
        jnp.concatenate(
            [tail[at * blocks + block : at * blocks + block + 1] for block in range(blocks)], axis=1
        )
        for at in range(3)
    )
    node_at = lax.broadcasted_iota(jnp.int32, (NODES, cols_ref.shape[1]), 0)
    here_node = node_at == node.astype(jnp.int32)
    for part, value in enumerate((gradient, hessian)):
        value = value * SCALE
        high = value.astype(F8).astype(F32)
        for offset, piece in ((0, high), (2, value - high)):
            at = (part + offset) * NODES
            cols_ref[at : at + NODES] = jnp.where(here_node, piece, 0.0).astype(F8)


def accumulate(sources, feats, first, last, *refs):
    block_refs, refs = refs[:sources], refs[sources:]
    if not first:
        before_ref, refs = refs[0], refs[1:]
    left_ref, refs = refs[0], refs[1:]
    if last:
        best_ref, refs = refs[0], refs[1:]
    bins_held, cols_held = refs
    series = bins_held.shape[3]
    pad = max(feats, 16)
    behind = series // LANES * pad
    for source, ref in enumerate(block_refs):
        bins = jnp.concatenate(
            [ref[block * pad : (block + 1) * pad] for block in range(series // LANES)], axis=1
        )
        bins = bins[:feats].astype(jnp.int32)
        bins_held[source, 0] = jnp.bitwise_and(bins, HALF - 1)
        bins_held[source, 1] = jnp.where(bins >= HALF, 1, 0)
        place(ref[behind:].astype(F32), cols_held.at[source])

    bin_at = lax.broadcasted_iota(jnp.int32, (32, series), 0)

    def spread(source, part, feature):
        row = bins_held[source, part, pl.ds(feature, 1)]
        return jnp.broadcast_to(row, (32, series)).astype(jnp.int8)

    def products(source, pair):
        every = cols_held[source]
        uptos, sets = [], [every]
        for feature in pair:
            within = spread(source, 0, feature)
            uptos += [
                jnp.where(
                    within <= (bin_at + at).astype(jnp.int8), jnp.ones((), F8), jnp.zeros((), F8)
                )
                for at in range(0, HALF, 32)
            ]
            upper = spread(source, 1, feature) == jnp.int8(1)
            sets += [
                jnp.where(upper, every[at : at + 32], jnp.zeros((), F8))
                for at in range(0, every.shape[0], 32)
            ]
        product = lax.dot_general(
            jnp.concatenate(sets, axis=0),
            jnp.concatenate(uptos, axis=0),
            ROW_BY_ROW,
            preferred_element_type=F32,
        )
        count = every.shape[0]
        found = []
        for at in range(len(pair)):
            mine = product[:, at * HALF : (at + 1) * HALF]
            both, upper = mine[:count], mine[(at + 1) * count : (at + 2) * count]
            both = both[: count // 2] + both[count // 2 :]
            upper = upper[: count // 2] + upper[count // 2 :]
            found.append(jnp.concatenate([both - upper, upper], axis=1))
        return found

    def two_features(feature):
        pair = (feature, feature + 1)
        found = products(0, pair)
        if sources > 1:
            found = lax.fori_loop(
                1,
                sources,
                lambda at, total: [a + b for a, b in zip(total, products(at, pair))],
                found,
            )
        if not first:
            found = [value + before_ref[at] for at, value in zip(pair, found)]
        return found

    group = min(feats, 32 if last else 16)

    if not last:

        def one_group(at, carry):
            for member in range(0, group, 2):
                feature = at * group + member
                left_ref[feature], left_ref[feature + 1] = two_features(feature)
            return carry

        lax.fori_loop(0, feats // group, one_group, 0)
        return

    feature_at = lax.broadcasted_iota(jnp.int32, (NODES, LANES), 1)
    last_bin = lax.broadcasted_iota(jnp.int32, (NODES, BINS), 1) == BINS - 1


    def over_all(halves):
        lower, upper = halves[:, :HALF], halves[:, HALF:]
        return jnp.concatenate([lower, upper + lower[:, HALF - 1 :]], axis=1) * (1.0 / SCALE)

    def gains(feature, left, best):
        grad, hess = left[:NODES], left[NODES:]
        all_grad, all_hess = grad[:, BINS - 1 :], hess[:, BINS - 1 :]
        over_grad, over_hess = all_grad - grad, all_hess - hess
        gain = grad * grad / (hess + 1.0) + over_grad * over_grad / (over_hess + 1.0)
        gain = jnp.max(jnp.where(last_bin, -jnp.inf, gain), axis=1, keepdims=True)
        gain = gain - all_grad * all_grad / (all_hess + 1.0)
        return jnp.where(feature_at == feature, gain, best)

    def final_group(at, best):
        for member in range(0, group, 2):
            feature = at * group + member
            for offset, halves in enumerate(two_features(feature)):
                left_ref[feature + offset] = halves
                best = gains(feature + offset, over_all(halves), best)
        return best

    best = lax.fori_loop(0, feats // group, final_group, jnp.zeros((NODES, LANES), F32))
    best = best.T
    width = LANES // NODES
    packed = jnp.concatenate(
        [best[at * (feats // width) : (at + 1) * (feats // width)] for at in range(width)], axis=1
    )
    for target in range(best_ref.shape[0]):
        best_ref[target] = packed


def results(left_ref, packed_ref, hist_ref, best_ref, hist_held, best_held, sems):
    feats = left_ref.shape[0]
    targets, packed_rows, _ = packed_ref.shape
    first_bin = lax.broadcasted_iota(jnp.int32, (2 * NODES, HALF), 1) == 0
    group = min(feats, 4)

    def one_group(at, carry):
        for member in range(group):
            feature = at * group + member
            for half in range(2):
                lanes = slice(half * HALF, (half + 1) * HALF)
                left = left_ref[feature, :, lanes] * (1.0 / SCALE)
                before = jnp.where(first_bin, 0.0, pltpu.roll(left, 1, axis=1))
                hist_held[feature, :, lanes] = left - before
        here = pl.ds(at * group, group)
        pltpu.make_async_copy(hist_held.at[here], hist_ref.at[here], sems.at[0]).start()
        return carry

    for step in range(feats // group):
        one_group(step, 0)
    for target in range(targets):
        packed = packed_ref[target]
        for at in range(LANES // NODES):
            best_held[target, at * packed_rows : (at + 1) * packed_rows] = packed[
                :, at * NODES : (at + 1) * NODES
            ]
    best_copy = pltpu.make_async_copy(best_held, best_ref, sems.at[1])
    best_copy.start()
    pltpu.make_async_copy(hist_held, hist_ref, sems.at[0]).wait()
    best_copy.wait()


def shards(daily_unit_counts, region_ids, node_ids, bin_ids, quant_index, filter_kernels):
    rows = lax.axis_size("rows")
    feat_count = lax.axis_size("feat")
    series = daily_unit_counts.shape[0]
    feats = bin_ids.shape[1] // rows
    pad = max(feats, 16)
    blocks = series // LANES
    vmem = pl.BlockSpec(memory_space=pltpu.VMEM)
    smem = pl.BlockSpec(memory_space=pltpu.SMEM)
    hbm = pl.BlockSpec(memory_space=pl.ANY)
    params = pltpu.CompilerParams(vmem_limit_bytes=VMEM_LIMIT)
    regions = region_ids.reshape(1, series)
    nodes = node_ids.reshape(1, series)

    def exchange(array, step):
        pairs = [(at, partner(at, step, rows)) for at in range(rows)]
        return lax.ppermute(array, "rows", pairs)

    sums, *passed = pl.pallas_call(
        prepare,
        out_shape=[
            jax.ShapeDtypeStruct((DAYS, LANES), BF16),
            jax.ShapeDtypeStruct(daily_unit_counts.shape, BF16),
            jax.ShapeDtypeStruct((1, series), jnp.int32),
            jax.ShapeDtypeStruct((1, series), jnp.int32),
            jax.ShapeDtypeStruct(bin_ids.shape, jnp.int32),
            jax.ShapeDtypeStruct((PIECES * DAYS, LANES), BF16),
        ],
        in_specs=[hbm] * 5,
        out_specs=[vmem] * 6,
        scratch_shapes=[pltpu.VMEM((TAPS, CHANNELS), F32), pltpu.SemaphoreType.DMA((5,))],
        compiler_params=params,
        name="prepare",
    )(
        *(
            pltpu.with_memory_space_constraint(array, pltpu.HBM)
            for array in (daily_unit_counts, regions, nodes, bin_ids, filter_kernels.T)
        )
    )
    own, *bins = pl.pallas_call(
        functools.partial(local_terms, rows),
        out_shape=[jax.ShapeDtypeStruct((DAYS, series), F32)]
        + [jax.ShapeDtypeStruct((blocks * pad, LANES), BF16)] * rows,
        in_specs=[vmem] * 5,
        out_specs=[vmem] * (1 + rows),
        scratch_shapes=[pltpu.VMEM((rows, pad, series), BF16)],
        compiler_params=params,
        name="local_terms",
    )(*passed)

    def exchange_sums(step):
        to = beside if step < 3 else int
        pairs = [
            (at * feat_count + lane, partner(at, step, rows) * feat_count + to(lane))
            for at in range(rows)
            for lane in range(feat_count)
        ]
        return lax.ppermute(sums, ("rows", "feat"), pairs)

    def beside(lane):
        return lane ^ 1 if lane ^ 1 < feat_count else lane

    every_sums = [sums] + [exchange_sums(step) for step in range(1, rows)]
    outgoing = pl.pallas_call(
        functools.partial(columns, rows),
        out_shape=[jax.ShapeDtypeStruct((blocks * pad + 4 * blocks, LANES), BF16)] * rows,
        in_specs=[smem] + [vmem] * (2 * rows + 1),
        out_specs=[vmem] * rows,
        compiler_params=params,
        name="columns",
    )(quant_index, *every_sums, own, *bins)
    order = [2, 1, *range(3, rows)] if rows > 2 else [*range(1, rows)]
    arrived = [outgoing[0]] + [exchange(outgoing[step], step) for step in order]

    targets = rows * feat_count
    packed_rows = feats * NODES // LANES
    hist_shape = jax.ShapeDtypeStruct((feats, 2 * NODES, BINS), F32)
    steps = [arrived[at : at + 1] for at in range(min(rows, 4) - 1)]
    steps.append(arrived[len(steps) :])
    histogram = None
    for at, sources in enumerate(steps):
        first, last = at == 0, at == len(steps) - 1
        count = len(sources)
        held = [
            pltpu.VMEM((count, 2, feats, series), jnp.int32),
            pltpu.VMEM((count, 4 * NODES, series), F8),
        ]
        operands = sources + ([] if first else [histogram])
        if last:
            out_shape = [hist_shape, jax.ShapeDtypeStruct((targets, packed_rows, LANES), F32)]
            out_specs = [vmem, vmem]
        else:
            out_shape, out_specs = hist_shape, vmem
        histogram = pl.pallas_call(
            functools.partial(accumulate, count, feats, first, last),
            out_shape=out_shape,
            in_specs=[vmem] * len(operands),
            out_specs=out_specs,
            scratch_shapes=held,
            input_output_aliases={} if first else {len(operands) - 1: 0},
            compiler_params=params,
            name=f"accumulate_{at}",
        )(*operands)
    left, best = histogram

    gathered = lax.all_to_all(best, ("feat", "rows"), 0, 0, tiled=True)
    best_shape = jax.ShapeDtypeStruct((targets, feats, NODES), F32)
    histogram, feature_best = pl.pallas_call(
        results,
        out_shape=[hist_shape, best_shape],
        in_specs=[vmem] * 2,
        out_specs=[hbm] * 2,
        scratch_shapes=[
            pltpu.VMEM(hist_shape.shape, F32),
            pltpu.VMEM(best_shape.shape, F32),
            pltpu.SemaphoreType.DMA((2,)),
        ],
        compiler_params=params,
        name="results",
    )(left, gathered)
    return (
        histogram.reshape(1, 1, feats, 2, NODES, BINS),
        feature_best.reshape(feat_count, rows, feats, NODES),
    )


def solution(mesh):
    in_specs = (
        P(("groups", "rows"), None),
        P(("groups", "rows")),
        P(("groups", "rows")),
        P(("groups", "rows"), "feat"),
        P("groups"),
        P(),
    )
    out_specs = (
        P(("groups", "feat"), "rows", None, None, None, None),
        P("groups", None, None, None),
    )
    return jax.shard_map(shards, mesh=mesh, in_specs=in_specs, out_specs=out_specs, check_vma=False)
```

```python
import functools

import jax
import jax.numpy as jnp
from jax import lax
from jax.experimental import pallas as pl
from jax.experimental.pallas import tpu as pltpu
from jax.sharding import PartitionSpec as P

BINS = 256
HALF = BINS // 2
NODES = 32
HIST = 512
HORIZON = 28
FIRST_DAY = HIST - HORIZON
REGIONS = 10
CHANNELS = 8
TAPS = 4
DILATE = (1, 7, 14, 28)
LEVELS = (0.005, 0.025, 0.165, 0.25, 0.5, 0.75, 0.835, 0.975, 0.995)

LANES = 128
DAYS = 32
REGION_ROW = HORIZON
NODE_ROW = HORIZON + 1
TOTAL_ROW = HORIZON
STORES = 16
PIECES = 3
SCALE = 256.0
BF16 = jnp.bfloat16
F32 = jnp.float32
F8 = jnp.float8_e4m3fn
ROW_BY_ROW = (((1,), (1,)), ((), ()))
VMEM_LIMIT = 24 * 2**20


def partner(position, step, count):
    if count & (count - 1) == 0:
        return position ^ step
    return (position + step) % count


def split_parts(values):
    parts = []
    rest = values
    for _ in range(PIECES):
        part = rest.astype(BF16)
        parts.append(part)
        rest = rest - part.astype(F32)
    return parts


def tap_matrix(taps_ref, parity):
    gap = lax.broadcasted_iota(jnp.int32, (DAYS, LANES), 1) - lax.broadcasted_iota(
        jnp.int32, (DAYS, LANES), 0
    )
    first = FIRST_DAY - (HIST - LANES)
    matrix = jnp.zeros((DAYS, LANES), F32)
    for channel in range(parity, CHANNELS, 2):
        for lag in range(TAPS):
            offset = first - 1 - lag * DILATE[(channel // 2) % 4]
            matrix = matrix + jnp.where(
                gap == offset, taps_ref[lag : lag + 1, channel : channel + 1], 0.0
            )
    if parity == 0:
        matrix = matrix - jnp.where(gap == first, 1.0, 0.0)
    day = lax.broadcasted_iota(jnp.int32, (DAYS, LANES), 0)
    return jnp.where(day < HORIZON, matrix, 0.0)


def prepare(*refs):
    given, sums_ref, refs = refs[:5], refs[5], refs[6:]
    counts_ref, region_ref, node_ref, bins_ref, own_taps_ref, taps_ref, sems = refs
    taken = (counts_ref, region_ref, node_ref, bins_ref, taps_ref)
    copies = [
        pltpu.make_async_copy(source, target, sems.at[at])
        for at, (source, target) in enumerate(zip(given, taken))
    ]
    for at in (4, 0, 1, 2, 3):
        copies[at].start()
    series = counts_ref.shape[0]
    copies[4].wait()
    own_taps_ref[...] = jnp.concatenate(split_parts(tap_matrix(taps_ref, 0)), axis=0)
    store_taps = tap_matrix(taps_ref, 1)

    for at in (0, 1, 2):
        copies[at].wait()
    counts = counts_ref[...]
    store = lax.broadcasted_iota(jnp.int32, (STORES, series), 0)
    pick = jnp.where(store == region_ref[...], 1.0, 0.0).astype(BF16)
    totals = jnp.dot(pick, counts, preferred_element_type=F32)
    forecast = lax.dot_general(
        store_taps,
        totals[:, HIST - LANES :],
        ROW_BY_ROW,
        precision=lax.Precision.HIGHEST,
        preferred_element_type=F32,
    )
    over_days = lax.dot_general(
        jnp.ones((DAYS, HIST), F32),
        totals,
        ROW_BY_ROW,
        precision=lax.Precision.HIGHEST,
        preferred_element_type=F32,
    )
    row = lax.broadcasted_iota(jnp.int32, (DAYS, STORES), 0)
    forecast = jnp.where(row == TOTAL_ROW, over_days, forecast)
    sums_ref[...] = jnp.concatenate(
        split_parts(forecast) + [jnp.zeros((DAYS, LANES - PIECES * STORES), BF16)], axis=1
    )
    copies[3].wait()


def local_terms(rows, counts_ref, region_ref, node_ref, bins_ref, taps_ref, own_ref, *refs):
    out_refs, held = refs[:rows], refs[rows]
    counts = counts_ref[...]
    series = counts.shape[0]
    feats = bins_ref.shape[1] // rows
    pad = held.shape[1]
    me = lax.axis_index("rows")
    own = lax.dot_general(
        taps_ref[...], counts[:, HIST - LANES :], ROW_BY_ROW, preferred_element_type=F32
    )
    own = own[:DAYS] + own[DAYS : 2 * DAYS] + own[2 * DAYS :]
    ones = jnp.ones((8, HIST), BF16)
    mean = lax.dot_general(ones, counts, ROW_BY_ROW, preferred_element_type=F32)[:1] / HIST
    own = own / mean
    day = lax.broadcasted_iota(jnp.int32, (DAYS, series), 0)
    own = jnp.where(day == REGION_ROW, region_ref[...].astype(F32), own)
    own_ref[...] = jnp.where(day == NODE_ROW, node_ref[...].astype(F32), own)

    turned = bins_ref[...].astype(F32).T
    for row_block in range(rows):
        part = turned[row_block * feats : (row_block + 1) * feats]
        if pad > feats:
            part = jnp.concatenate([part, jnp.zeros((pad - feats, series), F32)], axis=0)
        held[row_block] = part.astype(BF16)
    for step in range(rows):
        bins = held[partner(me, step, rows)]
        for block in range(series // LANES):
            lanes = slice(block * LANES, (block + 1) * LANES)
            out_refs[step][block * pad : (block + 1) * pad] = bins[:, lanes]


def columns(rows, quant_ref, *refs):
    sums_refs, own_ref, refs = refs[:rows], refs[rows], refs[rows + 1 :]
    bins_refs, out_refs = refs[:rows], refs[rows:]
    series = own_ref.shape[1]
    behind = bins_refs[0].shape[0]
    level = F32(0.0)
    for index, value in enumerate(LEVELS):
        level = jnp.where(quant_ref[0] == index, F32(value), level)
    sums = jnp.zeros((DAYS, STORES), F32)
    for ref in sums_refs:
        parts = ref[...].astype(F32)
        for piece in range(PIECES):
            sums = sums + parts[:, piece * STORES : (piece + 1) * STORES]
    shared = sums / (sums[TOTAL_ROW : TOTAL_ROW + 1] / HIST + 1.0)
    shared = jnp.concatenate(split_parts(shared), axis=1)

    own = own_ref[...]
    day = lax.broadcasted_iota(jnp.int32, (DAYS, series), 0)
    store = lax.broadcasted_iota(jnp.int32, (PIECES * STORES, series), 0) % STORES
    region = own[REGION_ROW : REGION_ROW + 1].astype(jnp.int32)
    pick = jnp.where(store == region, 1.0, 0.0).astype(BF16)
    regional = jnp.dot(shared, pick, preferred_element_type=F32)
    wave = jnp.where(day < HORIZON, jnp.tanh(own + regional), 0.0)
    mean = jnp.sum(wave, axis=0, keepdims=True) / HORIZON
    square = jnp.sum(wave * wave, axis=0, keepdims=True) / HORIZON
    gradient = 0.5 + 0.5 * mean - level
    hessian = 0.5 * (1.0 - square)
    rows_of = [
        value[:, block * LANES : (block + 1) * LANES]
        for value in (gradient, hessian, own[NODE_ROW : NODE_ROW + 1])
        for block in range(series // LANES)
    ]
    spare = jnp.zeros((out_refs[0].shape[0] - behind - len(rows_of), LANES), F32)
    tail = jnp.concatenate(rows_of + [spare], axis=0).astype(BF16)
    for bins_ref, out_ref in zip(bins_refs, out_refs):
        out_ref[:behind] = bins_ref[...]
        out_ref[behind:] = tail


def place(tail, cols_ref):
    blocks = cols_ref.shape[1] // LANES
    gradient, hessian, node = (
        jnp.concatenate(
            [tail[at * blocks + block : at * blocks + block + 1] for block in range(blocks)], axis=1
        )
        for at in range(3)
    )
    node_at = lax.broadcasted_iota(jnp.int32, (NODES, cols_ref.shape[1]), 0)
    here_node = node_at == node.astype(jnp.int32)
    for part, value in enumerate((gradient, hessian)):
        value = value * SCALE
        high = value.astype(F8).astype(F32)
        for offset, piece in ((0, high), (2, value - high)):
            at = (part + offset) * NODES
            cols_ref[at : at + NODES] = jnp.where(here_node, piece, 0.0).astype(F8)


def accumulate(sources, feats, first, last, *refs):
    block_refs, refs = refs[:sources], refs[sources:]
    if not first:
        before_ref, refs = refs[0], refs[1:]
    left_ref, refs = refs[0], refs[1:]
    if last:
        best_ref, refs = refs[0], refs[1:]
    bins_held, cols_held = refs
    series = bins_held.shape[3]
    pad = max(feats, 16)
    behind = series // LANES * pad
    for source, ref in enumerate(block_refs):
        bins = jnp.concatenate(
            [ref[block * pad : (block + 1) * pad] for block in range(series // LANES)], axis=1
        )
        bins = bins[:feats].astype(jnp.int32)
        bins_held[source, 0] = jnp.bitwise_and(bins, HALF - 1)
        bins_held[source, 1] = jnp.where(bins >= HALF, 1, 0)
        place(ref[behind:].astype(F32), cols_held.at[source])

    bin_at = lax.broadcasted_iota(jnp.int32, (32, series), 0)

    def spread(source, part, feature):
        row = bins_held[source, part, pl.ds(feature, 1)]
        return jnp.broadcast_to(row, (32, series)).astype(jnp.int8)

    def products(source, pair):
        every = cols_held[source]
        uptos, sets = [], [every]
        for feature in pair:
            within = spread(source, 0, feature)
            uptos += [
                jnp.where(
                    within <= (bin_at + at).astype(jnp.int8), jnp.ones((), F8), jnp.zeros((), F8)
                )
                for at in range(0, HALF, 32)
            ]
            upper = spread(source, 1, feature) == jnp.int8(1)
            sets += [
                jnp.where(upper, every[at : at + 32], jnp.zeros((), F8))
                for at in range(0, every.shape[0], 32)
            ]
        product = lax.dot_general(
            jnp.concatenate(sets, axis=0),
            jnp.concatenate(uptos, axis=0),
            ROW_BY_ROW,
            preferred_element_type=F32,
        )
        count = every.shape[0]
        found = []
        for at in range(len(pair)):
            mine = product[:, at * HALF : (at + 1) * HALF]
            both, upper = mine[:count], mine[(at + 1) * count : (at + 2) * count]
            both = both[: count // 2] + both[count // 2 :]
            upper = upper[: count // 2] + upper[count // 2 :]
            found.append(jnp.concatenate([both - upper, upper], axis=1))
        return found

    def two_features(feature):
        pair = (feature, feature + 1)
        found = products(0, pair)
        if sources > 1:
            found = lax.fori_loop(
                1,
                sources,
                lambda at, total: [a + b for a, b in zip(total, products(at, pair))],
                found,
            )
        if not first:
            found = [value + before_ref[at] for at, value in zip(pair, found)]
        return found

    group = min(feats, 32 if last else 16)

    if not last:

        def one_group(at, carry):
            for member in range(0, group, 2):
                feature = at * group + member
                left_ref[feature], left_ref[feature + 1] = two_features(feature)
            return carry

        lax.fori_loop(0, feats // group, one_group, 0)
        return

    feature_at = lax.broadcasted_iota(jnp.int32, (NODES, LANES), 1)
    last_bin = lax.broadcasted_iota(jnp.int32, (NODES, BINS), 1) == BINS - 1


    def over_all(halves):
        lower, upper = halves[:, :HALF], halves[:, HALF:]
        return jnp.concatenate([lower, upper + lower[:, HALF - 1 :]], axis=1) * (1.0 / SCALE)

    def gains(feature, left, best):
        grad, hess = left[:NODES], left[NODES:]
        all_grad, all_hess = grad[:, BINS - 1 :], hess[:, BINS - 1 :]
        over_grad, over_hess = all_grad - grad, all_hess - hess
        gain = grad * grad / (hess + 1.0) + over_grad * over_grad / (over_hess + 1.0)
        gain = jnp.max(jnp.where(last_bin, -jnp.inf, gain), axis=1, keepdims=True)
        gain = gain - all_grad * all_grad / (all_hess + 1.0)
        return jnp.where(feature_at == feature, gain, best)

    def final_group(at, best):
        for member in range(0, group, 2):
            feature = at * group + member
            for offset, halves in enumerate(two_features(feature)):
                left_ref[feature + offset] = halves
                best = gains(feature + offset, over_all(halves), best)
        return best

    best = lax.fori_loop(0, feats // group, final_group, jnp.zeros((NODES, LANES), F32))
    best = best.T
    width = LANES // NODES
    packed = jnp.concatenate(
        [best[at * (feats // width) : (at + 1) * (feats // width)] for at in range(width)], axis=1
    )
    for target in range(best_ref.shape[0]):
        best_ref[target] = packed


def results(left_ref, packed_ref, hist_ref, best_ref, hist_held, best_held, sems):
    feats = left_ref.shape[0]
    targets, packed_rows, _ = packed_ref.shape
    first_bin = lax.broadcasted_iota(jnp.int32, (2 * NODES, HALF), 1) == 0
    group = min(feats, 4)

    def one_group(at, carry):
        for member in range(group):
            feature = at * group + member
            for half in range(2):
                lanes = slice(half * HALF, (half + 1) * HALF)
                left = left_ref[feature, :, lanes] * (1.0 / SCALE)
                before = jnp.where(first_bin, 0.0, pltpu.roll(left, 1, axis=1))
                hist_held[feature, :, lanes] = left - before
        here = pl.ds(at * group, group)
        pltpu.make_async_copy(hist_held.at[here], hist_ref.at[here], sems.at[0]).start()
        return carry

    steps = feats // group
    early = -(-steps // 4)
    for step in range(early):
        one_group(step, 0)
    for target in range(targets):
        packed = packed_ref[target]
        for at in range(LANES // NODES):
            best_held[target, at * packed_rows : (at + 1) * packed_rows] = packed[
                :, at * NODES : (at + 1) * NODES
            ]
    best_copy = pltpu.make_async_copy(best_held, best_ref, sems.at[1])
    best_copy.start()
    for step in range(early, steps):
        one_group(step, 0)
    pltpu.make_async_copy(hist_held, hist_ref, sems.at[0]).wait()
    best_copy.wait()


def shards(daily_unit_counts, region_ids, node_ids, bin_ids, quant_index, filter_kernels):
    rows = lax.axis_size("rows")
    feat_count = lax.axis_size("feat")
    series = daily_unit_counts.shape[0]
    feats = bin_ids.shape[1] // rows
    pad = max(feats, 16)
    blocks = series // LANES
    vmem = pl.BlockSpec(memory_space=pltpu.VMEM)
    smem = pl.BlockSpec(memory_space=pltpu.SMEM)
    hbm = pl.BlockSpec(memory_space=pl.ANY)
    params = pltpu.CompilerParams(vmem_limit_bytes=VMEM_LIMIT)
    regions = region_ids.reshape(1, series)
    nodes = node_ids.reshape(1, series)

    def exchange(array, step):
        pairs = [(at, partner(at, step, rows)) for at in range(rows)]
        return lax.ppermute(array, "rows", pairs)

    sums, *passed = pl.pallas_call(
        prepare,
        out_shape=[
            jax.ShapeDtypeStruct((DAYS, LANES), BF16),
            jax.ShapeDtypeStruct(daily_unit_counts.shape, BF16),
            jax.ShapeDtypeStruct((1, series), jnp.int32),
            jax.ShapeDtypeStruct((1, series), jnp.int32),
            jax.ShapeDtypeStruct(bin_ids.shape, jnp.int32),
            jax.ShapeDtypeStruct((PIECES * DAYS, LANES), BF16),
        ],
        in_specs=[hbm] * 5,
        out_specs=[vmem] * 6,
        scratch_shapes=[pltpu.VMEM((TAPS, CHANNELS), F32), pltpu.SemaphoreType.DMA((5,))],
        compiler_params=params,
        name="prepare",
    )(
        *(
            pltpu.with_memory_space_constraint(array, pltpu.HBM)
            for array in (daily_unit_counts, regions, nodes, bin_ids, filter_kernels.T)
        )
    )
    own, *bins = pl.pallas_call(
        functools.partial(local_terms, rows),
        out_shape=[jax.ShapeDtypeStruct((DAYS, series), F32)]
        + [jax.ShapeDtypeStruct((blocks * pad, LANES), BF16)] * rows,
        in_specs=[vmem] * 5,
        out_specs=[vmem] * (1 + rows),
        scratch_shapes=[pltpu.VMEM((rows, pad, series), BF16)],
        compiler_params=params,
        name="local_terms",
    )(*passed)

    def exchange_sums(step):
        pairs = [
            (at * feat_count + lane, partner(at, step, rows) * feat_count + beside(lane))
            for at in range(rows)
            for lane in range(feat_count)
        ]
        return lax.ppermute(sums, ("rows", "feat"), pairs)

    def beside(lane):
        return lane ^ 1 if lane ^ 1 < feat_count else lane

    every_sums = [sums] + [exchange_sums(step) for step in range(1, rows)]
    outgoing = pl.pallas_call(
        functools.partial(columns, rows),
        out_shape=[jax.ShapeDtypeStruct((blocks * pad + 4 * blocks, LANES), BF16)] * rows,
        in_specs=[smem] + [vmem] * (2 * rows + 1),
        out_specs=[vmem] * rows,
        compiler_params=params,
        name="columns",
    )(quant_index, *every_sums, own, *bins)
    order = [2, 1, *range(3, rows)] if rows > 2 else [*range(1, rows)]
    arrived = [outgoing[0]] + [exchange(outgoing[step], step) for step in order]

    targets = rows * feat_count
    packed_rows = feats * NODES // LANES
    hist_shape = jax.ShapeDtypeStruct((feats, 2 * NODES, BINS), F32)
    steps = [arrived[at : at + 1] for at in range(min(rows, 4) - 1)]
    steps.append(arrived[len(steps) :])
    histogram = None
    for at, sources in enumerate(steps):
        first, last = at == 0, at == len(steps) - 1
        count = len(sources)
        held = [
            pltpu.VMEM((count, 2, feats, series), jnp.int32),
            pltpu.VMEM((count, 4 * NODES, series), F8),
        ]
        operands = sources + ([] if first else [histogram])
        if last:
            out_shape = [hist_shape, jax.ShapeDtypeStruct((targets, packed_rows, LANES), F32)]
            out_specs = [vmem, vmem]
        else:
            out_shape, out_specs = hist_shape, vmem
        histogram = pl.pallas_call(
            functools.partial(accumulate, count, feats, first, last),
            out_shape=out_shape,
            in_specs=[vmem] * len(operands),
            out_specs=out_specs,
            scratch_shapes=held,
            input_output_aliases={} if first else {len(operands) - 1: 0},
            compiler_params=params,
            name=f"accumulate_{at}",
        )(*operands)
    left, best = histogram

    gathered = lax.all_to_all(best, ("feat", "rows"), 0, 0, tiled=True)
    best_shape = jax.ShapeDtypeStruct((targets, feats, NODES), F32)
    histogram, feature_best = pl.pallas_call(
        results,
        out_shape=[hist_shape, best_shape],
        in_specs=[vmem] * 2,
        out_specs=[hbm] * 2,
        scratch_shapes=[
            pltpu.VMEM(hist_shape.shape, F32),
            pltpu.VMEM(best_shape.shape, F32),
            pltpu.SemaphoreType.DMA((2,)),
        ],
        compiler_params=params,
        name="results",
    )(left, gathered)
    return (
        histogram.reshape(1, 1, feats, 2, NODES, BINS),
        feature_best.reshape(feat_count, rows, feats, NODES),
    )


def solution(mesh):
    in_specs = (
        P(("groups", "rows"), None),
        P(("groups", "rows")),
        P(("groups", "rows")),
        P(("groups", "rows"), "feat"),
        P("groups"),
        P(),
    )
    out_specs = (
        P(("groups", "feat"), "rows", None, None, None, None),
        P("groups", None, None, None),
    )
    return jax.shard_map(shards, mesh=mesh, in_specs=in_specs, out_specs=out_specs, check_vma=False)
```
